32 devices in a mesh: dp: 8 (over z, core), tensor: 4 (over y, x).
Axes of the slice: x: 2, y: 2, z: 4, core: 2. Of those that a mesh axis runs over, the one named last changes fastest.
Arguments:
- tokens: bfloat16 [2048, 1536], P(('dp', 'tensor')), may hold values from -6 to 6
- cotangent: bfloat16 [2048, 1536], P(('dp', 'tensor')), may hold values from -6 to 6
- norm_gains: bfloat16 [4, 1536], replicated, may hold values from 0.5 to 1.5
- mix_in: bfloat16 [1536, 2, 3072], P(None, None, 'tensor'), may hold values from -0.15625 to 0.15625
- conv_weight: float32 [4, 3072], P(None, 'tensor'), may hold values from -3 to 3
- x_proj: bfloat16 [3072, 128], P('tensor'), may hold values from -0.109375 to 0.109375
- dt_proj: bfloat16 [96, 3072], P(None, 'tensor'), may hold values from -0.625 to 0.625
- dt_bias: float32 [3072], P('tensor'), may hold values from -4.5 to -1.5
- a_log: float32 [3072, 16], P('tensor'), may hold values from 0 to 2.77
- skip_gain: float32 [3072], P('tensor'), may hold values from 0.5 to 1.5
- mix_out: bfloat16 [3072, 1536], P('tensor'), may hold values from -0.109375 to 0.109375
- ffn_in: bfloat16 [1536, 2, 4096], P(None, None, 'tensor'), may hold values from -0.15625 to 0.15625
- ffn_out: bfloat16 [4096, 1536], P('tensor'), may hold values from -0.09375 to 0.09375
- attn_query: bfloat16 [1536, 1536], P(None, 'tensor'), may hold values from -0.15625 to 0.15625
- attn_keyval: bfloat16 [1536, 2, 512], P(None, None, 'tensor'), may hold values from -0.15625 to 0.15625
- attn_out: bfloat16 [1536, 1536], P('tensor'), may hold values from -1.25 to 1.25
- router: bfloat16 [1536, 16], replicated, may hold values from -0.15625 to 0.15625
- expert_in: bfloat16 [16, 1536, 2, 1024], P(None, None, None, 'tensor'), may hold values from -0.15625 to 0.15625
- expert_out: bfloat16 [16, 1024, 1536], P(None, 'tensor'), may hold values from -0.1875 to 0.1875
- routes: int32 [2048, 2], P('dp'), may hold values from 0 to 15, all different within a row; in each aligned block of 256 rows (0 to 255, 256 to 511, ...) at most 48 rows name the same one
Outputs:
- block_out: bfloat16 [2048, 1536], P(('dp', 'tensor'))
- tokens_grad: float32 [2048, 1536], P(('dp', 'tensor'))
- norm_gains_grad: float32 [4, 1536], P(None, 'dp')
- mix_in_grad: float32 [1536, 2, 3072], P('dp', None, 'tensor')
- conv_weight_grad: float32 [4, 3072], P(None, ('tensor', 'dp'))
- x_proj_grad: float32 [3072, 128], P('tensor', 'dp')
- dt_proj_grad: float32 [96, 3072], P('dp', 'tensor')
- dt_bias_grad: float32 [3072], P(('tensor', 'dp'))
- a_log_grad: float32 [3072, 16], P(('tensor', 'dp'))
- skip_gain_grad: float32 [3072], P(('tensor', 'dp'))
- mix_out_grad: float32 [3072, 1536], P('tensor', 'dp')
- ffn_in_grad: float32 [1536, 2, 4096], P('dp', None, 'tensor')
- ffn_out_grad: float32 [4096, 1536], P('tensor', 'dp')
- attn_query_grad: float32 [1536, 1536], P('dp', 'tensor')
- attn_keyval_grad: float32 [1536, 2, 512], P('dp', None, 'tensor')
- attn_out_grad: float32 [1536, 1536], P('tensor', 'dp')
- router_grad: float32 [1536, 16], P('dp')
- expert_in_grad: float32 [16, 1536, 2, 1024], P(None, 'dp', None, 'tensor')
- expert_out_grad: float32 [16, 1024, 1536], P(None, 'tensor', 'dp')
The draws below stay inside these ranges and needn't reach their ends.
Inputs may be any that keep to these rules, and one draw needn't show every extreme that they name: `routes`: each row names two different experts; in each sequence's 256 rows no expert is named by more than 48 rows, a bound that some block reaches.
All inputs are finite; a program needn't handle non-finite values.
Results may differ from the reference program's by a relative error of at most 0.04.
Values may be sent and summed in bfloat16 or wider, within the bound.
No kernel may reach another device: no remote copies, remote signals or barrier semaphores. Data moves between devices by JAX's collectives and lax.ppermute only.
A program may use at most 448 MiB of HBM per device.

```python
import math
import jax
import jax.numpy as jnp
import numpy as np
from jax import lax

D = 1536
INNER = 3072
STATE = 16
CONV = 4
DT_RANK = 96
FF = 4096
HEADS = 24
KV_HEADS = 8
HEAD_DIM = 64
EXPERTS = 16
EFF = 1024
TOP = 2
LEN = 256
SEQS = 8
TOKENS = 2048
CAP = 48


def raised(entries, own_key, source, target, shards_of, factor):
    owner, partner = [(jnp.arange(entries.shape[axis_at]) // (entries.shape[axis_at] // shards_of)).reshape([-1 if axis == axis_at else 1 for axis in range(entries.ndim)]) for axis_at in (source, target)]
    chosen = jax.random.permutation(own_key, shards_of)[partner]
    strong = (owner == chosen) | (owner == (partner + shards_of // 2) % shards_of)
    return jnp.where(strong, factor * entries, entries)


def steps_of(rng, dims, shards, smallest, top_value):
    level = 1.0
    for dim, shards_of in shards:
        draws = jax.random.uniform(jax.random.fold_in(jax.random.fold_in(rng, 6), dim), (shards_of,), jnp.float32, smallest / len(shards), top_value / len(shards))
        level = level * jnp.repeat(jnp.exp(draws), dims[dim] // shards_of).reshape((-1,) + (1,) * (len(dims) - 1 - dim))
    return level


def deal_out(key, own, number, rows, number_of, top, bound, lean):
    ranking = jax.random.permutation(key, number_of)
    crowded, ordinary = load_shares(number_of, rows * top, bound, lean, True), load_shares(number_of, rows * top, bound, lean, False)
    places = jnp.arange(number_of)

    def named(lengths, turn):
        used = int((lengths > 0).sum())
        fixed = max(1, used // 4)
        shifted = fixed + (places - fixed + turn * (used - fixed)) % max(1, number_of - fixed)
        return jnp.zeros((number_of,), jnp.int32).at[ranking[jnp.where(places < fixed, places, shifted)]].set(jnp.asarray(lengths, jnp.int32))

    lengths = jnp.where(number % 4 == 0, named(crowded, number // 4), named(ordinary, number - number // 4 - 1))
    mixed = jax.random.permutation(jax.random.fold_in(own, 3), number_of)
    donor, sink = mixed[0:number_of // 2 * 2:2], mixed[1:number_of // 2 * 2:2]
    slack = jnp.minimum(lengths[donor] - 1, bound - lengths[sink]) // 2
    slack = jnp.where((donor == ranking[0]) | (sink == ranking[0]) | (lengths[sink] == 0), 0, jnp.maximum(slack, 0))
    shifted = jax.random.randint(jax.random.fold_in(own, 4), (number_of // 2,), 0, 1 << 20) % (slack + 1)
    lengths = lengths.at[donor].add(-shifted).at[sink].add(shifted)
    labels = jnp.searchsorted(jnp.cumsum(lengths), jnp.arange(rows * top), side="right").astype(jnp.int32)
    grid = labels.reshape(top, rows).T
    grid = grid[jax.random.permutation(jax.random.fold_in(own, 1), rows)]
    turn = jax.random.randint(jax.random.fold_in(own, 2), (rows, 1), 0, top)
    return jnp.take_along_axis(grid, (jnp.arange(top)[None, :] + turn) % top, axis=1)


def load_shares(amount, total, limit, lean, full):
    portions = [(1 << 20) // math.isqrt(rank ** lean) + 1 for rank in range(1, amount + 1)]
    largest = limit if full else min(limit, max(-(-total // amount), total * portions[0] // sum(portions)))
    least = 1 if total - largest >= amount - 1 else 0
    holding, spare = [largest] + [least] * (amount - 1), total - largest - least * (amount - 1)
    while spare > 0:
        candidates = [i for i in range(1, amount) if holding[i] < largest] or [i for i in range(1, amount) if holding[i] < limit]
        whole, budget = sum([portions[i] for i in candidates]), spare
        for i in candidates:
            addition = min(limit - holding[i], max(1, budget * portions[i] // whole), spare)
            holding[i] = holding[i] + addition
            spare = spare - addition
    return np.array(holding)


def gaussian(stream_key, extent, spread, bound, cuts=(), kind=jnp.bfloat16):
    drawn = jax.random.normal(stream_key, extent, jnp.float32) * spread
    if len(cuts) > 0:
        drawn = steps_of(stream_key, extent, cuts, -0.22, 0.18) * drawn
    return jnp.clip(drawn, min=-bound, max=bound).astype(kind)


def noise_with(own_key, extent, spread, reach, cuts, heavy, kind=jnp.bfloat16):
    values = spread * jax.random.normal(own_key, extent, jnp.float32)
    if cuts:
        values = values * steps_of(own_key, extent, cuts, -0.22, 0.18)
    return jnp.clip(raised(values, jax.random.fold_in(own_key, 3), *heavy), -reach, reach).astype(kind)


def setup_inputs(seed: int = 0) -> dict:
    seeds = jax.random.split(jax.random.key(seed), 21)
    tokens = gaussian(seeds[0], (TOKENS, D), 1.0, 6.0, ((0, 32),))
    cotangent = noise_with(seeds[1], (TOKENS, D), 1.0, 6.0, ((0, 32),), (0, 1, 32, 2.75))
    norm_gains = jnp.clip(1.0 + 0.1 * jax.random.normal(seeds[2], (4, D), jnp.float32), 0.5, 1.5).astype(jnp.bfloat16)
    mix_in = gaussian(seeds[3], (D, 2, INNER), D ** -0.5, 0.15625, ((2, 4),))
    conv_weight = gaussian(seeds[4], (CONV, INNER), CONV ** -0.5, 3.0, ((1, 4),), jnp.float32)
    x_proj = gaussian(seeds[5], (INNER, DT_RANK + 2 * STATE), INNER ** -0.5, 0.109375, ((0, 4),))
    dt_proj = gaussian(seeds[6], (DT_RANK, INNER), DT_RANK ** -0.5, 0.625, ((1, 4),))
    dt_bias = jnp.clip(-4.5 + 3.0 * jax.random.uniform(seeds[7], (INNER,), jnp.float32) ** steps_of(seeds[7], (INNER,), ((0, 4),), -0.2, 0.2), -4.5, -1.5)
    a_log = jnp.clip(2.77 * jax.random.uniform(seeds[8], (INNER, STATE), jnp.float32) ** steps_of(seeds[8], (INNER, STATE), ((0, 4),), -0.2, 0.2), 0.0, 2.77)
    skip_gain = jnp.clip(0.5 + 1.0 * jax.random.uniform(seeds[9], (INNER,), jnp.float32) ** steps_of(seeds[9], (INNER,), ((0, 4),), -0.2, 0.2), 0.5, 1.5)
    mix_out = gaussian(seeds[10], (INNER, D), INNER ** -0.5, 0.109375, ((0, 4),))
    ffn_in = gaussian(seeds[11], (D, 2, FF), D ** -0.5, 0.15625, ((2, 4),))
    ffn_out = gaussian(seeds[12], (FF, D), FF ** -0.5, 0.09375, ((0, 4),))
    attn_query = gaussian(seeds[13], (D, HEADS * HEAD_DIM), D ** -0.5, 0.15625, ((1, 4),))
    attn_keyval = gaussian(seeds[14], (D, 2, KV_HEADS * HEAD_DIM), D ** -0.5, 0.15625, ((2, 4),))
    attn_out = gaussian(seeds[15], (HEADS * HEAD_DIM, D), (HEADS * HEAD_DIM // 64) ** -0.5, 1.25, ((0, 4),))
    router = gaussian(seeds[16], (D, EXPERTS), D ** -0.5, 0.15625)
    expert_in = gaussian(seeds[17], (EXPERTS, D, 2, EFF), D ** -0.5, 0.15625, ((3, 4),))
    expert_out = gaussian(seeds[18], (EXPERTS, EFF, D), EFF ** -0.5, 0.1875, ((1, 4),))
    routes_keys = jax.random.split(jax.random.fold_in(seeds[19], 1), TOKENS // LEN)
    routes_turns = jax.random.permutation(jax.random.fold_in(seeds[19], 3), TOKENS // LEN)
    routes = jax.vmap(lambda own, number: deal_out(jax.random.fold_in(seeds[19], 2), own, number, LEN, EXPERTS, TOP, CAP, 1))(routes_keys, routes_turns).reshape((TOKENS, TOP))
    return dict(tokens=tokens, cotangent=cotangent, norm_gains=norm_gains, mix_in=mix_in, conv_weight=conv_weight, x_proj=x_proj, dt_proj=dt_proj, dt_bias=dt_bias, a_log=a_log, skip_gain=skip_gain, mix_out=mix_out, ffn_in=ffn_in, ffn_out=ffn_out, attn_query=attn_query, attn_keyval=attn_keyval, attn_out=attn_out, router=router, expert_in=expert_in, expert_out=expert_out, routes=routes)


highest = lax.Precision.HIGHEST
epsilon = 1e-06
floor_square = 0.1
masked_score = -1e+30

@jax.custom_vjp
def low(v):
    return lax.optimization_barrier(v.astype(jnp.bfloat16)).astype(jnp.float32)

@jax.custom_vjp
def low_back(v):
    return v

def low_keep(v):
    return (low(v), None)

def low_pass(kept, grad):
    return (grad,)

def back_keep(v):
    return (v, None)

def back_low(kept, grad):
    return (low(grad),)
low.defvjp(low_keep, low_pass)
low_back.defvjp(back_keep, back_low)

def matmul(left, right):
    return jnp.dot(left, right, precision=highest, preferred_element_type=jnp.float32)

def root_norm(hidden, gain):
    return hidden * lax.rsqrt(lax.optimization_barrier(jnp.mean(hidden * hidden, axis=-1, keepdims=True)) + epsilon) * gain

def floored_norm(values):
    return values * lax.rsqrt(jnp.maximum(lax.optimization_barrier(jnp.mean(values * values, axis=-1, keepdims=True)), floor_square))

def column_norms(projected):
    step_part = projected[:, :DT_RANK]
    step_part = step_part * lax.rsqrt(lax.optimization_barrier(jnp.mean(step_part * step_part, axis=-1, keepdims=True)) + epsilon)
    return jnp.concatenate([step_part, floored_norm(projected[:, DT_RANK:DT_RANK + STATE]), floored_norm(projected[:, DT_RANK + STATE:])], axis=1)

def swiglu(gate_up):
    half = gate_up.shape[-1] // 2
    return jax.nn.silu(gate_up[..., :half]) * gate_up[..., half:]

def conv_act(inner, weights):
    length = inner.shape[0]
    padded = jnp.pad(inner, ((CONV - 1, 0), (0, 0)))
    total = weights[0] * padded[0:length]
    for offset in range(1, CONV):
        total = total + weights[offset] * padded[offset:offset + length]
    return jax.nn.silu(total)

def combine_pairs(earlier, later):
    return (earlier[0] * later[0], later[0] * earlier[1] + later[1])

def scan_sequence(conv_out, delta, b_norm, c_norm, a_matrix):
    length, channels = conv_out.shape
    block = min(128, length)
    count = length // block

    def one_block(state, pieces):
        input_block, delta_block, b_block, c_block = pieces
        decay = jnp.exp(delta_block[:, :, None] * a_matrix[None])
        drive = (delta_block * input_block)[:, :, None] * b_block[:, None, :]
        decay_run, drive_run = lax.associative_scan(combine_pairs, (decay, drive), axis=0)
        states = drive_run + decay_run * state[None]
        return (states[-1], lax.optimization_barrier(jnp.sum(states * c_block[:, None, :], axis=-1)))
    pieces = (conv_out.reshape(count, block, channels), delta.reshape(count, block, channels), b_norm.reshape(count, block, -1), c_norm.reshape(count, block, -1))
    start_state = jnp.zeros((channels, a_matrix.shape[1]), jnp.float32)
    _, outputs = lax.scan(jax.checkpoint(one_block), start_state, pieces)
    return outputs.reshape(length, channels)

def mixer_core(conv_out, gate_z, pre_act, dt_bias, a_log, skip_gain, b_norm, c_norm):
    delta = jax.nn.softplus(pre_act + dt_bias)
    scanned = scan_sequence(conv_out, delta, b_norm, c_norm, -jnp.exp(a_log))
    return (scanned + skip_gain * conv_out) * jax.nn.silu(gate_z)

def dispatch(route_table, capacity):
    flat = route_table.reshape(-1).astype(jnp.int32)
    count = flat.shape[0]
    onehot = (flat[:, None] == jnp.arange(EXPERTS, dtype=jnp.int32)[None, :]).astype(jnp.int32)
    before = jnp.cumsum(onehot, axis=0) - onehot
    ranked = lax.optimization_barrier(jnp.sum(before * onehot, axis=1))
    position = flat * capacity + ranked
    source = jnp.zeros((EXPERTS * capacity,), jnp.int32).at[position].set(jnp.arange(count, dtype=jnp.int32))
    filled = jnp.zeros((EXPERTS * capacity,), jnp.float32).at[position].set(1.0)
    return (source, filled)

def attention(normed, w_query, w_keyval, w_out):
    length = normed.shape[0]
    group = HEADS // KV_HEADS
    query = low(low_back(matmul(normed, w_query)))
    keyval = low(low_back(matmul(normed, w_keyval.reshape(D, 2 * KV_HEADS * HEAD_DIM))))
    queries = query.reshape(length, KV_HEADS, group, HEAD_DIM)
    keys = keyval[:, :KV_HEADS * HEAD_DIM].reshape(length, KV_HEADS, HEAD_DIM)
    values = keyval[:, KV_HEADS * HEAD_DIM:].reshape(length, KV_HEADS, HEAD_DIM)
    block = min(512, length)
    scale = 1.0 / math.sqrt(HEAD_DIM)
    key_pos = jnp.arange(length, dtype=jnp.int32)

    def one_block(first):
        query_block = lax.dynamic_slice_in_dim(queries, first, block, 0)
        scores = low_back(jnp.einsum('qkgd,tkd->kgqt', query_block, keys, precision=highest) * scale)
        allowed = key_pos[None, :] <= (first + jnp.arange(block, dtype=jnp.int32))[:, None]
        soft = jax.nn.softmax(jnp.where(allowed, scores, masked_score), axis=-1)
        return jnp.einsum('kgqt,tkd->qkgd', low(soft), values, precision=highest)
    starts = jnp.arange(length // block, dtype=jnp.int32) * block
    attended = lax.map(jax.checkpoint(one_block), starts).reshape(length, HEADS * HEAD_DIM)
    attended = low(low_back(attended))
    return low_back(matmul(attended, w_out))

def experts(normed, route_table, w_router, w_in, w_out):
    length = normed.shape[0]
    logits = low_back(matmul(normed, w_router))
    weights = jax.nn.softmax(jnp.take_along_axis(logits, route_table, axis=1), axis=-1)
    source, filled = dispatch(route_table, CAP)
    token_index = source // 2
    slot_weight = (weights.reshape(-1)[source] * filled).reshape(EXPERTS, CAP)
    gathered = normed[token_index].reshape(EXPERTS, CAP, D)
    gate_up = low_back(jnp.einsum('ecd,edf->ecf', gathered, w_in.reshape(EXPERTS, D, 2 * EFF), precision=highest))
    acted = low(swiglu(gate_up))
    rows_out = low_back(jnp.einsum('ecf,efd->ecd', acted, w_out, precision=highest))
    combined = jnp.zeros((length, D), jnp.float32).at[token_index].add((slot_weight[..., None] * rows_out).reshape(-1, D))
    return low_back(combined)

def layers(hidden, route_table, weights):
    gains, mix_in, conv_weight, x_proj, dt_proj, dt_bias, a_log, skip_gain, mix_out, ffn_in, ffn_out, attn_query, attn_keyval, attn_out, router, expert_in, expert_out = weights
    normed = low(root_norm(hidden, gains[0]))
    mixed = low_back(matmul(normed, mix_in.reshape(D, 2 * INNER)))
    conv_out = conv_act(mixed[:, :INNER], conv_weight)
    projected = low_back(matmul(low(conv_out), x_proj))
    normed_cols = column_norms(projected)
    pre_act = low_back(matmul(low(normed_cols[:, :DT_RANK]), dt_proj))
    gated = mixer_core(conv_out, mixed[:, INNER:], pre_act, dt_bias, a_log, skip_gain, normed_cols[:, DT_RANK:DT_RANK + STATE], normed_cols[:, DT_RANK + STATE:])
    hidden = hidden + low_back(matmul(low(gated), mix_out))
    normed = low(root_norm(hidden, gains[1]))
    gate_up = low_back(matmul(normed, ffn_in.reshape(D, 2 * FF)))
    hidden = hidden + low_back(matmul(low(swiglu(gate_up)), ffn_out))
    normed = low(root_norm(hidden, gains[2]))
    hidden = hidden + attention(normed, attn_query, attn_keyval, attn_out)
    normed = low(root_norm(hidden, gains[3]))
    return hidden + experts(normed, route_table, router, expert_in, expert_out)

def reference(tokens, cotangent, norm_gains, mix_in, conv_weight, x_proj, dt_proj, dt_bias, a_log, skip_gain, mix_out, ffn_in, ffn_out, attn_query, attn_keyval, attn_out, router, expert_in, expert_out, routes):
    weights = tuple((item.astype(jnp.float32) for item in (norm_gains, mix_in, conv_weight, x_proj, dt_proj, dt_bias, a_log, skip_gain, mix_out, ffn_in, ffn_out, attn_query, attn_keyval, attn_out, router, expert_in, expert_out)))
    hidden = tokens.astype(jnp.float32).reshape(SEQS, LEN, D)
    route_seqs = routes.astype(jnp.int32).reshape(SEQS, LEN, TOP)

    def forward(hidden, weights):

        def one_sequence(carry, pieces):
            return (carry, jax.checkpoint(layers)(pieces[0], pieces[1], weights))
        _, result = lax.scan(one_sequence, jnp.zeros((), jnp.float32), (hidden, route_seqs))
        return result
    output, pullback = jax.vjp(forward, hidden, weights)
    grad_hidden, grads = pullback(cotangent.astype(jnp.float32).reshape(SEQS, LEN, D))
    return (output.reshape(TOKENS, D).astype(jnp.bfloat16), grad_hidden.reshape(TOKENS, D), grads[0], grads[1], grads[2], grads[3], grads[4], grads[5], grads[6], grads[7], grads[8], grads[9], grads[10], grads[11], grads[12], grads[13], grads[14], grads[15], grads[16])
```

```python
import functools
import math

import jax
import jax.numpy as jnp
from jax import lax
from jax.experimental import pallas as pl
from jax.experimental.pallas import tpu as pltpu
from jax.sharding import PartitionSpec as P

D = 1536
STATE = 16
CONV = 4
DT_RANK = 96
HEADS = 24
KV_HEADS = 8
HEAD_DIM = 64
EXPERTS = 16
LEN = 256
CAP = 48

epsilon = 1e-06
floor_square = 0.1
masked_score = -1e30
LOG2E = 1.4426950408889634
PAD = 8
CHUNK = 16
GROUP = 8
VMEM_LIMIT = 56 * 1024 * 1024

f32 = jnp.float32
bf16 = jnp.bfloat16


def matmul(left, right):
    return jnp.dot(left, right, preferred_element_type=f32)


def times_transposed(left, right):
    return lax.dot_general(left, right, (((1,), (1,)), ((), ())), preferred_element_type=f32)


def transposed_times(left, right):
    return lax.dot_general(left, right, (((0,), (0,)), ((), ())), preferred_element_type=f32)


def sigmoid(v):
    return 1.0 / (1.0 + jnp.exp(-v))


def dot_exact(left, right):
    return jnp.dot(left, right, precision=lax.Precision.HIGHEST, preferred_element_type=f32)


def column_norm_parts(projected):
    lane = lax.broadcasted_iota(jnp.int32, projected.shape, 1)
    square = projected * projected
    in_step = lane < DT_RANK
    in_b = jnp.logical_and(lane >= DT_RANK, lane < DT_RANK + STATE)
    in_c = lane >= DT_RANK + STATE
    mean_step = jnp.sum(jnp.where(in_step, square, 0.0), axis=1, keepdims=True) / DT_RANK
    mean_b = jnp.sum(jnp.where(in_b, square, 0.0), axis=1, keepdims=True) / STATE
    mean_c = jnp.sum(jnp.where(in_c, square, 0.0), axis=1, keepdims=True) / STATE
    r_step = lax.rsqrt(mean_step + epsilon)
    r_b = lax.rsqrt(jnp.maximum(mean_b, floor_square))
    r_c = lax.rsqrt(jnp.maximum(mean_c, floor_square))
    scale = jnp.where(in_step, r_step, jnp.where(in_b, r_b, r_c))
    return scale, in_step, in_b, in_c, mean_b, mean_c


def row_spread(cols_ref, first, out_ref):
    pick = (
        lax.broadcasted_iota(jnp.int32, (128, CHUNK * STATE), 0) - first
        == lax.broadcasted_iota(jnp.int32, (128, CHUNK * STATE), 1) % STATE
    ).astype(f32)
    out_ref[...] = (dot_exact(cols_ref[...], pick) * chunk_mask(LEN)).astype(bf16)


def chunk_mask(rows):
    return (
        lax.broadcasted_iota(jnp.int32, (rows, CHUNK * STATE), 0) % CHUNK
        == lax.broadcasted_iota(jnp.int32, (rows, CHUNK * STATE), 1) // STATE
    ).astype(f32)


def conv_total(pad_ref, weight_ref, length):
    total = weight_ref[0:1, :] * pad_ref[pl.ds(PAD - CONV + 1, length), :]
    for tap in range(1, CONV):
        total = total + weight_ref[tap : tap + 1, :] * pad_ref[pl.ds(PAD - CONV + 1 + tap, length), :]
    return total


def conv_forward_kernel(blocks, me_ref, xz_ref, weight_ref, xproj_ref, u_ref, proj_ref, pad_ref):
    me = me_ref[0]
    size = LEN // blocks
    pad_ref[0:PAD, :] = jnp.zeros((PAD, pad_ref.shape[1]), f32)
    for m in range(blocks):
        at = pl.multiple_of(jnp.bitwise_xor(me, m) * size, size)
        pad_ref[PAD + m * size : PAD + (m + 1) * size, :] = xz_ref[0, pl.ds(at, size), :]
    total = conv_total(pad_ref, weight_ref, LEN)
    u = total * sigmoid(total)
    for m in range(blocks):
        at = pl.multiple_of(jnp.bitwise_xor(me, m) * size, size)
        u_ref[pl.ds(at, size), :] = u[m * size : (m + 1) * size, :]
    proj_ref[...] = matmul(u_ref[...].astype(bf16), xproj_ref[...])


def scan_setup(proj_ref, cols_ref, b_ref, c_ref):
    projected = proj_ref[...]
    scale = column_norm_parts(projected)[0]
    cols_ref[...] = projected * scale
    row_spread(cols_ref, DT_RANK, b_ref)
    row_spread(cols_ref, DT_RANK + STATE, c_ref)


def step_sizes(cols_ref, dt_proj_ref, bias_ref):
    low = cols_ref[:, :DT_RANK].astype(bf16)
    pre = matmul(low, dt_proj_ref[...]) + bias_ref[...]
    return low, pre, jnp.maximum(pre, 0.0) + jnp.log1p(jnp.exp(-jnp.abs(pre)))


def chunk_place(index, me, size):
    block = index // (size // CHUNK)
    inner = index % (size // CHUNK)
    return pl.multiple_of(jnp.bitwise_xor(block, me) * size + inner * CHUNK, CHUNK)


def chunk_group(index):
    out = []
    for q in range(GROUP):
        base = (index * GROUP + q) * CHUNK
        out.append(
            (
                pl.ds(pl.multiple_of(base, CHUNK), CHUNK),
                pl.ds(pl.multiple_of(base * STATE, CHUNK * STATE), CHUNK * STATE),
            )
        )
    return out


def push_chunks(left_ref, right_ref, out_ref):
    def body(index, carry):
        for rows, many in chunk_group(index):
            out_ref[many, :] = transposed_times(left_ref[rows, :], right_ref[rows, :])
        return carry

    lax.fori_loop(0, LEN // CHUNK // GROUP, body, 0)


def scan_forward_kernel(
    blocks,
    me_ref,
    proj_ref,
    dt_proj_ref,
    bias_ref,
    alog_ref,
    skip_ref,
    u_ref,
    xz_ref,
    out_w_ref,
    gated_ref,
    ys_ref,
    states_ref,
    *rest,
):
    out_refs = rest[:blocks]
    cols_ref, b_ref, c_ref, delta_ref, drive_ref, push_ref, total_ref = rest[blocks:]
    me = me_ref[0]
    size = LEN // blocks
    lanes = u_ref.shape[1]
    step = pl.program_id(0)

    @pl.when(step == 0)
    def _():
        scan_setup(proj_ref, cols_ref, b_ref, c_ref)

    _, _, delta = step_sizes(cols_ref, dt_proj_ref, bias_ref)
    delta_ref[...] = delta
    drive_ref[...] = (delta * u_ref[...]).astype(bf16)
    rate = -jnp.exp(alog_ref[...]) * LOG2E
    push_chunks(b_ref, drive_ref, push_ref)

    def chunk(index, state):
        base = chunk_place(index, me, size)
        steps = delta_ref[pl.ds(base, CHUNK), :]
        for j in range(CHUNK):
            at = pl.ds(pl.multiple_of((base + j) * STATE, STATE), STATE)
            state = jnp.exp2(steps[j : j + 1, :] * rate) * state + push_ref[at, :]
            states_ref[at, :] = state.astype(bf16)
        return state

    lax.fori_loop(0, LEN // CHUNK, chunk, jnp.zeros((STATE, lanes), f32))

    def output(index, carry):
        for rows, many in chunk_group(index):
            ys_ref[rows, :] = matmul(c_ref[rows, :], states_ref[many, :])
        return carry

    lax.fori_loop(0, LEN // CHUNK // GROUP, output, 0)
    ys = ys_ref[...] + skip_ref[...] * u_ref[...]
    ys_ref[...] = ys
    zs = xz_ref[0]
    gated = (ys * (zs * sigmoid(zs))).astype(bf16)
    gated_ref[...] = gated
    part = matmul(gated, out_w_ref[...])

    @pl.when(step == 0)
    def _():
        total_ref[...] = part

    @pl.when(step > 0)
    def _():
        total_ref[...] += part

    @pl.when(step == pl.num_programs(0) - 1)
    def _():
        store_blocks(out_refs, total_ref[...])


def scan_backward_kernel(
    blocks,
    me_ref,
    proj_ref,
    dt_proj_ref,
    bias_ref,
    alog_ref,
    skip_ref,
    u_ref,
    xz_ref,
    out_w_ref,
    ys_ref,
    states_ref,
    *rest,
):
    grad_refs = rest[:blocks]
    (
        du_ref,
        dzs_ref,
        small_ref,
        dalog_ref,
        ddt_ref,
        dcols_ref,
        grad_ref,
        cols_ref,
        b_ref,
        c_ref,
        pb_ref,
        pc_ref,
        delta_ref,
        drive_ref,
        dys_ref,
        ddrive_ref,
        drate_ref,
        dlow_ref,
        push_ref,
        grads_ref,
        rates_ref,
    ) = rest[blocks:]
    me = me_ref[0]
    size = LEN // blocks
    lanes = u_ref.shape[1]
    step = pl.program_id(0)

    @pl.when(step == 0)
    def _():
        scan_setup(proj_ref, cols_ref, b_ref, c_ref)
        join_blocks(grad_refs, grad_ref)
        pb_ref[...] = jnp.zeros(pb_ref.shape, f32)
        pc_ref[...] = jnp.zeros(pc_ref.shape, f32)

    low, pre, delta = step_sizes(cols_ref, dt_proj_ref, bias_ref)
    u = u_ref[...]
    delta_ref[...] = delta
    drive_ref[...] = (delta * u).astype(bf16)
    dgated = times_transposed(grad_ref[...], out_w_ref[...])
    zs = xz_ref[0]
    gate = sigmoid(zs)
    dys = dgated * (zs * gate)
    dys_ref[...] = dys.astype(bf16)
    dzs_ref[...] = (dgated * ys_ref[...] * (gate * (1.0 + zs * (1.0 - gate)))).astype(bf16)
    a_matrix = -jnp.exp(alog_ref[...])
    rate = a_matrix * LOG2E
    chunks = LEN // CHUNK
    mask = chunk_mask(CHUNK)
    push_chunks(c_ref, dys_ref, push_ref)

    def chunk(step_index, carry):
        adjoint, da = carry
        index = chunks - 1 - step_index
        base = chunk_place(index, me, size)
        before = chunk_place(jnp.maximum(index - 1, 0), me, size)
        first = (index > 0).astype(f32)
        steps = delta_ref[pl.ds(base, CHUNK), :]
        for j in range(CHUNK - 1, -1, -1):
            at = pl.ds(pl.multiple_of((base + j) * STATE, STATE), STATE)
            if j > 0:
                last = (base + j - 1) * STATE
                earlier = states_ref[pl.ds(pl.multiple_of(last, STATE), STATE), :].astype(f32)
            else:
                last = (before + CHUNK - 1) * STATE
                earlier = states_ref[pl.ds(pl.multiple_of(last, STATE), STATE), :].astype(f32) * first
            grad = adjoint + push_ref[at, :]
            grads_ref[at, :] = grad.astype(bf16)
            adjoint = grad * jnp.exp2(steps[j : j + 1, :] * rate)
            through = adjoint * earlier
            rates_ref[at, :] = (through * a_matrix).astype(bf16)
            da = da + through * steps[j : j + 1, :]
        return adjoint, da

    zero = jnp.zeros((STATE, lanes), f32)
    _, da = lax.fori_loop(0, chunks, chunk, (zero, zero))
    mask_low = mask.astype(bf16)

    def output(index, carry):
        for rows, many in chunk_group(index):
            grads = grads_ref[many, :]
            ddrive_ref[rows, :] = matmul(b_ref[rows, :], grads)
            drate_ref[rows, :] = matmul(mask_low, rates_ref[many, :])
            pb_ref[rows, :] += times_transposed(drive_ref[rows, :], grads) * mask
            pc_ref[rows, :] += times_transposed(dys_ref[rows, :], states_ref[many, :]) * mask
        return carry

    lax.fori_loop(0, chunks // GROUP, output, 0)
    dalog_ref[...] = da * a_matrix
    ddrive = ddrive_ref[...]
    du_ref[...] = ddrive * delta + skip_ref[...] * dys
    dpre = (ddrive * u + drate_ref[...]) * sigmoid(pre)
    dpre_low = dpre.astype(bf16)
    small_ref[...] = jnp.concatenate(
        [
            jnp.sum(dpre, axis=0, keepdims=True),
            jnp.sum(dys * u, axis=0, keepdims=True),
            jnp.zeros((6, lanes), f32),
        ],
        axis=0,
    )
    ddt_ref[...] = transposed_times(low, dpre_low)
    part = times_transposed(dpre_low, dt_proj_ref[...])

    @pl.when(step == 0)
    def _():
        dlow_ref[...] = part

    @pl.when(step > 0)
    def _():
        dlow_ref[...] += part

    @pl.when(step == pl.num_programs(0) - 1)
    def _():
        collect = (
            lax.broadcasted_iota(jnp.int32, (CHUNK * STATE, STATE), 0) % STATE
            == lax.broadcasted_iota(jnp.int32, (CHUNK * STATE, STATE), 1)
        ).astype(f32)
        dcols_ref[...] = jnp.concatenate(
            [dlow_ref[...], dot_exact(pb_ref[...], collect), dot_exact(pc_ref[...], collect)], axis=1
        )


def conv_backward_kernel(
    blocks,
    me_ref,
    dcols_ref,
    proj_ref,
    u_ref,
    xz_ref,
    du_ref,
    weight_ref,
    xproj_ref,
    dxs_ref,
    dxproj_ref,
    dweight_ref,
    pad_ref,
    grad_ref,
):
    me = me_ref[0]
    size = LEN // blocks
    lanes = u_ref.shape[1]
    projected = proj_ref[...]
    scale, in_step, in_b, in_c, mean_b, mean_c = column_norm_parts(projected)
    normed = projected * scale
    dcols = dcols_ref[...]
    product = dcols * normed
    dot_step = jnp.sum(jnp.where(in_step, product, 0.0), axis=1, keepdims=True) / DT_RANK
    dot_b = jnp.sum(jnp.where(in_b, product, 0.0), axis=1, keepdims=True) / STATE
    dot_c = jnp.sum(jnp.where(in_c, product, 0.0), axis=1, keepdims=True) / STATE
    dot_b = jnp.where(mean_b > floor_square, dot_b, 0.0)
    dot_c = jnp.where(mean_c > floor_square, dot_c, 0.0)
    mean = jnp.where(in_step, dot_step, jnp.where(in_b, dot_b, dot_c))
    dproj = (scale * (dcols - normed * mean)).astype(bf16)
    dxproj_ref[...] = transposed_times(dproj, u_ref[...].astype(bf16))
    du = du_ref[...] + times_transposed(dproj, xproj_ref[...])
    pad_ref[0:PAD, :] = jnp.zeros((PAD, lanes), f32)
    grad_ref[LEN : LEN + PAD, :] = jnp.zeros((PAD, lanes), f32)
    for m in range(blocks):
        at = pl.multiple_of(jnp.bitwise_xor(me, m) * size, size)
        pad_ref[PAD + m * size : PAD + (m + 1) * size, :] = xz_ref[0, pl.ds(at, size), :]
    dxs_ref[...] = du.astype(bf16)
    du_ref_rows = []
    grad_ref[0:LEN, :] = du
    total = conv_total(pad_ref, weight_ref, LEN)
    gate = sigmoid(total)
    slope = gate * (1.0 + total * (1.0 - gate))
    for m in range(blocks):
        at = pl.multiple_of(jnp.bitwise_xor(me, m) * size, size)
        du_ref_rows.append(grad_ref[pl.ds(at, size), :])
    grad_ref[0:LEN, :] = jnp.concatenate(du_ref_rows, axis=0) * slope
    dcv = grad_ref[0:LEN, :]
    dweight_ref[...] = jnp.concatenate(
        [
            jnp.sum(dcv * pad_ref[pl.ds(PAD - CONV + 1 + tap, LEN), :], axis=0, keepdims=True)
            for tap in range(CONV)
        ],
        axis=0,
    )
    dxs = weight_ref[CONV - 1 : CONV, :] * dcv
    for tap in range(CONV - 1):
        dxs = dxs + weight_ref[tap : tap + 1, :] * grad_ref[pl.ds(CONV - 1 - tap, LEN), :]
    dxs = dxs.astype(bf16)
    for m in range(blocks):
        at = pl.multiple_of(jnp.bitwise_xor(me, m) * size, size)
        dxs_ref[pl.ds(at, size), :] = dxs[m * size : (m + 1) * size, :]


def store_blocks(refs, value):
    size = value.shape[0] // len(refs)
    for k, ref in enumerate(refs):
        ref[...] = value[k * size : (k + 1) * size].astype(ref.dtype)


def join_blocks(refs, out_ref):
    size = out_ref.shape[0] // len(refs)
    for k, ref in enumerate(refs):
        out_ref[k * size : (k + 1) * size, :] = ref[...]


SMEM = pl.BlockSpec(memory_space=pltpu.SMEM)


def whole(shape):
    return pl.BlockSpec(shape, lambda *_: (0,) * len(shape))


def params():
    return pltpu.CompilerParams(vmem_limit_bytes=VMEM_LIMIT)


def takes(microseconds):
    return pl.CostEstimate(
        flops=int(microseconds * 1.15e9), bytes_accessed=1 << 20, transcendentals=0
    )


def shape_of(shape, dtype=f32):
    return jax.ShapeDtypeStruct(shape, dtype)


def conv_forward(me, blocks, xz, weight, x_proj):
    channels = xz.shape[2]
    return pl.pallas_call(
        functools.partial(conv_forward_kernel, blocks),
        grid=(1,),
        in_specs=[
            SMEM,
            pl.BlockSpec((1, LEN, channels), lambda i: (0, 0, 0)),
            whole(weight.shape),
            whole(x_proj.shape),
        ],
        out_specs=(whole((LEN, channels)), whole((LEN, 128))),
        out_shape=(shape_of((LEN, channels)), shape_of((LEN, 128))),
        scratch_shapes=[pltpu.VMEM((LEN + PAD, channels), f32)],
        compiler_params=params(),
        cost_estimate=takes(3),
        name="conv_forward",
    )(me, xz, weight, x_proj)


def lane_block(channels):
    return channels


def scan_forward(me, blocks, proj, dt_proj, bias, alog, skip, u, xz, out_w):
    channels = u.shape[1]
    lanes = lane_block(channels)
    col = lambda i: (0, i)
    return pl.pallas_call(
        functools.partial(scan_forward_kernel, blocks),
        grid=(channels // lanes,),
        in_specs=[
            SMEM,
            whole((LEN, 128)),
            pl.BlockSpec((DT_RANK, lanes), col),
            pl.BlockSpec((1, lanes), col),
            pl.BlockSpec((STATE, lanes), col),
            pl.BlockSpec((1, lanes), col),
            pl.BlockSpec((LEN, lanes), col),
            pl.BlockSpec((1, LEN, lanes), lambda i: (1, 0, i)),
            pl.BlockSpec((lanes, D), lambda i: (i, 0)),
        ],
        out_specs=(
            pl.BlockSpec((LEN, lanes), col),
            pl.BlockSpec((LEN, lanes), col),
            pl.BlockSpec((LEN * STATE, lanes), col),
        )
        + (whole((LEN // blocks, D)),) * blocks,
        out_shape=(
            shape_of((LEN, channels), bf16),
            shape_of((LEN, channels)),
            shape_of((LEN * STATE, channels), bf16),
        )
        + (shape_of((LEN // blocks, D), bf16),) * blocks,
        scratch_shapes=[
            pltpu.VMEM((LEN, 128), f32),
            pltpu.VMEM((LEN, CHUNK * STATE), bf16),
            pltpu.VMEM((LEN, CHUNK * STATE), bf16),
            pltpu.VMEM((LEN, lanes), f32),
            pltpu.VMEM((LEN, lanes), bf16),
            pltpu.VMEM((LEN * STATE, lanes), f32),
            pltpu.VMEM((LEN, D), f32),
        ],
        compiler_params=params(),
        cost_estimate=takes(13),
        name="scan_forward",
    )(me, proj, dt_proj, bias, alog, skip, u, xz, out_w)


def scan_backward(me, blocks, proj, dt_proj, bias, alog, skip, u, xz, out_w, grad, ys, states):
    channels = u.shape[1]
    lanes = lane_block(channels)
    col = lambda i: (0, i)
    rows = pl.BlockSpec((LEN, lanes), col)
    return pl.pallas_call(
        functools.partial(scan_backward_kernel, blocks),
        grid=(channels // lanes,),
        in_specs=[
            SMEM,
            whole((LEN, 128)),
            pl.BlockSpec((DT_RANK, lanes), col),
            pl.BlockSpec((1, lanes), col),
            pl.BlockSpec((STATE, lanes), col),
            pl.BlockSpec((1, lanes), col),
            rows,
            pl.BlockSpec((1, LEN, lanes), lambda i: (1, 0, i)),
            pl.BlockSpec((lanes, D), lambda i: (i, 0)),
            rows,
            pl.BlockSpec((LEN * STATE, lanes), col),
        ]
        + [whole((LEN // blocks, D))] * blocks,
        out_specs=(
            rows,
            rows,
            pl.BlockSpec((8, lanes), col),
            pl.BlockSpec((STATE, lanes), col),
            pl.BlockSpec((DT_RANK, lanes), col),
            whole((LEN, 128)),
        ),
        out_shape=(
            shape_of((LEN, channels)),
            shape_of((LEN, channels), bf16),
            shape_of((8, channels)),
            shape_of((STATE, channels)),
            shape_of((DT_RANK, channels)),
            shape_of((LEN, 128)),
        ),
        scratch_shapes=[
            pltpu.VMEM((LEN, D), bf16),
            pltpu.VMEM((LEN, 128), f32),
            pltpu.VMEM((LEN, CHUNK * STATE), bf16),
            pltpu.VMEM((LEN, CHUNK * STATE), bf16),
            pltpu.VMEM((LEN, CHUNK * STATE), f32),
            pltpu.VMEM((LEN, CHUNK * STATE), f32),
            pltpu.VMEM((LEN, lanes), f32),
            pltpu.VMEM((LEN, lanes), bf16),
            pltpu.VMEM((LEN, lanes), bf16),
            pltpu.VMEM((LEN, lanes), f32),
            pltpu.VMEM((LEN, lanes), f32),
            pltpu.VMEM((LEN, DT_RANK), f32),
            pltpu.VMEM((LEN * STATE, lanes), f32),
            pltpu.VMEM((LEN * STATE, lanes), bf16),
            pltpu.VMEM((LEN * STATE, lanes), bf16),
        ],
        compiler_params=params(),
        cost_estimate=takes(21),
        name="scan_backward",
    )(me, proj, dt_proj, bias, alog, skip, u, xz, out_w, ys, states, *grad)


def conv_backward(me, blocks, dcols, proj, u, xz, du, weight, x_proj):
    channels = u.shape[1]
    return pl.pallas_call(
        functools.partial(conv_backward_kernel, blocks),
        grid=(1,),
        in_specs=[
            SMEM,
            whole((LEN, 128)),
            whole((LEN, 128)),
            whole((LEN, channels)),
            pl.BlockSpec((1, LEN, channels), lambda i: (0, 0, 0)),
            whole((LEN, channels)),
            whole(weight.shape),
            whole(x_proj.shape),
        ],
        out_specs=(whole((LEN, channels)), whole((128, channels)), whole((CONV, channels))),
        out_shape=(
            shape_of((LEN, channels), bf16),
            shape_of((128, channels)),
            shape_of((CONV, channels)),
        ),
        scratch_shapes=[
            pltpu.VMEM((LEN + PAD, channels), f32),
            pltpu.VMEM((LEN + PAD, channels), f32),
        ],
        compiler_params=params(),
        cost_estimate=takes(5),
        name="conv_backward",
    )(me, dcols, proj, u, xz, du, weight, x_proj)


def attention_probabilities(q, k, allowed):
    scores = times_transposed(q, k) * (1.0 / math.sqrt(HEAD_DIM))
    scores = jnp.where(allowed, scores, masked_score)
    peak = jnp.max(scores, axis=1, keepdims=True)
    exponent = jnp.exp(scores - peak)
    return exponent / jnp.sum(exponent, axis=1, keepdims=True)


def causal(me, blocks):
    size = LEN // blocks

    def position(axis):
        index = lax.broadcasted_iota(jnp.int32, (LEN, LEN), axis)
        return jnp.bitwise_xor(index // size, me) * size + index % size

    return position(1) <= position(0)


def attention_forward_kernel(
    blocks, me_ref, wq_ref, wkv_ref, wo_ref, *rest
):
    joined_ref, q_ref, kv_ref, o_ref = rest[blocks : blocks + 4]
    out_refs = rest[blocks + 4 :]
    join_blocks(rest[:blocks], joined_ref)
    normed = joined_ref[...]
    q_ref[...] = matmul(normed, wq_ref[...]).astype(bf16)
    kv_ref[...] = matmul(normed, wkv_ref[...]).astype(bf16)
    kv_heads = wkv_ref.shape[1] // (2 * HEAD_DIM)
    group = HEADS // KV_HEADS
    allowed = causal(me_ref[0], blocks)
    outs = []
    for head in range(kv_heads * group):
        kv = head // group
        q = q_ref[:, head * HEAD_DIM : (head + 1) * HEAD_DIM]
        k = kv_ref[:, kv * HEAD_DIM : (kv + 1) * HEAD_DIM]
        v = kv_ref[:, (kv_heads + kv) * HEAD_DIM : (kv_heads + kv + 1) * HEAD_DIM]
        soft = attention_probabilities(q, k, allowed)
        outs.append(matmul(soft.astype(bf16), v).astype(bf16))
    o_ref[...] = jnp.concatenate(outs, axis=1)
    store_blocks(out_refs, matmul(o_ref[...], wo_ref[...]))


def attention_backward_kernel(
    blocks,
    me_ref,
    q_ref,
    kv_ref,
    wq_ref,
    wkv_ref,
    wo_ref,
    *rest,
):
    dqkv_ref, grad_ref = rest[blocks], rest[-1]
    join_blocks(rest[:blocks], grad_ref)
    dout = times_transposed(grad_ref[...], wo_ref[...]).astype(bf16)
    kv_heads = wkv_ref.shape[1] // (2 * HEAD_DIM)
    group = HEADS // KV_HEADS
    allowed = causal(me_ref[0], blocks)
    scale = 1.0 / math.sqrt(HEAD_DIM)
    dqs, dks, dvs = [], [], []
    for kv in range(kv_heads):
        k = kv_ref[:, kv * HEAD_DIM : (kv + 1) * HEAD_DIM]
        v = kv_ref[:, (kv_heads + kv) * HEAD_DIM : (kv_heads + kv + 1) * HEAD_DIM]
        dk = jnp.zeros((LEN, HEAD_DIM), f32)
        dv = jnp.zeros((LEN, HEAD_DIM), f32)
        for head in range(kv * group, (kv + 1) * group):
            q = q_ref[:, head * HEAD_DIM : (head + 1) * HEAD_DIM]
            do = dout[:, head * HEAD_DIM : (head + 1) * HEAD_DIM]
            soft = attention_probabilities(q, k, allowed)
            dsoft = times_transposed(do, v)
            dscore = soft * (dsoft - jnp.sum(soft * dsoft, axis=1, keepdims=True))
            dscore = dscore.astype(bf16)
            dqs.append((matmul(dscore, k) * scale).astype(bf16))
            dk = dk + transposed_times(dscore, q) * scale
            dv = dv + transposed_times(soft.astype(bf16), do)
        dks.append(dk.astype(bf16))
        dvs.append(dv.astype(bf16))
    dq = jnp.concatenate(dqs, axis=1)
    dkv = jnp.concatenate(dks + dvs, axis=1)
    dqkv_ref[:, : dq.shape[1]] = dq
    dqkv_ref[:, dq.shape[1] :] = dkv
    dn = times_transposed(dq, wq_ref[...]) + times_transposed(dkv, wkv_ref[...])
    store_blocks(rest[blocks + 1 : -1], dn)


def attention_forward(me, blocks, normed, wq, wkv, wo):
    size = LEN // blocks
    heads = shape_of((LEN, wq.shape[1]), bf16)
    kept = (shape_of((LEN, D), bf16), heads, shape_of((LEN, wkv.shape[1]), bf16), heads)
    return pl.pallas_call(
        functools.partial(attention_forward_kernel, blocks),
        grid=(1,),
        in_specs=[SMEM, whole(wq.shape), whole(wkv.shape), whole(wo.shape)]
        + [whole((size, D))] * blocks,
        out_specs=tuple(whole(item.shape) for item in kept) + (whole((size, D)),) * blocks,
        out_shape=kept + (shape_of((size, D), bf16),) * blocks,
        compiler_params=params(),
        cost_estimate=takes(6),
        name="attention_forward",
    )(me, wq, wkv, wo, *normed)


def attention_backward(me, blocks, grad, q, kv, wq, wkv, wo):
    size = LEN // blocks
    cols = wq.shape[1] + wkv.shape[1]
    return pl.pallas_call(
        functools.partial(attention_backward_kernel, blocks),
        grid=(1,),
        in_specs=[
            SMEM,
            whole(q.shape),
            whole(kv.shape),
            whole(wq.shape),
            whole(wkv.shape),
            whole(wo.shape),
        ]
        + [whole((size, D))] * blocks,
        out_specs=(whole((LEN, cols)),) + (whole((size, D)),) * blocks,
        out_shape=(shape_of((LEN, cols), bf16),) + (shape_of((size, D), bf16),) * blocks,
        scratch_shapes=[pltpu.VMEM((LEN, D), bf16)],
        compiler_params=params(),
        cost_estimate=takes(8),
        name="attention_backward",
    )(me, q, kv, wq, wkv, wo, *grad)


def norm_forward_kernel(hidden_ref, gain_ref, *rest):
    part_refs, (out_ref, normed_ref) = rest[:-2], rest[-2:]
    hidden = hidden_ref[...]
    for ref in part_refs:
        hidden = hidden + ref[...].astype(f32)
    scale = lax.rsqrt(jnp.mean(hidden * hidden, axis=1, keepdims=True) + epsilon)
    out_ref[...] = hidden
    normed_ref[...] = (hidden * scale * gain_ref[...]).astype(bf16)


def norm_forward(hidden, gain, parts):
    shape = hidden.shape
    return pl.pallas_call(
        norm_forward_kernel,
        grid=(1,),
        in_specs=[whole(shape), whole((1, D))] + [whole(shape)] * len(parts),
        out_specs=(whole(shape), whole(shape)),
        out_shape=(shape_of(shape), shape_of(shape, bf16)),
        compiler_params=params(),
        cost_estimate=takes(2),
        name="norm_forward",
    )(hidden, gain, *parts)


def pull_norm(grad, hidden, gain):
    scale = lax.rsqrt(jnp.mean(hidden * hidden, axis=1, keepdims=True) + epsilon)
    unit = hidden * scale
    through = grad * gain
    back = scale * (through - unit * jnp.mean(through * unit, axis=1, keepdims=True))
    return back, jnp.sum(grad * unit, axis=0, keepdims=True)


def norm_backward_kernel(grad_ref, hidden_ref, gain_ref, *rest):
    part_refs, (out_ref, low_ref, dgain_ref) = rest[:-3], rest[-3:]
    dn = part_refs[0][...].astype(f32)
    for ref in part_refs[1:]:
        dn = dn + ref[...].astype(f32)
    back, dgain = pull_norm(dn, hidden_ref[...], gain_ref[...])
    grad = grad_ref[...] + back
    out_ref[...] = grad
    low_ref[...] = grad.astype(bf16)
    dgain_ref[...] = dgain


def norm_backward(grad, hidden, gain, parts):
    shape = hidden.shape
    return pl.pallas_call(
        norm_backward_kernel,
        grid=(1,),
        in_specs=[whole(shape), whole(shape), whole((1, D))] + [whole(shape)] * len(parts),
        out_specs=(whole(shape), whole(shape), whole((1, D))),
        out_shape=(shape_of(shape), shape_of(shape, bf16), shape_of((1, D))),
        compiler_params=params(),
        cost_estimate=takes(2.5),
        name="norm_backward",
    )(grad, hidden, gain, *parts)


def router_backward_kernel(grad_ref, hidden_ref, gain_ref, normed_ref, picks_ref, router_ref, *rest):
    part_refs, (out_ref, low_ref, dgain_ref, drouter_ref) = rest[:-4], rest[-4:]
    dn = part_refs[0][...].astype(f32)
    for ref in part_refs[1:]:
        dn = dn + ref[...].astype(f32)
    normed, router = normed_ref[...], router_ref[...]
    rows = normed.shape[0]
    ids = lax.broadcasted_iota(jnp.int32, (rows, EXPERTS), 1)
    logits = times_transposed(normed, router)
    hot = [(ids == picks_ref[:, k : k + 1]).astype(f32) for k in (0, 1)]
    chosen = [jnp.sum(hot[k] * logits, axis=1, keepdims=True) for k in (0, 1)]
    peak = jnp.maximum(chosen[0], chosen[1])
    weight = [jnp.exp(value - peak) for value in chosen]
    total = weight[0] + weight[1]
    weight = [value / total for value in weight]
    dw = [dn[:, D + k : D + k + 1] for k in (0, 1)]
    mean = weight[0] * dw[0] + weight[1] * dw[1]
    dlog = sum(hot[k] * (weight[k] * (dw[k] - mean)) for k in (0, 1)).astype(bf16)
    dn = dn[:, :D] + matmul(dlog, router)
    back, dgain = pull_norm(dn, hidden_ref[...], gain_ref[...])
    grad = grad_ref[...].astype(f32) + back
    out_ref[...] = grad
    low_ref[...] = grad.astype(bf16)
    dgain_ref[...] = dgain
    drouter_ref[...] = transposed_times(dlog, normed)


def router_backward(grad, hidden, gain, normed, picks, router, parts):
    shape = hidden.shape
    wide_rows = whole((shape[0], D + 128))
    return pl.pallas_call(
        router_backward_kernel,
        grid=(1,),
        in_specs=[
            whole(shape),
            whole(shape),
            whole((1, D)),
            whole(shape),
            whole((shape[0], 2)),
            whole((EXPERTS, D)),
        ]
        + [wide_rows] * len(parts),
        out_specs=(whole(shape), whole(shape), whole((1, D)), whole((EXPERTS, D))),
        out_shape=(
            shape_of(shape),
            shape_of(shape, bf16),
            shape_of((1, D)),
            shape_of((EXPERTS, D)),
        ),
        compiler_params=params(),
        cost_estimate=takes(3),
        name="router_backward",
    )(grad, hidden, gain, normed, picks, router, *parts)


def experts_kernel(blocks, routes_ref, router_ref, w_in_ref, w_out_ref, *rest):
    normed_refs, grad_refs = rest[:blocks], rest[blocks : 2 * blocks]
    moved_ref, act_ref, weighted_ref = rest[2 * blocks : 2 * blocks + 3]
    dn_refs = rest[2 * blocks + 3 : 3 * blocks + 3]
    (
        normed_ref,
        grad_ref,
        even_ref,
        odd_ref,
        grads_ref,
        place_ref,
        first_ref,
        second_ref,
        scale_ref,
        back_ref,
        kept_ref,
        dw_ref,
    ) = rest[3 * blocks + 3 :]
    expert = pl.program_id(0)
    slots = EXPERTS * CAP
    units = w_out_ref.shape[1]

    @pl.when(expert == 0)
    def _():
        join_blocks(normed_refs, normed_ref)
        join_blocks(grad_refs, grad_ref)
        routes = routes_ref[...]
        ids = lax.broadcasted_iota(jnp.int32, (EXPERTS, LEN), 0)
        hot = [(ids == routes[k : k + 1, :]).astype(f32) for k in (0, 1)]
        earlier = (
            lax.broadcasted_iota(jnp.int32, (LEN, LEN), 0)
            < lax.broadcasted_iota(jnp.int32, (LEN, LEN), 1)
        ).astype(bf16)
        rank0 = matmul(hot[0].astype(bf16), earlier)
        rank1 = matmul(hot[1].astype(bf16), earlier) + jnp.sum(hot[0], axis=1, keepdims=True)
        first = ids.astype(f32) * CAP
        position = [
            jnp.sum(hot[k] * (first + rank), axis=0, keepdims=True).astype(jnp.int32)
            for k, rank in ((0, rank0), (1, rank1))
        ]
        logits = times_transposed(router_ref[...], normed_ref[...])
        chosen = [jnp.sum(hot[k] * logits, axis=0, keepdims=True) for k in (0, 1)]
        peak = jnp.maximum(chosen[0], chosen[1])
        weight = [jnp.exp(value - peak) for value in chosen]
        total = weight[0] + weight[1]
        weight = [value / total for value in weight]
        slot = lax.broadcasted_iota(jnp.int32, (slots, LEN), 0)
        in0 = (slot == position[0]).astype(f32)
        in1 = (slot == position[1]).astype(f32)
        weighted = in0 * weight[0] + in1 * weight[1]
        place = (in0 + in1).astype(bf16)
        first_ref[...] = in0.astype(bf16)
        second_ref[...] = in1.astype(bf16)
        place_ref[...] = place
        weighted_ref[...] = weighted.astype(bf16)
        scale_ref[...] = jnp.broadcast_to(jnp.sum(weighted, axis=1, keepdims=True), (slots, 128))
        grads_ref[...] = matmul(place, grad_ref[...]).astype(bf16)
        spread = lax.broadcasted_iota(jnp.int32, (128, 256), 1) - 2 * lax.broadcasted_iota(
            jnp.int32, (128, 256), 0
        )
        for block in range(D // 128):
            rows = matmul(place, normed_ref[:, block * 128 : (block + 1) * 128]).astype(bf16)
            cols = slice(block * 256, (block + 1) * 256)
            even_ref[:, cols] = matmul(rows, (spread == 0).astype(bf16)).astype(bf16)
            odd_ref[:, cols] = matmul(rows, (spread == 1).astype(bf16)).astype(bf16)

    mine = pl.ds(pl.multiple_of(expert * CAP, CAP), CAP)
    w_in = w_in_ref[0].reshape(2 * D, units)
    w_out = w_out_ref[0]
    both = matmul(jnp.concatenate([even_ref[mine, :], odd_ref[mine, :]], axis=0), w_in)
    gate, up = both[:CAP], both[CAP:]
    sig = sigmoid(gate)
    silu = gate * sig
    act = silu * up
    act_low = act.astype(bf16)
    act_ref[0] = act_low
    scale = scale_ref[mine, 0:1]
    plain = times_transposed(grads_ref[mine, :], w_out)
    dw_ref[mine, :] = jnp.broadcast_to(
        jnp.sum(plain * act_low.astype(f32), axis=1, keepdims=True), (CAP, 128)
    ).astype(bf16)
    dact = plain * scale
    dgate = (dact * sig * (1.0 + gate * (1.0 - sig)) * up).astype(bf16)
    dup = (dact * silu).astype(bf16)
    back = times_transposed(jnp.concatenate([dgate, dup], axis=0), w_in)
    lane = lax.broadcasted_iota(jnp.int32, (CAP, 2 * D), 1)
    back_ref[mine, :] = jnp.where(lane % 2 == 0, back[:CAP], back[CAP:]).astype(bf16)
    kept_ref[mine, :] = jnp.concatenate([dgate, dup, (act * scale).astype(bf16)], axis=1)

    @pl.when(expert == EXPERTS - 1)
    def _():
        pairs = (
            lax.broadcasted_iota(jnp.int32, (256, 128), 0) // 2
            == lax.broadcasted_iota(jnp.int32, (256, 128), 1)
        ).astype(bf16)
        size = LEN // blocks
        for block in range(D // 128):
            cols = slice(block * 256, (block + 1) * 256)
            wide_rows = transposed_times(place_ref[...], back_ref[:, cols]).astype(bf16)
            dn = matmul(wide_rows, pairs).astype(bf16)
            for k, ref in enumerate(dn_refs):
                ref[:, block * 128 : (block + 1) * 128] = dn[k * size : (k + 1) * size]
        lanes = lax.broadcasted_iota(jnp.int32, (LEN, 128), 1)
        gates = [transposed_times(ref[...], dw_ref[...]) for ref in (first_ref, second_ref)]
        gates = jnp.where(lanes == 0, gates[0], jnp.where(lanes == 1, gates[1], 0.0)).astype(bf16)
        for k, ref in enumerate(dn_refs):
            ref[:, D:] = gates[k * size : (k + 1) * size]
        for k, ref in enumerate((first_ref, second_ref)):
            moved_ref[:, k * 3 * units : (k + 1) * 3 * units] = transposed_times(
                ref[...], kept_ref[...]
            ).astype(bf16)


def experts(blocks, routes, router, normed, grad, w_in, w_out):
    units = w_out.shape[1]
    slots = EXPERTS * CAP
    size = LEN // blocks
    return pl.pallas_call(
        functools.partial(experts_kernel, blocks),
        grid=(EXPERTS,),
        in_specs=[
            whole((2, LEN)),
            whole((EXPERTS, D)),
            pl.BlockSpec((1, D, 2, units), lambda e: (e, 0, 0, 0)),
            pl.BlockSpec((1, units, D), lambda e: (e, 0, 0)),
        ]
        + [whole((size, D))] * (2 * blocks),
        out_specs=(
            whole((LEN, 6 * units)),
            pl.BlockSpec((1, CAP, units), lambda e: (e, 0, 0)),
            whole((slots, LEN)),
        )
        + (whole((size, D + 128)),) * blocks,
        out_shape=(
            shape_of((LEN, 6 * units), bf16),
            shape_of((EXPERTS, CAP, units), bf16),
            shape_of((slots, LEN), bf16),
        )
        + (shape_of((size, D + 128), bf16),) * blocks,
        scratch_shapes=[
            pltpu.VMEM((LEN, D), bf16),
            pltpu.VMEM((LEN, D), bf16),
            pltpu.VMEM((slots, 2 * D), bf16),
            pltpu.VMEM((slots, 2 * D), bf16),
            pltpu.VMEM((slots, D), bf16),
            pltpu.VMEM((slots, LEN), bf16),
            pltpu.VMEM((slots, LEN), bf16),
            pltpu.VMEM((slots, LEN), bf16),
            pltpu.VMEM((slots, 128), f32),
            pltpu.VMEM((slots, 2 * D), bf16),
            pltpu.VMEM((slots, 3 * units), bf16),
            pltpu.VMEM((slots, 128), bf16),
        ],
        compiler_params=params(),
        cost_estimate=takes(37),
        name="experts",
    )(routes, router, w_in, w_out, *normed, *grad)


def experts_out_kernel(act_ref, weighted_ref, w_out_ref, *rest):
    made_refs, ye_ref = rest[:-1], rest[-1]
    expert = pl.program_id(0)
    mine = pl.ds(pl.multiple_of(expert * CAP, CAP), CAP)
    ye_ref[mine, :] = matmul(act_ref[0], w_out_ref[0]).astype(bf16)

    @pl.when(expert == EXPERTS - 1)
    def _():
        store_blocks(made_refs, transposed_times(weighted_ref[...], ye_ref[...]))


def experts_out(blocks, act, weighted, w_out):
    units = w_out.shape[1]
    slots = EXPERTS * CAP
    return pl.pallas_call(
        experts_out_kernel,
        grid=(EXPERTS,),
        in_specs=[
            pl.BlockSpec((1, CAP, units), lambda e: (e, 0, 0)),
            whole((slots, LEN)),
            pl.BlockSpec((1, units, D), lambda e: (e, 0, 0)),
        ],
        out_specs=(whole((LEN // blocks, D)),) * blocks,
        out_shape=(shape_of((LEN // blocks, D), bf16),) * blocks,
        scratch_shapes=[pltpu.VMEM((slots, D), bf16)],
        compiler_params=params(),
        cost_estimate=takes(14),
        name="experts_out",
    )(act, weighted, w_out)


def sort_rows(refs, groups, out_ref):
    share = LEN // len(refs)
    for group in range(groups):
        for k, ref in enumerate(refs):
            at = group * LEN + k * share
            out_ref[at : at + share, :] = ref[group * share : (group + 1) * share, :]


def sorted_columns_kernel(groups, *refs):
    column_refs, (left_ref, right_ref, picks_ref, rows_ref) = refs[:-4], refs[-4:]
    width = left_ref.shape[0]
    sort_rows(column_refs, groups, rows_ref)
    left_ref[...] = rows_ref[:, :width].astype(f32).T.astype(bf16)
    right_ref[...] = rows_ref[:, width : 2 * width].astype(f32).T.astype(bf16)
    picks_ref[...] = rows_ref[:, 4 * width : 4 * width + 2].astype(f32)


def sorted_columns(groups, columns):
    tokens, width = groups * LEN, D // groups
    shapes = ((width, tokens), (width, tokens))
    return pl.pallas_call(
        functools.partial(sorted_columns_kernel, groups),
        grid=(1,),
        in_specs=[whole(item.shape) for item in columns],
        out_specs=tuple(whole(shape) for shape in shapes) + (whole((tokens, 2)),),
        out_shape=tuple(shape_of(shape, bf16) for shape in shapes) + (shape_of((tokens, 2)),),
        scratch_shapes=[pltpu.VMEM((tokens, columns[0].shape[1]), bf16)],
        compiler_params=params(),
        cost_estimate=takes(4),
        name="sorted_columns",
    )(*columns)


def expert_grad_kernel(first, moved_ref, left_ref, right_ref, picks_ref, *rest):
    din_ref, dout_ref = rest[-2:]
    units = moved_ref.shape[1] // 6
    which = (pl.program_id(0) + first).astype(f32)
    at0 = (picks_ref[:, 0:1] == which).astype(bf16)
    at1 = (picks_ref[:, 1:2] == which).astype(bf16)
    moved = moved_ref[:, : 3 * units] * at0 + moved_ref[:, 3 * units :] * at1
    din = matmul(left_ref[...], moved[:, : 2 * units])
    din_ref[0, :, 0, :] = din[:, :units]
    din_ref[0, :, 1, :] = din[:, units:]
    dout_ref[0] = matmul(right_ref[...], moved[:, 2 * units :])


def expert_grads(first, count, moved, left, right, picks, earlier=()):
    width = left.shape[0]
    units = moved.shape[1] // 6
    inputs = (moved, left, right, picks)
    return pl.pallas_call(
        functools.partial(expert_grad_kernel, first),
        grid=(count,),
        in_specs=[whole(item.shape) for item in inputs]
        + [pl.BlockSpec(memory_space=pl.ANY)] * len(earlier),
        out_specs=(
            pl.BlockSpec((1, width, 2, units), lambda e: (e + first, 0, 0, 0)),
            pl.BlockSpec((1, width, units), lambda e: (e + first, 0, 0)),
        ),
        out_shape=(
            shape_of((EXPERTS, width, 2, units)),
            shape_of((EXPERTS, width, units)),
        ),
        input_output_aliases={4: 0, 5: 1} if earlier else {},
        compiler_params=params(),
        cost_estimate=takes(1.5 * count),
        name="expert_grads",
    )(*inputs, *earlier)


def pack_columns_kernel(groups, lanes, *refs):
    in_refs, out_ref = refs[:-1], refs[-1]
    width = D // groups
    values = [ref[...].astype(f32) for ref in in_refs]
    rows = values[0].shape[0]
    for group in range(groups):
        parts = [
            value[:, group * width : (group + 1) * width] if value.shape[1] == D else value
            for value in values
        ]
        spare = lanes - sum(part.shape[1] for part in parts)
        if spare:
            parts.append(jnp.zeros((rows, spare), f32))
        whole_row = jnp.concatenate(parts, axis=1) if len(parts) > 1 else parts[0]
        out_ref[group] = whole_row.astype(bf16)


def pack_columns(groups, *values):
    width, rows = D // groups, values[0].shape[0]
    lanes = sum(width if value.shape[1] == D else value.shape[1] for value in values)
    if len(values) > 1:
        lanes += -lanes % 128
    return pl.pallas_call(
        functools.partial(pack_columns_kernel, groups, lanes),
        grid=(1,),
        in_specs=[whole(value.shape) for value in values],
        out_specs=whole((groups, rows, lanes)),
        out_shape=shape_of((groups, rows, lanes), bf16),
        compiler_params=params(),
        cost_estimate=takes(3),
        name="pack_columns",
    )(*values)


def mix_grad_kernel(groups, normed_ref, first_ref, second_ref, *refs):
    extra_refs, out_ref = refs[:-1], refs[-1]
    width = D // groups
    grads = [
        transposed_times(normed_ref[...], ref[...]).astype(bf16) for ref in (first_ref, second_ref)
    ]
    channels = grads[0].shape[1]
    share = channels // groups
    extras = [ref[...] for ref in extra_refs]
    for group in range(groups):
        at = 0
        for grad in grads:
            out_ref[group, at : at + width, :] = grad[group * width : (group + 1) * width]
            at += width
        for extra in extras:
            if extra.shape[0] > STATE:
                count = extra.shape[0] // groups
                part = extra[group * count : (group + 1) * count]
            else:
                count = extra.shape[0]
                part = extra[:, group * share : (group + 1) * share]
                part = jnp.concatenate([part, jnp.zeros((count, channels - share), f32)], axis=1)
            spare = -count % 16
            if spare:
                part = jnp.concatenate([part, jnp.zeros((spare, channels), f32)], axis=0)
            out_ref[group, at : at + count + spare, :] = part.astype(bf16)
            at += count + spare


def mix_grads(groups, normed, first, second, *extras):
    channels = first.shape[1]
    rows = 2 * (D // groups)
    for extra in extras:
        count = extra.shape[0] // groups if extra.shape[0] > STATE else extra.shape[0]
        rows += count + -count % 16
    return pl.pallas_call(
        functools.partial(mix_grad_kernel, groups),
        grid=(1,),
        in_specs=[whole(item.shape) for item in (normed, first, second) + extras],
        out_specs=whole((groups, rows, channels)),
        out_shape=shape_of((groups, rows, channels), bf16),
        compiler_params=params(),
        cost_estimate=takes(7),
        name="mix_grads",
    )(normed, first, second, *extras)


def out_grad_kernel(groups, first, heads_ref, acted_ref, *rest):
    column_refs, out_refs, rows_ref = rest[:-3], rest[-3:-1], rest[-1]
    width = out_refs[0].shape[0]
    sort_rows(column_refs, groups, rows_ref)
    for k, (left_ref, out_ref) in enumerate(zip((heads_ref, acted_ref), out_refs)):
        columns = rows_ref[:, (first + k) * width : (first + k + 1) * width]
        out_ref[...] = transposed_times(columns, left_ref[...])


def out_grads(groups, first, columns, heads, acted):
    width = D // groups
    lefts = (heads, acted)
    return pl.pallas_call(
        functools.partial(out_grad_kernel, groups, first),
        grid=(1,),
        in_specs=[whole(item.shape) for item in lefts + tuple(columns)],
        out_specs=tuple(whole((width, item.shape[1])) for item in lefts),
        out_shape=tuple(shape_of((width, item.shape[1])) for item in lefts),
        scratch_shapes=[pltpu.VMEM((groups * LEN, columns[0].shape[1]), bf16)],
        compiler_params=params(),
        cost_estimate=takes(6),
        name="out_grads",
    )(*lefts, *columns)


def last_grad_kernel(groups, gated_ref, *rest):
    column_refs, (out_ref, sums_ref, rows_ref) = rest[:-3], rest[-3:]
    share = LEN // len(column_refs)
    stride = column_refs[0].shape[0] // groups
    sums = jnp.zeros(sums_ref.shape, f32)
    for group in range(groups):
        for k, ref in enumerate(column_refs):
            at = group * LEN + k * share
            first = group * stride
            rows_ref[at : at + share, :] = ref[first : first + share, :]
            sums = sums + ref[first + share : first + stride, :].astype(f32)
    sums_ref[...] = sums
    out_ref[...] = transposed_times(rows_ref[...], gated_ref[...])


def last_grads(groups, columns, gated):
    width = D // groups
    extra = columns[0].shape[0] // groups - LEN // len(columns)
    shapes = ((width, gated.shape[1]), (extra, width))
    return pl.pallas_call(
        functools.partial(last_grad_kernel, groups),
        grid=(1,),
        in_specs=[whole(gated.shape)] + [whole(item.shape) for item in columns],
        out_specs=tuple(whole(shape) for shape in shapes),
        out_shape=tuple(shape_of(shape) for shape in shapes),
        scratch_shapes=[pltpu.VMEM((groups * LEN, width), bf16)],
        compiler_params=params(),
        cost_estimate=takes(5),
        name="last_grads",
    )(gated, *columns)


def shards(
    tokens,
    cotangent,
    norm_gains,
    mix_in,
    conv_weight,
    x_proj,
    dt_proj,
    dt_bias,
    a_log,
    skip_gain,
    mix_out,
    ffn_in,
    ffn_out,
    attn_query,
    attn_keyval,
    attn_out,
    router,
    expert_in,
    expert_out,
    routes,
):
    members = lax.axis_size("tensor")
    member = lax.axis_index("tensor")
    share = LEN // members
    groups = lax.axis_size("dp")
    gains = norm_gains.astype(f32)
    me = member.astype(jnp.int32).reshape(1)

    def swap(value, k):
        return lax.ppermute(value, "tensor", [(i, i ^ k) for i in range(members)])

    def join_list(rows):
        return [rows] + [swap(rows, k) for k in range(1, members)]

    def join(rows):
        return jnp.concatenate(join_list(rows), axis=0)

    def split_list(blocks):
        return [blocks[0]] + [swap(blocks[k], k) for k in range(1, members)]

    def blocks_of(partial):
        return [partial[k * share : (k + 1) * share].astype(bf16) for k in range(members)]

    def all_sum(partial):
        total = partial.astype(f32)
        for k in range(1, members):
            total = total + swap(partial, k).astype(f32)
        return total

    def all_sum_rows(partial):
        total = partial.astype(f32)
        for k in range(1, members):
            blocks = swap(partial, k).reshape(members, share, -1)
            ordered = jnp.concatenate([blocks[j ^ k] for j in range(members)], axis=0)
            total = total + ordered.astype(f32)
        return total

    def dp_scatter(value):
        return lax.psum_scatter(value, "dp", scatter_dimension=0, tiled=True)

    def dp_gather(value):
        return lax.all_gather(value, "dp", axis=0, tiled=True)

    def to_columns(*rows):
        came = lax.all_to_all(pack_columns(groups, *rows), "dp", 0, 0, tiled=True)
        return came.reshape(-1, came.shape[2])

    def hold(value, *others):
        return lax.optimization_barrier((value,) + others)[0]

    def gain(index):
        return gains[index : index + 1]

    hidden1, rows1 = norm_forward(tokens.astype(f32), gain(0), [])
    normed1 = join(rows1)
    channels = mix_in.shape[2]
    bias, skip = dt_bias.reshape(1, channels), skip_gain.reshape(1, channels)
    alog = a_log.T
    xz = jnp.einsum("td,dgc->gtc", normed1, mix_in, preferred_element_type=f32)
    u, proj_part = conv_forward(me, members, xz, conv_weight, x_proj)
    proj = all_sum_rows(proj_part)
    gated_low, ys, states, *mixed = scan_forward(
        me, members, proj, dt_proj, bias, alog, skip, u, xz, mix_out
    )
    all_gated = dp_gather(gated_low)
    hidden2, rows2 = norm_forward(hidden1, gain(1), split_list(mixed))
    normed2 = join(rows2)
    gate_up = jnp.einsum("td,dgc->gtc", normed2, ffn_in, preferred_element_type=f32)
    ffn_gate = sigmoid(gate_up[0])
    acted_low = (gate_up[0] * ffn_gate * gate_up[1]).astype(bf16)
    all_acted = dp_gather(acted_low)
    hidden3, rows3 = norm_forward(
        hidden2, gain(2), split_list(blocks_of(matmul(acted_low, ffn_out)))
    )
    keyval = attn_keyval.reshape(D, -1)
    rows3 = join_list(rows3)
    rows3[0] = hold(rows3[0], all_gated)
    normed3, query_low, keyval_low, attended_low, *attended = attention_forward(
        me, members, rows3, attn_query, keyval, attn_out
    )
    all_attended = dp_gather(attended_low)
    hidden4, rows4 = norm_forward(hidden3, gain(3), split_list(attended))
    normed4 = join_list(rows4)

    at = jnp.bitwise_xor(jnp.arange(members, dtype=jnp.int32), member)
    picks = routes.reshape(members, share, 2)[at].reshape(LEN, 2)
    own_picks = picks[:share]
    router_rows = router.T
    moved, expert_low, slot_weights, *dn_part = experts(
        members, picks.T, router_rows, normed4, join_list(cotangent), expert_in, expert_out
    )
    dn_part[0] = hold(dn_part[0], all_acted, all_attended)
    all_moved = dp_gather(moved)
    grad, low4, gain4, grad_router = router_backward(
        cotangent, hidden4, gain(3), rows4, own_picks, router_rows, split_list(dn_part)
    )
    grad_low4 = join_list(low4)

    width = D // groups
    units = expert_out.shape[1]

    dqkv, *dnormed = attention_backward(
        me, members, grad_low4, query_low, keyval_low, attn_query, keyval, attn_out
    )
    dn_blocks = split_list(dnormed)
    attn_in_part = transposed_times(normed3, dqkv).astype(bf16)
    attn_in_sum = dp_scatter(attn_in_part)
    grad, low3, gain3 = norm_backward(
        hold(grad, attn_in_part), hidden3, gain(2), dn_blocks
    )
    grad_low3 = join(low3)

    dact = times_transposed(grad_low3, ffn_out)
    dgate_up = jnp.concatenate(
        [
            dact * ffn_gate * (1.0 + gate_up[0] * (1.0 - ffn_gate)) * gate_up[1],
            dact * gate_up[0] * ffn_gate,
        ],
        axis=1,
    ).astype(bf16)
    hidden_units = ffn_in.shape[2]
    dnormed = jnp.einsum(
        "tgc,dgc->td",
        dgate_up.reshape(LEN, 2, hidden_units),
        ffn_in,
        preferred_element_type=f32,
    )
    dn_blocks = blocks_of(dnormed)
    ffn_in_part = transposed_times(normed2, hold(dgate_up, dn_blocks[0])).astype(bf16)
    ffn_in_sum = dp_scatter(ffn_in_part)
    columns = to_columns(
        hold(rows4, dn_blocks[0]), cotangent, low4, low3, own_picks.astype(f32)
    )
    grad, low2, gain2 = norm_backward(
        hold(grad, ffn_in_part, all_moved),
        hidden2,
        gain(1),
        split_list(dn_blocks),
    )
    grad_low2 = join_list(low2)
    grad_low2[0] = hold(grad_low2[0], columns)

    du, dzs, small, dalog, ddt, dcols_part = scan_backward(
        me, members, proj, dt_proj, bias, alog, skip, u, xz, mix_out, grad_low2, ys, states
    )
    dcols = all_sum_rows(dcols_part.astype(bf16))
    dcols = hold(dcols, attn_in_sum)
    dxs, dxproj, dconv = conv_backward(
        me, members, dcols, proj, u, xz, du, conv_weight, x_proj
    )
    dmixed = jnp.stack([dxs, dzs])
    dnormed = jnp.einsum("gtc,dgc->td", dmixed, mix_in, preferred_element_type=f32)
    dn_blocks = blocks_of(dnormed)
    mix_part = mix_grads(
        groups, normed1, hold(dxs, dn_blocks[0]), dzs, dxproj, ddt, dalog, small, dconv
    )
    mix_sum = dp_scatter(mix_part.reshape(-1, channels)).astype(f32)
    dn_blocks = split_list(dn_blocks)
    dn_blocks[0] = hold(dn_blocks[0], mix_part)
    grad, _, gain1 = norm_backward(grad, hidden1, gain(0), dn_blocks)

    columns = join_list(hold(columns, grad))
    extra = jnp.concatenate([gain1, gain2, gain3, gain4, grad_router], axis=0).astype(bf16)
    extra = jnp.pad(extra, ((0, -extra.shape[0] % 16), (0, 0)))
    last = to_columns(jnp.concatenate([low2, extra], axis=0))
    made = experts_out(members, hold(expert_low, grad), slot_weights, expert_out)
    made = hold(made[0], ffn_in_sum, *columns), *made[1:]
    sorted_rows = sorted_columns(groups, [hold(columns[0], made[0])] + columns[1:])
    part = expert_grads(0, EXPERTS // 2, all_moved, *sorted_rows)
    made = split_list([hold(made[0], part[0])] + list(made[1:]))
    hidden5 = hidden4
    for block in made:
        hidden5 = hidden5 + block.astype(f32)
    last = join_list(hold(last, part[0]))
    columns[0] = hold(columns[0], part[0])
    attn_out_sum, ffn_out_sum = out_grads(groups, 2, columns, all_attended, all_acted)
    last[0] = hold(last[0], ffn_out_sum)
    mix_out_sum, model_sum = last_grads(groups, last, all_gated)
    expert_in_grad, expert_out_grad = expert_grads(
        EXPERTS // 2,
        EXPERTS // 2,
        hold(all_moved, mix_out_sum, hidden5),
        *sorted_rows,
        earlier=part,
    )

    def padded(count):
        return count + -count % 16

    slice_of = channels // groups
    xproj_rows, dt_rows = 128 // groups, DT_RANK // groups
    dt_at = 2 * width + padded(xproj_rows)
    flat = mix_sum[dt_at + padded(dt_rows) :, :slice_of]
    heads_cols = attn_query.shape[1]
    attn_in = attn_in_sum.astype(f32)
    return (
        hidden5.astype(bf16),
        grad,
        model_sum[:4],
        jnp.stack([mix_sum[:width], mix_sum[width : 2 * width]], axis=1),
        flat[2 * STATE : 2 * STATE + CONV],
        mix_sum[2 * width : 2 * width + xproj_rows].T,
        mix_sum[dt_at : dt_at + dt_rows],
        flat[STATE],
        flat[:STATE].T,
        flat[STATE + 1],
        mix_out_sum.T,
        ffn_in_sum.astype(f32).reshape(width, 2, hidden_units),
        ffn_out_sum.T,
        attn_in[:, :heads_cols],
        attn_in[:, heads_cols:].reshape(-1, 2, attn_keyval.shape[2]),
        attn_out_sum.T,
        model_sum[4 : 4 + EXPERTS].T,
        expert_in_grad,
        expert_out_grad.transpose(0, 2, 1),
    )


def solution(mesh):
    return jax.shard_map(
        shards,
        mesh=mesh,
        in_specs=(
            P(("dp", "tensor"), None),
            P(("dp", "tensor"), None),
            P(),
            P(None, None, "tensor"),
            P(None, "tensor"),
            P("tensor", None),
            P(None, "tensor"),
            P("tensor"),
            P("tensor", None),
            P("tensor"),
            P("tensor", None),
            P(None, None, "tensor"),
            P("tensor", None),
            P(None, "tensor"),
            P(None, None, "tensor"),
            P("tensor", None),
            P(),
            P(None, None, None, "tensor"),
            P(None, "tensor", None),
            P("dp", None),
        ),
        out_specs=(
            P(("dp", "tensor"), None),
            P(("dp", "tensor"), None),
            P(None, "dp"),
            P("dp", None, "tensor"),
            P(None, ("tensor", "dp")),
            P("tensor", "dp"),
            P("dp", "tensor"),
            P(("tensor", "dp")),
            P(("tensor", "dp"), None),
            P(("tensor", "dp")),
            P("tensor", "dp"),
            P("dp", None, "tensor"),
            P("tensor", "dp"),
            P("dp", "tensor"),
            P("dp", None, "tensor"),
            P("tensor", "dp"),
            P("dp", None),
            P(None, "dp", None, "tensor"),
            P(None, "tensor", "dp"),
        ),
        check_vma=False,
    )
```

```python
import functools
import math

import jax
import jax.numpy as jnp
from jax import lax
from jax.experimental import pallas as pl
from jax.experimental.pallas import tpu as pltpu
from jax.sharding import PartitionSpec as P

D = 1536
STATE = 16
CONV = 4
DT_RANK = 96
HEADS = 24
KV_HEADS = 8
HEAD_DIM = 64
EXPERTS = 16
LEN = 256
CAP = 48

epsilon = 1e-06
floor_square = 0.1
masked_score = -1e30
LOG2E = 1.4426950408889634
PAD = 8
CHUNK = 16
GROUP = 8
VMEM_LIMIT = 56 * 1024 * 1024

f32 = jnp.float32
bf16 = jnp.bfloat16


def matmul(left, right):
    return jnp.dot(left, right, preferred_element_type=f32)


def times_transposed(left, right):
    return lax.dot_general(left, right, (((1,), (1,)), ((), ())), preferred_element_type=f32)


def transposed_times(left, right):
    return lax.dot_general(left, right, (((0,), (0,)), ((), ())), preferred_element_type=f32)


def sigmoid(v):
    return 1.0 / (1.0 + jnp.exp(-v))


def dot_exact(left, right):
    return jnp.dot(left, right, precision=lax.Precision.HIGHEST, preferred_element_type=f32)


def column_norm_parts(projected):
    lane = lax.broadcasted_iota(jnp.int32, projected.shape, 1)
    square = projected * projected
    in_step = lane < DT_RANK
    in_b = jnp.logical_and(lane >= DT_RANK, lane < DT_RANK + STATE)
    in_c = lane >= DT_RANK + STATE
    mean_step = jnp.sum(jnp.where(in_step, square, 0.0), axis=1, keepdims=True) / DT_RANK
    mean_b = jnp.sum(jnp.where(in_b, square, 0.0), axis=1, keepdims=True) / STATE
    mean_c = jnp.sum(jnp.where(in_c, square, 0.0), axis=1, keepdims=True) / STATE
    r_step = lax.rsqrt(mean_step + epsilon)
    r_b = lax.rsqrt(jnp.maximum(mean_b, floor_square))
    r_c = lax.rsqrt(jnp.maximum(mean_c, floor_square))
    scale = jnp.where(in_step, r_step, jnp.where(in_b, r_b, r_c))
    return scale, in_step, in_b, in_c, mean_b, mean_c


def row_spread(cols_ref, first, out_ref):
    pick = (
        lax.broadcasted_iota(jnp.int32, (128, CHUNK * STATE), 0) - first
        == lax.broadcasted_iota(jnp.int32, (128, CHUNK * STATE), 1) % STATE
    ).astype(f32)
    out_ref[...] = (dot_exact(cols_ref[...], pick) * chunk_mask(LEN)).astype(bf16)


def chunk_mask(rows):
    return (
        lax.broadcasted_iota(jnp.int32, (rows, CHUNK * STATE), 0) % CHUNK
        == lax.broadcasted_iota(jnp.int32, (rows, CHUNK * STATE), 1) // STATE
    ).astype(f32)


def conv_total(pad_ref, weight_ref, length):
    total = weight_ref[0:1, :] * pad_ref[pl.ds(PAD - CONV + 1, length), :]
    for tap in range(1, CONV):
        total = total + weight_ref[tap : tap + 1, :] * pad_ref[pl.ds(PAD - CONV + 1 + tap, length), :]
    return total


def conv_forward_kernel(blocks, me_ref, xz_ref, weight_ref, xproj_ref, u_ref, proj_ref, pad_ref):
    me = me_ref[0]
    size = LEN // blocks
    pad_ref[0:PAD, :] = jnp.zeros((PAD, pad_ref.shape[1]), f32)
    for m in range(blocks):
        at = pl.multiple_of(jnp.bitwise_xor(me, m) * size, size)
        pad_ref[PAD + m * size : PAD + (m + 1) * size, :] = xz_ref[0, pl.ds(at, size), :]
    total = conv_total(pad_ref, weight_ref, LEN)
    u = total * sigmoid(total)
    for m in range(blocks):
        at = pl.multiple_of(jnp.bitwise_xor(me, m) * size, size)
        u_ref[pl.ds(at, size), :] = u[m * size : (m + 1) * size, :]
    proj_ref[...] = matmul(u_ref[...].astype(bf16), xproj_ref[...])


def scan_setup(proj_ref, cols_ref, b_ref, c_ref):
    projected = proj_ref[...]
    scale = column_norm_parts(projected)[0]
    cols_ref[...] = projected * scale
    row_spread(cols_ref, DT_RANK, b_ref)
    row_spread(cols_ref, DT_RANK + STATE, c_ref)


def step_sizes(cols_ref, dt_proj_ref, bias_ref):
    low = cols_ref[:, :DT_RANK].astype(bf16)
    pre = matmul(low, dt_proj_ref[...]) + bias_ref[...]
    return low, pre, jnp.maximum(pre, 0.0) + jnp.log1p(jnp.exp(-jnp.abs(pre)))


def chunk_place(index, me, size):
    block = index // (size // CHUNK)
    inner = index % (size // CHUNK)
    return pl.multiple_of(jnp.bitwise_xor(block, me) * size + inner * CHUNK, CHUNK)


def chunk_group(index):
    out = []
    for q in range(GROUP):
        base = (index * GROUP + q) * CHUNK
        out.append(
            (
                pl.ds(pl.multiple_of(base, CHUNK), CHUNK),
                pl.ds(pl.multiple_of(base * STATE, CHUNK * STATE), CHUNK * STATE),
            )
        )
    return out


def push_chunks(left_ref, right_ref, out_ref):
    def body(index, carry):
        for rows, many in chunk_group(index):
            out_ref[many, :] = transposed_times(left_ref[rows, :], right_ref[rows, :])
        return carry

    lax.fori_loop(0, LEN // CHUNK // GROUP, body, 0)


def scan_forward_kernel(
    blocks,
    me_ref,
    proj_ref,
    dt_proj_ref,
    bias_ref,
    alog_ref,
    skip_ref,
    u_ref,
    xz_ref,
    out_w_ref,
    gated_ref,
    ys_ref,
    states_ref,
    *rest,
):
    out_refs = rest[:blocks]
    cols_ref, b_ref, c_ref, delta_ref, drive_ref, push_ref, total_ref = rest[blocks:]
    me = me_ref[0]
    size = LEN // blocks
    lanes = u_ref.shape[1]
    step = pl.program_id(0)

    @pl.when(step == 0)
    def _():
        scan_setup(proj_ref, cols_ref, b_ref, c_ref)

    _, _, delta = step_sizes(cols_ref, dt_proj_ref, bias_ref)
    delta_ref[...] = delta
    drive_ref[...] = (delta * u_ref[...]).astype(bf16)
    rate = -jnp.exp(alog_ref[...]) * LOG2E
    push_chunks(b_ref, drive_ref, push_ref)

    def chunk(index, state):
        base = chunk_place(index, me, size)
        steps = delta_ref[pl.ds(base, CHUNK), :]
        for j in range(CHUNK):
            at = pl.ds(pl.multiple_of((base + j) * STATE, STATE), STATE)
            state = jnp.exp2(steps[j : j + 1, :] * rate) * state + push_ref[at, :]
            states_ref[at, :] = state.astype(bf16)
        return state

    lax.fori_loop(0, LEN // CHUNK, chunk, jnp.zeros((STATE, lanes), f32))

    def output(index, carry):
        for rows, many in chunk_group(index):
            ys_ref[rows, :] = matmul(c_ref[rows, :], states_ref[many, :])
        return carry

    lax.fori_loop(0, LEN // CHUNK // GROUP, output, 0)
    ys = ys_ref[...] + skip_ref[...] * u_ref[...]
    ys_ref[...] = ys
    zs = xz_ref[0]
    gated = (ys * (zs * sigmoid(zs))).astype(bf16)
    gated_ref[...] = gated
    part = matmul(gated, out_w_ref[...])

    @pl.when(step == 0)
    def _():
        total_ref[...] = part

    @pl.when(step > 0)
    def _():
        total_ref[...] += part

    @pl.when(step == pl.num_programs(0) - 1)
    def _():
        store_blocks(out_refs, total_ref[...])


def scan_backward_kernel(
    blocks,
    me_ref,
    proj_ref,
    dt_proj_ref,
    bias_ref,
    alog_ref,
    skip_ref,
    u_ref,
    xz_ref,
    out_w_ref,
    ys_ref,
    states_ref,
    *rest,
):
    grad_refs = rest[:blocks]
    (
        du_ref,
        dzs_ref,
        small_ref,
        dalog_ref,
        ddt_ref,
        dcols_ref,
        grad_ref,
        cols_ref,
        b_ref,
        c_ref,
        pb_ref,
        pc_ref,
        delta_ref,
        drive_ref,
        dys_ref,
        ddrive_ref,
        drate_ref,
        dlow_ref,
        push_ref,
        grads_ref,
        rates_ref,
    ) = rest[blocks:]
    me = me_ref[0]
    size = LEN // blocks
    lanes = u_ref.shape[1]
    step = pl.program_id(0)

    @pl.when(step == 0)
    def _():
        scan_setup(proj_ref, cols_ref, b_ref, c_ref)
        join_blocks(grad_refs, grad_ref)
        pb_ref[...] = jnp.zeros(pb_ref.shape, f32)
        pc_ref[...] = jnp.zeros(pc_ref.shape, f32)

    low, pre, delta = step_sizes(cols_ref, dt_proj_ref, bias_ref)
    u = u_ref[...]
    delta_ref[...] = delta
    drive_ref[...] = (delta * u).astype(bf16)
    dgated = times_transposed(grad_ref[...], out_w_ref[...])
    zs = xz_ref[0]
    gate = sigmoid(zs)
    dys = dgated * (zs * gate)
    dys_ref[...] = dys.astype(bf16)
    dzs_ref[...] = (dgated * ys_ref[...] * (gate * (1.0 + zs * (1.0 - gate)))).astype(bf16)
    a_matrix = -jnp.exp(alog_ref[...])
    rate = a_matrix * LOG2E
    chunks = LEN // CHUNK
    mask = chunk_mask(CHUNK)
    push_chunks(c_ref, dys_ref, push_ref)

    def chunk(step_index, carry):
        adjoint, da = carry
        index = chunks - 1 - step_index
        base = chunk_place(index, me, size)
        before = chunk_place(jnp.maximum(index - 1, 0), me, size)
        first = (index > 0).astype(f32)
        steps = delta_ref[pl.ds(base, CHUNK), :]
        for j in range(CHUNK - 1, -1, -1):
            at = pl.ds(pl.multiple_of((base + j) * STATE, STATE), STATE)
            if j > 0:
                last = (base + j - 1) * STATE
                earlier = states_ref[pl.ds(pl.multiple_of(last, STATE), STATE), :].astype(f32)
            else:
                last = (before + CHUNK - 1) * STATE
                earlier = states_ref[pl.ds(pl.multiple_of(last, STATE), STATE), :].astype(f32) * first
            grad = adjoint + push_ref[at, :]
            grads_ref[at, :] = grad.astype(bf16)
            adjoint = grad * jnp.exp2(steps[j : j + 1, :] * rate)
            through = adjoint * earlier
            rates_ref[at, :] = (through * a_matrix).astype(bf16)
            da = da + through * steps[j : j + 1, :]
        return adjoint, da

    zero = jnp.zeros((STATE, lanes), f32)
    _, da = lax.fori_loop(0, chunks, chunk, (zero, zero))
    mask_low = mask.astype(bf16)

    def output(index, carry):
        for rows, many in chunk_group(index):
            grads = grads_ref[many, :]
            ddrive_ref[rows, :] = matmul(b_ref[rows, :], grads)
            drate_ref[rows, :] = matmul(mask_low, rates_ref[many, :])
            pb_ref[rows, :] += times_transposed(drive_ref[rows, :], grads) * mask
            pc_ref[rows, :] += times_transposed(dys_ref[rows, :], states_ref[many, :]) * mask
        return carry

    lax.fori_loop(0, chunks // GROUP, output, 0)
    dalog_ref[...] = da * a_matrix
    ddrive = ddrive_ref[...]
    du_ref[...] = ddrive * delta + skip_ref[...] * dys
    dpre = (ddrive * u + drate_ref[...]) * sigmoid(pre)
    dpre_low = dpre.astype(bf16)
    small_ref[...] = jnp.concatenate(
        [
            jnp.sum(dpre, axis=0, keepdims=True),
            jnp.sum(dys * u, axis=0, keepdims=True),
            jnp.zeros((6, lanes), f32),
        ],
        axis=0,
    )
    ddt_ref[...] = transposed_times(low, dpre_low)
    part = times_transposed(dpre_low, dt_proj_ref[...])

    @pl.when(step == 0)
    def _():
        dlow_ref[...] = part

    @pl.when(step > 0)
    def _():
        dlow_ref[...] += part

    @pl.when(step == pl.num_programs(0) - 1)
    def _():
        collect = (
            lax.broadcasted_iota(jnp.int32, (CHUNK * STATE, STATE), 0) % STATE
            == lax.broadcasted_iota(jnp.int32, (CHUNK * STATE, STATE), 1)
        ).astype(f32)
        dcols_ref[...] = jnp.concatenate(
            [dlow_ref[...], dot_exact(pb_ref[...], collect), dot_exact(pc_ref[...], collect)], axis=1
        )


def conv_backward_kernel(
    blocks,
    me_ref,
    dcols_ref,
    proj_ref,
    u_ref,
    xz_ref,
    du_ref,
    weight_ref,
    xproj_ref,
    dxs_ref,
    dxproj_ref,
    dweight_ref,
    pad_ref,
    grad_ref,
):
    me = me_ref[0]
    size = LEN // blocks
    lanes = u_ref.shape[1]
    projected = proj_ref[...]
    scale, in_step, in_b, in_c, mean_b, mean_c = column_norm_parts(projected)
    normed = projected * scale
    dcols = dcols_ref[...]
    product = dcols * normed
    dot_step = jnp.sum(jnp.where(in_step, product, 0.0), axis=1, keepdims=True) / DT_RANK
    dot_b = jnp.sum(jnp.where(in_b, product, 0.0), axis=1, keepdims=True) / STATE
    dot_c = jnp.sum(jnp.where(in_c, product, 0.0), axis=1, keepdims=True) / STATE
    dot_b = jnp.where(mean_b > floor_square, dot_b, 0.0)
    dot_c = jnp.where(mean_c > floor_square, dot_c, 0.0)
    mean = jnp.where(in_step, dot_step, jnp.where(in_b, dot_b, dot_c))
    dproj = (scale * (dcols - normed * mean)).astype(bf16)
    dxproj_ref[...] = transposed_times(dproj, u_ref[...].astype(bf16))
    du = du_ref[...] + times_transposed(dproj, xproj_ref[...])
    pad_ref[0:PAD, :] = jnp.zeros((PAD, lanes), f32)
    grad_ref[LEN : LEN + PAD, :] = jnp.zeros((PAD, lanes), f32)
    for m in range(blocks):
        at = pl.multiple_of(jnp.bitwise_xor(me, m) * size, size)
        pad_ref[PAD + m * size : PAD + (m + 1) * size, :] = xz_ref[0, pl.ds(at, size), :]
    dxs_ref[...] = du.astype(bf16)
    du_ref_rows = []
    grad_ref[0:LEN, :] = du
    total = conv_total(pad_ref, weight_ref, LEN)
    gate = sigmoid(total)
    slope = gate * (1.0 + total * (1.0 - gate))
    for m in range(blocks):
        at = pl.multiple_of(jnp.bitwise_xor(me, m) * size, size)
        du_ref_rows.append(grad_ref[pl.ds(at, size), :])
    grad_ref[0:LEN, :] = jnp.concatenate(du_ref_rows, axis=0) * slope
    dcv = grad_ref[0:LEN, :]
    dweight_ref[...] = jnp.concatenate(
        [
            jnp.sum(dcv * pad_ref[pl.ds(PAD - CONV + 1 + tap, LEN), :], axis=0, keepdims=True)
            for tap in range(CONV)
        ],
        axis=0,
    )
    dxs = weight_ref[CONV - 1 : CONV, :] * dcv
    for tap in range(CONV - 1):
        dxs = dxs + weight_ref[tap : tap + 1, :] * grad_ref[pl.ds(CONV - 1 - tap, LEN), :]
    dxs = dxs.astype(bf16)
    for m in range(blocks):
        at = pl.multiple_of(jnp.bitwise_xor(me, m) * size, size)
        dxs_ref[pl.ds(at, size), :] = dxs[m * size : (m + 1) * size, :]


def store_blocks(refs, value):
    size = value.shape[0] // len(refs)
    for k, ref in enumerate(refs):
        ref[...] = value[k * size : (k + 1) * size].astype(ref.dtype)


def join_blocks(refs, out_ref):
    size = out_ref.shape[0] // len(refs)
    for k, ref in enumerate(refs):
        out_ref[k * size : (k + 1) * size, :] = ref[...]


SMEM = pl.BlockSpec(memory_space=pltpu.SMEM)


def whole(shape):
    return pl.BlockSpec(shape, lambda *_: (0,) * len(shape))


def params():
    return pltpu.CompilerParams(vmem_limit_bytes=VMEM_LIMIT)


def takes(microseconds):
    return pl.CostEstimate(
        flops=int(microseconds * 1.15e9), bytes_accessed=1 << 20, transcendentals=0
    )


def shape_of(shape, dtype=f32):
    return jax.ShapeDtypeStruct(shape, dtype)


def conv_forward(me, blocks, xz, weight, x_proj):
    channels = xz.shape[2]
    return pl.pallas_call(
        functools.partial(conv_forward_kernel, blocks),
        grid=(1,),
        in_specs=[
            SMEM,
            pl.BlockSpec((1, LEN, channels), lambda i: (0, 0, 0)),
            whole(weight.shape),
            whole(x_proj.shape),
        ],
        out_specs=(whole((LEN, channels)), whole((LEN, 128))),
        out_shape=(shape_of((LEN, channels)), shape_of((LEN, 128))),
        scratch_shapes=[pltpu.VMEM((LEN + PAD, channels), f32)],
        compiler_params=params(),
        cost_estimate=takes(3),
        name="conv_forward",
    )(me, xz, weight, x_proj)


def lane_block(channels):
    return channels


def scan_forward(me, blocks, proj, dt_proj, bias, alog, skip, u, xz, out_w):
    channels = u.shape[1]
    lanes = lane_block(channels)
    col = lambda i: (0, i)
    return pl.pallas_call(
        functools.partial(scan_forward_kernel, blocks),
        grid=(channels // lanes,),
        in_specs=[
            SMEM,
            whole((LEN, 128)),
            pl.BlockSpec((DT_RANK, lanes), col),
            pl.BlockSpec((1, lanes), col),
            pl.BlockSpec((STATE, lanes), col),
            pl.BlockSpec((1, lanes), col),
            pl.BlockSpec((LEN, lanes), col),
            pl.BlockSpec((1, LEN, lanes), lambda i: (1, 0, i)),
            pl.BlockSpec((lanes, D), lambda i: (i, 0)),
        ],
        out_specs=(
            pl.BlockSpec((LEN, lanes), col),
            pl.BlockSpec((LEN, lanes), col),
            pl.BlockSpec((LEN * STATE, lanes), col),
        )
        + (whole((LEN // blocks, D)),) * blocks,
        out_shape=(
            shape_of((LEN, channels), bf16),
            shape_of((LEN, channels)),
            shape_of((LEN * STATE, channels), bf16),
        )
        + (shape_of((LEN // blocks, D), bf16),) * blocks,
        scratch_shapes=[
            pltpu.VMEM((LEN, 128), f32),
            pltpu.VMEM((LEN, CHUNK * STATE), bf16),
            pltpu.VMEM((LEN, CHUNK * STATE), bf16),
            pltpu.VMEM((LEN, lanes), f32),
            pltpu.VMEM((LEN, lanes), bf16),
            pltpu.VMEM((LEN * STATE, lanes), f32),
            pltpu.VMEM((LEN, D), f32),
        ],
        compiler_params=params(),
        cost_estimate=takes(13),
        name="scan_forward",
    )(me, proj, dt_proj, bias, alog, skip, u, xz, out_w)


def scan_backward(me, blocks, proj, dt_proj, bias, alog, skip, u, xz, out_w, grad, ys, states):
    channels = u.shape[1]
    lanes = lane_block(channels)
    col = lambda i: (0, i)
    rows = pl.BlockSpec((LEN, lanes), col)
    return pl.pallas_call(
        functools.partial(scan_backward_kernel, blocks),
        grid=(channels // lanes,),
        in_specs=[
            SMEM,
            whole((LEN, 128)),
            pl.BlockSpec((DT_RANK, lanes), col),
            pl.BlockSpec((1, lanes), col),
            pl.BlockSpec((STATE, lanes), col),
            pl.BlockSpec((1, lanes), col),
            rows,
            pl.BlockSpec((1, LEN, lanes), lambda i: (1, 0, i)),
            pl.BlockSpec((lanes, D), lambda i: (i, 0)),
            rows,
            pl.BlockSpec((LEN * STATE, lanes), col),
        ]
        + [whole((LEN // blocks, D))] * blocks,
        out_specs=(
            rows,
            rows,
            pl.BlockSpec((8, lanes), col),
            pl.BlockSpec((STATE, lanes), col),
            pl.BlockSpec((DT_RANK, lanes), col),
            whole((LEN, 128)),
        ),
        out_shape=(
            shape_of((LEN, channels)),
            shape_of((LEN, channels), bf16),
            shape_of((8, channels)),
            shape_of((STATE, channels)),
            shape_of((DT_RANK, channels)),
            shape_of((LEN, 128)),
        ),
        scratch_shapes=[
            pltpu.VMEM((LEN, D), bf16),
            pltpu.VMEM((LEN, 128), f32),
            pltpu.VMEM((LEN, CHUNK * STATE), bf16),
            pltpu.VMEM((LEN, CHUNK * STATE), bf16),
            pltpu.VMEM((LEN, CHUNK * STATE), f32),
            pltpu.VMEM((LEN, CHUNK * STATE), f32),
            pltpu.VMEM((LEN, lanes), f32),
            pltpu.VMEM((LEN, lanes), bf16),
            pltpu.VMEM((LEN, lanes), bf16),
            pltpu.VMEM((LEN, lanes), f32),
            pltpu.VMEM((LEN, lanes), f32),
            pltpu.VMEM((LEN, DT_RANK), f32),
            pltpu.VMEM((LEN * STATE, lanes), f32),
            pltpu.VMEM((LEN * STATE, lanes), bf16),
            pltpu.VMEM((LEN * STATE, lanes), bf16),
        ],
        compiler_params=params(),
        cost_estimate=takes(21),
        name="scan_backward",
    )(me, proj, dt_proj, bias, alog, skip, u, xz, out_w, ys, states, *grad)


def conv_backward(me, blocks, dcols, proj, u, xz, du, weight, x_proj):
    channels = u.shape[1]
    return pl.pallas_call(
        functools.partial(conv_backward_kernel, blocks),
        grid=(1,),
        in_specs=[
            SMEM,
            whole((LEN, 128)),
            whole((LEN, 128)),
            whole((LEN, channels)),
            pl.BlockSpec((1, LEN, channels), lambda i: (0, 0, 0)),
            whole((LEN, channels)),
            whole(weight.shape),
            whole(x_proj.shape),
        ],
        out_specs=(whole((LEN, channels)), whole((128, channels)), whole((CONV, channels))),
        out_shape=(
            shape_of((LEN, channels), bf16),
            shape_of((128, channels)),
            shape_of((CONV, channels)),
        ),
        scratch_shapes=[
            pltpu.VMEM((LEN + PAD, channels), f32),
            pltpu.VMEM((LEN + PAD, channels), f32),
        ],
        compiler_params=params(),
        cost_estimate=takes(5),
        name="conv_backward",
    )(me, dcols, proj, u, xz, du, weight, x_proj)


def attention_probabilities(q, k, allowed):
    scores = times_transposed(q, k) * (1.0 / math.sqrt(HEAD_DIM))
    scores = jnp.where(allowed, scores, masked_score)
    peak = jnp.max(scores, axis=1, keepdims=True)
    exponent = jnp.exp(scores - peak)
    return exponent / jnp.sum(exponent, axis=1, keepdims=True)


def causal(me, blocks):
    size = LEN // blocks

    def position(axis):
        index = lax.broadcasted_iota(jnp.int32, (LEN, LEN), axis)
        return jnp.bitwise_xor(index // size, me) * size + index % size

    return position(1) <= position(0)


def attention_forward_kernel(
    blocks, me_ref, wq_ref, wkv_ref, wo_ref, *rest
):
    joined_ref, q_ref, kv_ref, o_ref = rest[blocks : blocks + 4]
    out_refs = rest[blocks + 4 :]
    join_blocks(rest[:blocks], joined_ref)
    normed = joined_ref[...]
    q_ref[...] = matmul(normed, wq_ref[...]).astype(bf16)
    kv_ref[...] = matmul(normed, wkv_ref[...]).astype(bf16)
    kv_heads = wkv_ref.shape[1] // (2 * HEAD_DIM)
    group = HEADS // KV_HEADS
    allowed = causal(me_ref[0], blocks)
    outs = []
    for head in range(kv_heads * group):
        kv = head // group
        q = q_ref[:, head * HEAD_DIM : (head + 1) * HEAD_DIM]
        k = kv_ref[:, kv * HEAD_DIM : (kv + 1) * HEAD_DIM]
        v = kv_ref[:, (kv_heads + kv) * HEAD_DIM : (kv_heads + kv + 1) * HEAD_DIM]
        soft = attention_probabilities(q, k, allowed)
        outs.append(matmul(soft.astype(bf16), v).astype(bf16))
    o_ref[...] = jnp.concatenate(outs, axis=1)
    store_blocks(out_refs, matmul(o_ref[...], wo_ref[...]))


def attention_backward_kernel(
    blocks,
    me_ref,
    q_ref,
    kv_ref,
    wq_ref,
    wkv_ref,
    wo_ref,
    *rest,
):
    dqkv_ref, grad_ref = rest[blocks], rest[-1]
    join_blocks(rest[:blocks], grad_ref)
    dout = times_transposed(grad_ref[...], wo_ref[...]).astype(bf16)
    kv_heads = wkv_ref.shape[1] // (2 * HEAD_DIM)
    group = HEADS // KV_HEADS
    allowed = causal(me_ref[0], blocks)
    scale = 1.0 / math.sqrt(HEAD_DIM)
    dqs, dks, dvs = [], [], []
    for kv in range(kv_heads):
        k = kv_ref[:, kv * HEAD_DIM : (kv + 1) * HEAD_DIM]
        v = kv_ref[:, (kv_heads + kv) * HEAD_DIM : (kv_heads + kv + 1) * HEAD_DIM]
        dk = jnp.zeros((LEN, HEAD_DIM), f32)
        dv = jnp.zeros((LEN, HEAD_DIM), f32)
        for head in range(kv * group, (kv + 1) * group):
            q = q_ref[:, head * HEAD_DIM : (head + 1) * HEAD_DIM]
            do = dout[:, head * HEAD_DIM : (head + 1) * HEAD_DIM]
            soft = attention_probabilities(q, k, allowed)
            dsoft = times_transposed(do, v)
            dscore = soft * (dsoft - jnp.sum(soft * dsoft, axis=1, keepdims=True))
            dscore = dscore.astype(bf16)
            dqs.append((matmul(dscore, k) * scale).astype(bf16))
            dk = dk + transposed_times(dscore, q) * scale
            dv = dv + transposed_times(soft.astype(bf16), do)
        dks.append(dk.astype(bf16))
        dvs.append(dv.astype(bf16))
    dq = jnp.concatenate(dqs, axis=1)
    dkv = jnp.concatenate(dks + dvs, axis=1)
    dqkv_ref[:, : dq.shape[1]] = dq
    dqkv_ref[:, dq.shape[1] :] = dkv
    dn = times_transposed(dq, wq_ref[...]) + times_transposed(dkv, wkv_ref[...])
    store_blocks(rest[blocks + 1 : -1], dn)


def attention_forward(me, blocks, normed, wq, wkv, wo):
    size = LEN // blocks
    heads = shape_of((LEN, wq.shape[1]), bf16)
    kept = (shape_of((LEN, D), bf16), heads, shape_of((LEN, wkv.shape[1]), bf16), heads)
    return pl.pallas_call(
        functools.partial(attention_forward_kernel, blocks),
        grid=(1,),
        in_specs=[SMEM, whole(wq.shape), whole(wkv.shape), whole(wo.shape)]
        + [whole((size, D))] * blocks,
        out_specs=tuple(whole(item.shape) for item in kept) + (whole((size, D)),) * blocks,
        out_shape=kept + (shape_of((size, D), bf16),) * blocks,
        compiler_params=params(),
        cost_estimate=takes(6),
        name="attention_forward",
    )(me, wq, wkv, wo, *normed)


def attention_backward(me, blocks, grad, q, kv, wq, wkv, wo):
    size = LEN // blocks
    cols = wq.shape[1] + wkv.shape[1]
    return pl.pallas_call(
        functools.partial(attention_backward_kernel, blocks),
        grid=(1,),
        in_specs=[
            SMEM,
            whole(q.shape),
            whole(kv.shape),
            whole(wq.shape),
            whole(wkv.shape),
            whole(wo.shape),
        ]
        + [whole((size, D))] * blocks,
        out_specs=(whole((LEN, cols)),) + (whole((size, D)),) * blocks,
        out_shape=(shape_of((LEN, cols), bf16),) + (shape_of((size, D), bf16),) * blocks,
        scratch_shapes=[pltpu.VMEM((LEN, D), bf16)],
        compiler_params=params(),
        cost_estimate=takes(8),
        name="attention_backward",
    )(me, q, kv, wq, wkv, wo, *grad)


def norm_forward_kernel(hidden_ref, gain_ref, *rest):
    part_refs, (out_ref, normed_ref) = rest[:-2], rest[-2:]
    hidden = hidden_ref[...]
    for ref in part_refs:
        hidden = hidden + ref[...].astype(f32)
    scale = lax.rsqrt(jnp.mean(hidden * hidden, axis=1, keepdims=True) + epsilon)
    out_ref[...] = hidden
    normed_ref[...] = (hidden * scale * gain_ref[...]).astype(bf16)


def norm_forward(hidden, gain, parts):
    shape = hidden.shape
    return pl.pallas_call(
        norm_forward_kernel,
        grid=(1,),
        in_specs=[whole(shape), whole((1, D))] + [whole(shape)] * len(parts),
        out_specs=(whole(shape), whole(shape)),
        out_shape=(shape_of(shape), shape_of(shape, bf16)),
        compiler_params=params(),
        cost_estimate=takes(2),
        name="norm_forward",
    )(hidden, gain, *parts)


def pull_norm(grad, hidden, gain):
    scale = lax.rsqrt(jnp.mean(hidden * hidden, axis=1, keepdims=True) + epsilon)
    unit = hidden * scale
    through = grad * gain
    back = scale * (through - unit * jnp.mean(through * unit, axis=1, keepdims=True))
    return back, jnp.sum(grad * unit, axis=0, keepdims=True)


def norm_backward_kernel(grad_ref, hidden_ref, gain_ref, *rest):
    part_refs, (out_ref, low_ref, dgain_ref) = rest[:-3], rest[-3:]
    dn = part_refs[0][...].astype(f32)
    for ref in part_refs[1:]:
        dn = dn + ref[...].astype(f32)
    back, dgain = pull_norm(dn, hidden_ref[...], gain_ref[...])
    grad = grad_ref[...] + back
    out_ref[...] = grad
    low_ref[...] = grad.astype(bf16)
    dgain_ref[...] = dgain


def norm_backward(grad, hidden, gain, parts):
    shape = hidden.shape
    return pl.pallas_call(
        norm_backward_kernel,
        grid=(1,),
        in_specs=[whole(shape), whole(shape), whole((1, D))] + [whole(shape)] * len(parts),
        out_specs=(whole(shape), whole(shape), whole((1, D))),
        out_shape=(shape_of(shape), shape_of(shape, bf16), shape_of((1, D))),
        compiler_params=params(),
        cost_estimate=takes(2.5),
        name="norm_backward",
    )(grad, hidden, gain, *parts)


def router_backward_kernel(grad_ref, hidden_ref, gain_ref, normed_ref, picks_ref, router_ref, *rest):
    part_refs, (out_ref, low_ref, dgain_ref, drouter_ref) = rest[:-4], rest[-4:]
    dn = part_refs[0][...].astype(f32)
    for ref in part_refs[1:]:
        dn = dn + ref[...].astype(f32)
    normed, router = normed_ref[...], router_ref[...]
    rows = normed.shape[0]
    ids = lax.broadcasted_iota(jnp.int32, (rows, EXPERTS), 1)
    logits = times_transposed(normed, router)
    hot = [(ids == picks_ref[:, k : k + 1]).astype(f32) for k in (0, 1)]
    chosen = [jnp.sum(hot[k] * logits, axis=1, keepdims=True) for k in (0, 1)]
    peak = jnp.maximum(chosen[0], chosen[1])
    weight = [jnp.exp(value - peak) for value in chosen]
    total = weight[0] + weight[1]
    weight = [value / total for value in weight]
    dw = [dn[:, D + k : D + k + 1] for k in (0, 1)]
    mean = weight[0] * dw[0] + weight[1] * dw[1]
    dlog = sum(hot[k] * (weight[k] * (dw[k] - mean)) for k in (0, 1)).astype(bf16)
    dn = dn[:, :D] + matmul(dlog, router)
    back, dgain = pull_norm(dn, hidden_ref[...], gain_ref[...])
    grad = grad_ref[...].astype(f32) + back
    out_ref[...] = grad
    low_ref[...] = grad.astype(bf16)
    dgain_ref[...] = dgain
    drouter_ref[...] = transposed_times(dlog, normed)


def router_backward(grad, hidden, gain, normed, picks, router, parts):
    shape = hidden.shape
    wide_rows = whole((shape[0], D + 128))
    return pl.pallas_call(
        router_backward_kernel,
        grid=(1,),
        in_specs=[
            whole(shape),
            whole(shape),
            whole((1, D)),
            whole(shape),
            whole((shape[0], 2)),
            whole((EXPERTS, D)),
        ]
        + [wide_rows] * len(parts),
        out_specs=(whole(shape), whole(shape), whole((1, D)), whole((EXPERTS, D))),
        out_shape=(
            shape_of(shape),
            shape_of(shape, bf16),
            shape_of((1, D)),
            shape_of((EXPERTS, D)),
        ),
        compiler_params=params(),
        cost_estimate=takes(3),
        name="router_backward",
    )(grad, hidden, gain, normed, picks, router, *parts)


def experts_kernel(blocks, routes_ref, router_ref, w_in_ref, w_out_ref, *rest):
    normed_refs, grad_refs = rest[:blocks], rest[blocks : 2 * blocks]
    moved_ref, act_ref, weighted_ref = rest[2 * blocks : 2 * blocks + 3]
    dn_refs = rest[2 * blocks + 3 : 3 * blocks + 3]
    (
        normed_ref,
        grad_ref,
        even_ref,
        odd_ref,
        grads_ref,
        place_ref,
        first_ref,
        second_ref,
        scale_ref,
        back_ref,
        kept_ref,
        dw_ref,
    ) = rest[3 * blocks + 3 :]
    expert = pl.program_id(0)
    slots = EXPERTS * CAP
    units = w_out_ref.shape[1]

    @pl.when(expert == 0)
    def _():
        join_blocks(normed_refs, normed_ref)
        join_blocks(grad_refs, grad_ref)
        routes = routes_ref[...]
        ids = lax.broadcasted_iota(jnp.int32, (EXPERTS, LEN), 0)
        hot = [(ids == routes[k : k + 1, :]).astype(f32) for k in (0, 1)]
        earlier = (
            lax.broadcasted_iota(jnp.int32, (LEN, LEN), 0)
            < lax.broadcasted_iota(jnp.int32, (LEN, LEN), 1)
        ).astype(bf16)
        rank0 = matmul(hot[0].astype(bf16), earlier)
        rank1 = matmul(hot[1].astype(bf16), earlier) + jnp.sum(hot[0], axis=1, keepdims=True)
        first = ids.astype(f32) * CAP
        position = [
            jnp.sum(hot[k] * (first + rank), axis=0, keepdims=True).astype(jnp.int32)
            for k, rank in ((0, rank0), (1, rank1))
        ]
        logits = times_transposed(router_ref[...], normed_ref[...])
        chosen = [jnp.sum(hot[k] * logits, axis=0, keepdims=True) for k in (0, 1)]
        peak = jnp.maximum(chosen[0], chosen[1])
        weight = [jnp.exp(value - peak) for value in chosen]
        total = weight[0] + weight[1]
        weight = [value / total for value in weight]
        slot = lax.broadcasted_iota(jnp.int32, (slots, LEN), 0)
        in0 = (slot == position[0]).astype(f32)
        in1 = (slot == position[1]).astype(f32)
        weighted = in0 * weight[0] + in1 * weight[1]
        place = (in0 + in1).astype(bf16)
        first_ref[...] = in0.astype(bf16)
        second_ref[...] = in1.astype(bf16)
        place_ref[...] = place
        weighted_ref[...] = weighted.astype(bf16)
        scale_ref[...] = jnp.broadcast_to(jnp.sum(weighted, axis=1, keepdims=True), (slots, 128))
        grads_ref[...] = matmul(place, grad_ref[...]).astype(bf16)
        spread = lax.broadcasted_iota(jnp.int32, (128, 256), 1) - 2 * lax.broadcasted_iota(
            jnp.int32, (128, 256), 0
        )
        for block in range(D // 128):
            rows = matmul(place, normed_ref[:, block * 128 : (block + 1) * 128]).astype(bf16)
            cols = slice(block * 256, (block + 1) * 256)
            even_ref[:, cols] = matmul(rows, (spread == 0).astype(bf16)).astype(bf16)
            odd_ref[:, cols] = matmul(rows, (spread == 1).astype(bf16)).astype(bf16)

    mine = pl.ds(pl.multiple_of(expert * CAP, CAP), CAP)
    w_in = w_in_ref[0].reshape(2 * D, units)
    w_out = w_out_ref[0]
    both = matmul(jnp.concatenate([even_ref[mine, :], odd_ref[mine, :]], axis=0), w_in)
    gate, up = both[:CAP], both[CAP:]
    sig = sigmoid(gate)
    silu = gate * sig
    act = silu * up
    act_low = act.astype(bf16)
    act_ref[0] = act_low
    scale = scale_ref[mine, 0:1]
    plain = times_transposed(grads_ref[mine, :], w_out)
    dw_ref[mine, :] = jnp.broadcast_to(
        jnp.sum(plain * act_low.astype(f32), axis=1, keepdims=True), (CAP, 128)
    ).astype(bf16)
    dact = plain * scale
    dgate = (dact * sig * (1.0 + gate * (1.0 - sig)) * up).astype(bf16)
    dup = (dact * silu).astype(bf16)
    back = times_transposed(jnp.concatenate([dgate, dup], axis=0), w_in)
    lane = lax.broadcasted_iota(jnp.int32, (CAP, 2 * D), 1)
    back_ref[mine, :] = jnp.where(lane % 2 == 0, back[:CAP], back[CAP:]).astype(bf16)
    kept_ref[mine, :] = jnp.concatenate([dgate, dup, (act * scale).astype(bf16)], axis=1)

    @pl.when(expert == EXPERTS - 1)
    def _():
        pairs = (
            lax.broadcasted_iota(jnp.int32, (256, 128), 0) // 2
            == lax.broadcasted_iota(jnp.int32, (256, 128), 1)
        ).astype(bf16)
        size = LEN // blocks
        for block in range(D // 128):
            cols = slice(block * 256, (block + 1) * 256)
            wide_rows = transposed_times(place_ref[...], back_ref[:, cols]).astype(bf16)
            dn = matmul(wide_rows, pairs).astype(bf16)
            for k, ref in enumerate(dn_refs):
                ref[:, block * 128 : (block + 1) * 128] = dn[k * size : (k + 1) * size]
        lanes = lax.broadcasted_iota(jnp.int32, (LEN, 128), 1)
        gates = [transposed_times(ref[...], dw_ref[...]) for ref in (first_ref, second_ref)]
        gates = jnp.where(lanes == 0, gates[0], jnp.where(lanes == 1, gates[1], 0.0)).astype(bf16)
        for k, ref in enumerate(dn_refs):
            ref[:, D:] = gates[k * size : (k + 1) * size]
        for k, ref in enumerate((first_ref, second_ref)):
            moved_ref[:, k * 3 * units : (k + 1) * 3 * units] = transposed_times(
                ref[...], kept_ref[...]
            ).astype(bf16)


def experts(blocks, routes, router, normed, grad, w_in, w_out):
    units = w_out.shape[1]
    slots = EXPERTS * CAP
    size = LEN // blocks
    return pl.pallas_call(
        functools.partial(experts_kernel, blocks),
        grid=(EXPERTS,),
        in_specs=[
            whole((2, LEN)),
            whole((EXPERTS, D)),
            pl.BlockSpec((1, D, 2, units), lambda e: (e, 0, 0, 0)),
            pl.BlockSpec((1, units, D), lambda e: (e, 0, 0)),
        ]
        + [whole((size, D))] * (2 * blocks),
        out_specs=(
            whole((LEN, 6 * units)),
            pl.BlockSpec((1, CAP, units), lambda e: (e, 0, 0)),
            whole((slots, LEN)),
        )
        + (whole((size, D + 128)),) * blocks,
        out_shape=(
            shape_of((LEN, 6 * units), bf16),
            shape_of((EXPERTS, CAP, units), bf16),
            shape_of((slots, LEN), bf16),
        )
        + (shape_of((size, D + 128), bf16),) * blocks,
        scratch_shapes=[
            pltpu.VMEM((LEN, D), bf16),
            pltpu.VMEM((LEN, D), bf16),
            pltpu.VMEM((slots, 2 * D), bf16),
            pltpu.VMEM((slots, 2 * D), bf16),
            pltpu.VMEM((slots, D), bf16),
            pltpu.VMEM((slots, LEN), bf16),
            pltpu.VMEM((slots, LEN), bf16),
            pltpu.VMEM((slots, LEN), bf16),
            pltpu.VMEM((slots, 128), f32),
            pltpu.VMEM((slots, 2 * D), bf16),
            pltpu.VMEM((slots, 3 * units), bf16),
            pltpu.VMEM((slots, 128), bf16),
        ],
        compiler_params=params(),
        cost_estimate=takes(37),
        name="experts",
    )(routes, router, w_in, w_out, *normed, *grad)


def experts_out_kernel(blocks, act_ref, weighted_ref, w_out_ref, *rest):
    made_refs, ye_ref = rest[-1 - blocks : -1], rest[-1]
    expert = pl.program_id(0)
    mine = pl.ds(pl.multiple_of(expert * CAP, CAP), CAP)
    ye_ref[mine, :] = matmul(act_ref[0], w_out_ref[0]).astype(bf16)

    @pl.when(expert == pl.num_programs(0) - 1)
    def _():
        made = transposed_times(weighted_ref[...], ye_ref[...])
        size = LEN // blocks
        if len(rest) > blocks + 1:
            made = made + jnp.concatenate([ref[...].astype(f32) for ref in rest[:blocks]], axis=0)
        for k, ref in enumerate(made_refs):
            ref[...] = made[k * size : (k + 1) * size].astype(bf16)


def experts_out(blocks, part, parts, act, weighted, w_out, earlier=()):
    units = w_out.shape[1]
    count = EXPERTS // parts
    slots = count * CAP
    rows = whole((LEN // blocks, D))
    return pl.pallas_call(
        functools.partial(experts_out_kernel, blocks),
        grid=(count,),
        in_specs=[
            pl.BlockSpec((1, CAP, units), lambda e: (e + part * count, 0, 0)),
            pl.BlockSpec((slots, LEN), lambda e: (part, 0)),
            pl.BlockSpec((1, units, D), lambda e: (e + part * count, 0, 0)),
        ]
        + [rows] * len(earlier),
        out_specs=(rows,) * blocks,
        out_shape=(shape_of((LEN // blocks, D), bf16),) * blocks,
        scratch_shapes=[pltpu.VMEM((slots, D), bf16)],
        compiler_params=params(),
        cost_estimate=takes(14 / parts),
        name="experts_out",
    )(act, weighted, w_out, *earlier)


def sort_rows(refs, groups, out_ref):
    share = LEN // len(refs)
    for group in range(groups):
        for k, ref in enumerate(refs):
            at = group * LEN + k * share
            out_ref[at : at + share, :] = ref[group * share : (group + 1) * share, :]


def sorted_columns_kernel(groups, *refs):
    column_refs, (left_ref, right_ref, picks_ref, rows_ref) = refs[:-4], refs[-4:]
    width = left_ref.shape[0]
    sort_rows(column_refs, groups, rows_ref)
    left_ref[...] = rows_ref[:, :width].astype(f32).T.astype(bf16)
    right_ref[...] = rows_ref[:, width : 2 * width].astype(f32).T.astype(bf16)
    picks_ref[...] = rows_ref[:, 4 * width : 4 * width + 2].astype(f32)


def sorted_columns(groups, columns):
    tokens, width = groups * LEN, D // groups
    shapes = ((width, tokens), (width, tokens))
    return pl.pallas_call(
        functools.partial(sorted_columns_kernel, groups),
        grid=(1,),
        in_specs=[whole(item.shape) for item in columns],
        out_specs=tuple(whole(shape) for shape in shapes) + (whole((tokens, 2)),),
        out_shape=tuple(shape_of(shape, bf16) for shape in shapes) + (shape_of((tokens, 2)),),
        scratch_shapes=[pltpu.VMEM((tokens, columns[0].shape[1]), bf16)],
        compiler_params=params(),
        cost_estimate=takes(4),
        name="sorted_columns",
    )(*columns)


def expert_grad_kernel(first, moved_ref, left_ref, right_ref, picks_ref, *rest):
    din_ref, dout_ref = rest[-2:]
    units = moved_ref.shape[1] // 6
    which = (pl.program_id(0) + first).astype(f32)
    at0 = (picks_ref[:, 0:1] == which).astype(bf16)
    at1 = (picks_ref[:, 1:2] == which).astype(bf16)
    moved = moved_ref[:, : 3 * units] * at0 + moved_ref[:, 3 * units :] * at1
    din = matmul(left_ref[...], moved[:, : 2 * units])
    din_ref[0, :, 0, :] = din[:, :units]
    din_ref[0, :, 1, :] = din[:, units:]
    dout_ref[0] = matmul(right_ref[...], moved[:, 2 * units :])


def expert_grads(first, count, moved, left, right, picks, earlier=()):
    width = left.shape[0]
    units = moved.shape[1] // 6
    inputs = (moved, left, right, picks)
    return pl.pallas_call(
        functools.partial(expert_grad_kernel, first),
        grid=(count,),
        in_specs=[whole(item.shape) for item in inputs]
        + [pl.BlockSpec(memory_space=pl.ANY)] * len(earlier),
        out_specs=(
            pl.BlockSpec((1, width, 2, units), lambda e: (e + first, 0, 0, 0)),
            pl.BlockSpec((1, width, units), lambda e: (e + first, 0, 0)),
        ),
        out_shape=(
            shape_of((EXPERTS, width, 2, units)),
            shape_of((EXPERTS, width, units)),
        ),
        input_output_aliases={4: 0, 5: 1} if earlier else {},
        compiler_params=params(),
        cost_estimate=takes(1.5 * count),
        name="expert_grads",
    )(*inputs, *earlier)


def pack_columns_kernel(groups, lanes, *refs):
    in_refs, out_ref = refs[:-1], refs[-1]
    width = D // groups
    values = [ref[...].astype(f32) for ref in in_refs]
    rows = values[0].shape[0]
    for group in range(groups):
        parts = [
            value[:, group * width : (group + 1) * width] if value.shape[1] == D else value
            for value in values
        ]
        spare = lanes - sum(part.shape[1] for part in parts)
        if spare:
            parts.append(jnp.zeros((rows, spare), f32))
        whole_row = jnp.concatenate(parts, axis=1) if len(parts) > 1 else parts[0]
        out_ref[group] = whole_row.astype(bf16)


def pack_columns(groups, *values):
    width, rows = D // groups, values[0].shape[0]
    lanes = sum(width if value.shape[1] == D else value.shape[1] for value in values)
    if len(values) > 1:
        lanes += -lanes % 128
    return pl.pallas_call(
        functools.partial(pack_columns_kernel, groups, lanes),
        grid=(1,),
        in_specs=[whole(value.shape) for value in values],
        out_specs=whole((groups, rows, lanes)),
        out_shape=shape_of((groups, rows, lanes), bf16),
        compiler_params=params(),
        cost_estimate=takes(3),
        name="pack_columns",
    )(*values)


def mix_grad_kernel(groups, normed_ref, first_ref, second_ref, *refs):
    extra_refs, out_ref = refs[:-1], refs[-1]
    width = D // groups
    grads = [
        transposed_times(normed_ref[...], ref[...]).astype(bf16) for ref in (first_ref, second_ref)
    ]
    channels = grads[0].shape[1]
    share = channels // groups
    extras = [ref[...] for ref in extra_refs]
    tall = [extra for extra in extras if extra.shape[0] > STATE]
    flat = [extra for extra in extras if extra.shape[0] <= STATE]
    for group in range(groups):
        at = 0
        for grad in grads:
            out_ref[group, at : at + width, :] = grad[group * width : (group + 1) * width]
            at += width
        rows = [
            extra[group * (extra.shape[0] // groups) : (group + 1) * (extra.shape[0] // groups)]
            for extra in tall
        ]
        line = jnp.concatenate(
            [
                extra[row : row + 1, group * share : (group + 1) * share]
                for extra in flat
                for row in range(extra.shape[0])
            ],
            axis=1,
        )
        spare = -line.shape[1] % channels
        line = jnp.concatenate([line, jnp.zeros((1, spare), f32)], axis=1)
        for first in range(0, line.shape[1], channels):
            rows.append(line[:, first : first + channels])
        spare = out_ref.shape[1] - at - sum(row.shape[0] for row in rows)
        if spare:
            rows.append(jnp.zeros((spare, channels), f32))
        out_ref[group, at:, :] = jnp.concatenate(rows, axis=0).astype(bf16)


def mix_grads(groups, normed, first, second, *extras):
    channels = first.shape[1]
    rows = sum(extra.shape[0] // groups for extra in extras if extra.shape[0] > STATE)
    lines = sum(extra.shape[0] for extra in extras if extra.shape[0] <= STATE)
    rows += -(-lines // groups)
    rows += -rows % 16 + 2 * (D // groups)
    return pl.pallas_call(
        functools.partial(mix_grad_kernel, groups),
        grid=(1,),
        in_specs=[whole(item.shape) for item in (normed, first, second) + extras],
        out_specs=whole((groups, rows, channels)),
        out_shape=shape_of((groups, rows, channels), bf16),
        compiler_params=params(),
        cost_estimate=takes(7),
        name="mix_grads",
    )(normed, first, second, *extras)


def out_grad_kernel(groups, first, heads_ref, acted_ref, *rest):
    column_refs, out_refs, rows_ref = rest[:-3], rest[-3:-1], rest[-1]
    width = out_refs[0].shape[0]
    sort_rows(column_refs, groups, rows_ref)
    for k, (left_ref, out_ref) in enumerate(zip((heads_ref, acted_ref), out_refs)):
        columns = rows_ref[:, (first + k) * width : (first + k + 1) * width]
        out_ref[...] = transposed_times(columns, left_ref[...])


def out_grads(groups, first, columns, heads, acted):
    width = D // groups
    lefts = (heads, acted)
    return pl.pallas_call(
        functools.partial(out_grad_kernel, groups, first),
        grid=(1,),
        in_specs=[whole(item.shape) for item in lefts + tuple(columns)],
        out_specs=tuple(whole((width, item.shape[1])) for item in lefts),
        out_shape=tuple(shape_of((width, item.shape[1])) for item in lefts),
        scratch_shapes=[pltpu.VMEM((groups * LEN, columns[0].shape[1]), bf16)],
        compiler_params=params(),
        cost_estimate=takes(6),
        name="out_grads",
    )(*lefts, *columns)


def last_grad_kernel(groups, gated_ref, *rest):
    column_refs, (out_ref, sums_ref, rows_ref) = rest[:-3], rest[-3:]
    share = LEN // len(column_refs)
    stride = column_refs[0].shape[0] // groups
    sums = jnp.zeros(sums_ref.shape, f32)
    for group in range(groups):
        for k, ref in enumerate(column_refs):
            at = group * LEN + k * share
            first = group * stride
            rows_ref[at : at + share, :] = ref[first : first + share, :]
            sums = sums + ref[first + share : first + stride, :].astype(f32)
    sums_ref[...] = sums
    out_ref[...] = transposed_times(rows_ref[...], gated_ref[...])


def last_grads(groups, columns, gated):
    width = D // groups
    extra = columns[0].shape[0] // groups - LEN // len(columns)
    shapes = ((width, gated.shape[1]), (extra, width))
    return pl.pallas_call(
        functools.partial(last_grad_kernel, groups),
        grid=(1,),
        in_specs=[whole(gated.shape)] + [whole(item.shape) for item in columns],
        out_specs=tuple(whole(shape) for shape in shapes),
        out_shape=tuple(shape_of(shape) for shape in shapes),
        scratch_shapes=[pltpu.VMEM((groups * LEN, width), bf16)],
        compiler_params=params(),
        cost_estimate=takes(5),
        name="last_grads",
    )(gated, *columns)


def shards(
    tokens,
    cotangent,
    norm_gains,
    mix_in,
    conv_weight,
    x_proj,
    dt_proj,
    dt_bias,
    a_log,
    skip_gain,
    mix_out,
    ffn_in,
    ffn_out,
    attn_query,
    attn_keyval,
    attn_out,
    router,
    expert_in,
    expert_out,
    routes,
):
    members = lax.axis_size("tensor")
    member = lax.axis_index("tensor")
    share = LEN // members
    groups = lax.axis_size("dp")
    gains = norm_gains.astype(f32)
    me = member.astype(jnp.int32).reshape(1)

    def swap(value, k):
        return lax.ppermute(value, "tensor", [(i, i ^ k) for i in range(members)])

    def join_list(rows):
        return [rows] + [swap(rows, k) for k in range(1, members)]

    def join(rows):
        return jnp.concatenate(join_list(rows), axis=0)

    def split_list(blocks):
        return [blocks[0]] + [swap(blocks[k], k) for k in range(1, members)]

    def blocks_of(partial):
        return [partial[k * share : (k + 1) * share].astype(bf16) for k in range(members)]

    def all_sum(partial):
        total = partial.astype(f32)
        for k in range(1, members):
            total = total + swap(partial, k).astype(f32)
        return total

    def all_sum_rows(partial):
        total = partial.astype(f32)
        for k in range(1, members):
            blocks = swap(partial, k).reshape(members, share, -1)
            ordered = jnp.concatenate([blocks[j ^ k] for j in range(members)], axis=0)
            total = total + ordered.astype(f32)
        return total

    def dp_scatter(value):
        return lax.psum_scatter(value, "dp", scatter_dimension=0, tiled=True)

    def dp_gather(value):
        return lax.all_gather(value, "dp", axis=0, tiled=True)

    def to_columns(*rows):
        came = lax.all_to_all(pack_columns(groups, *rows), "dp", 0, 0, tiled=True)
        return came.reshape(-1, came.shape[2])

    def hold(value, *others):
        return lax.optimization_barrier((value,) + others)[0]

    def gain(index):
        return gains[index : index + 1]

    hidden1, rows1 = norm_forward(tokens.astype(f32), gain(0), [])
    normed1 = join(rows1)
    channels = mix_in.shape[2]
    bias, skip = dt_bias.reshape(1, channels), skip_gain.reshape(1, channels)
    alog = a_log.T
    xz = jnp.einsum("td,dgc->gtc", normed1, mix_in, preferred_element_type=f32)
    u, proj_part = conv_forward(me, members, xz, conv_weight, x_proj)
    proj = all_sum_rows(proj_part)
    gated_low, ys, states, *mixed = scan_forward(
        me, members, proj, dt_proj, bias, alog, skip, u, xz, mix_out
    )
    all_gated = dp_gather(gated_low)
    hidden2, rows2 = norm_forward(hidden1, gain(1), split_list(mixed))
    normed2 = join(rows2)
    gate_up = jnp.einsum("td,dgc->gtc", normed2, ffn_in, preferred_element_type=f32)
    ffn_gate = sigmoid(gate_up[0])
    acted_low = (gate_up[0] * ffn_gate * gate_up[1]).astype(bf16)
    all_acted = dp_gather(acted_low)
    hidden3, rows3 = norm_forward(
        hidden2, gain(2), split_list(blocks_of(matmul(acted_low, ffn_out)))
    )
    keyval = attn_keyval.reshape(D, -1)
    rows3 = join_list(rows3)
    rows3[0] = hold(rows3[0], all_gated)
    normed3, query_low, keyval_low, attended_low, *attended = attention_forward(
        me, members, rows3, attn_query, keyval, attn_out
    )
    all_attended = dp_gather(attended_low)
    hidden4, rows4 = norm_forward(hidden3, gain(3), split_list(attended))
    normed4 = join_list(rows4)

    at = jnp.bitwise_xor(jnp.arange(members, dtype=jnp.int32), member)
    picks = routes.reshape(members, share, 2)[at].reshape(LEN, 2)
    own_picks = picks[:share]
    router_rows = router.T
    moved, expert_low, slot_weights, *dn_part = experts(
        members, picks.T, router_rows, normed4, join_list(cotangent), expert_in, expert_out
    )
    dn_part[0] = hold(dn_part[0], all_acted, all_attended)
    all_moved = dp_gather(moved)
    dn_part = split_list(dn_part)
    made = experts_out(members, 0, 2, expert_low, slot_weights, expert_out)
    dn_part[0] = hold(dn_part[0], made[0])
    grad, low4, gain4, grad_router = router_backward(
        cotangent, hidden4, gain(3), rows4, own_picks, router_rows, dn_part
    )
    grad_low4 = join_list(low4)

    width = D // groups
    units = expert_out.shape[1]

    dqkv, *dnormed = attention_backward(
        me, members, grad_low4, query_low, keyval_low, attn_query, keyval, attn_out
    )
    dn_blocks = split_list(dnormed)
    made = [hold(made[0], dn_blocks[0])] + list(made[1:])
    made = experts_out(members, 1, 2, expert_low, slot_weights, expert_out, made)
    attn_in_part = transposed_times(normed3, dqkv).astype(bf16)
    attn_in_sum = dp_scatter(attn_in_part)
    grad, low3, gain3 = norm_backward(
        hold(grad, attn_in_part, made[0]), hidden3, gain(2), dn_blocks
    )
    grad_low3 = join(low3)

    dact = times_transposed(grad_low3, ffn_out)
    dgate_up = jnp.concatenate(
        [
            dact * ffn_gate * (1.0 + gate_up[0] * (1.0 - ffn_gate)) * gate_up[1],
            dact * gate_up[0] * ffn_gate,
        ],
        axis=1,
    ).astype(bf16)
    hidden_units = ffn_in.shape[2]
    dnormed = jnp.einsum(
        "tgc,dgc->td",
        dgate_up.reshape(LEN, 2, hidden_units),
        ffn_in,
        preferred_element_type=f32,
    )
    dn_blocks = blocks_of(dnormed)
    ffn_in_part = transposed_times(normed2, hold(dgate_up, dn_blocks[0])).astype(bf16)
    ffn_in_sum = dp_scatter(ffn_in_part)
    columns = to_columns(
        hold(rows4, dn_blocks[0]), cotangent, low4, low3, own_picks.astype(f32)
    )
    grad, low2, gain2 = norm_backward(
        hold(grad, ffn_in_part, all_moved),
        hidden2,
        gain(1),
        split_list(dn_blocks),
    )
    grad_low2 = join_list(low2)

    du, dzs, small, dalog, ddt, dcols_part = scan_backward(
        me, members, proj, dt_proj, bias, alog, skip, u, xz, mix_out, grad_low2, ys, states
    )
    dcols = all_sum_rows(dcols_part.astype(bf16))
    dcols = hold(dcols, attn_in_sum, columns)
    columns = join_list(hold(columns, dcols))
    dxs, dxproj, dconv = conv_backward(
        me, members, dcols, proj, u, xz, du, conv_weight, x_proj
    )
    dmixed = jnp.stack([dxs, dzs])
    dnormed = jnp.einsum("gtc,dgc->td", dmixed, mix_in, preferred_element_type=f32)
    dn_blocks = blocks_of(dnormed)
    mix_part = mix_grads(
        groups, normed1, hold(dxs, dn_blocks[0]), dzs, dxproj, ddt, dalog, small[:2], dconv
    )
    mix_sum = dp_scatter(mix_part.reshape(-1, channels)).astype(f32)
    dn_blocks = split_list(dn_blocks)
    dn_blocks[0] = hold(dn_blocks[0], mix_part)
    grad, _, gain1 = norm_backward(grad, hidden1, gain(0), dn_blocks)

    extra = jnp.concatenate([gain1, gain2, gain3, gain4, grad_router], axis=0).astype(bf16)
    extra = jnp.pad(extra, ((0, -extra.shape[0] % 16), (0, 0)))
    last = to_columns(jnp.concatenate([low2, extra], axis=0))
    sorted_rows = sorted_columns(groups, [hold(columns[0], grad, ffn_in_sum)] + columns[1:])
    part = expert_grads(0, EXPERTS // 2, all_moved, *sorted_rows)
    made = split_list([hold(made[0], part[0])] + list(made[1:]))
    hidden5 = hidden4
    for block in made:
        hidden5 = hidden5 + block.astype(f32)
    last = join_list(hold(last, part[0]))
    columns[0] = hold(columns[0], part[0])
    attn_out_sum, ffn_out_sum = out_grads(groups, 2, columns, all_attended, all_acted)
    last[0] = hold(last[0], ffn_out_sum)
    mix_out_sum, model_sum = last_grads(groups, last, all_gated)
    expert_in_grad, expert_out_grad = expert_grads(
        EXPERTS // 2,
        EXPERTS // 2,
        hold(all_moved, mix_out_sum, hidden5),
        *sorted_rows,
        earlier=part,
    )

    slice_of = channels // groups
    xproj_rows, dt_rows = 128 // groups, DT_RANK // groups
    dt_at = 2 * width + xproj_rows
    flat = mix_sum[dt_at + dt_rows :].reshape(-1)
    flat = flat[: (STATE + 2 + CONV) * slice_of].reshape(STATE + 2 + CONV, slice_of)
    heads_cols = attn_query.shape[1]
    attn_in = attn_in_sum.astype(f32)
    return (
        hidden5.astype(bf16),
        grad,
        model_sum[:4],
        jnp.stack([mix_sum[:width], mix_sum[width : 2 * width]], axis=1),
        flat[STATE + 2 :],
        mix_sum[2 * width : 2 * width + xproj_rows].T,
        mix_sum[dt_at : dt_at + dt_rows],
        flat[STATE],
        flat[:STATE].T,
        flat[STATE + 1],
        mix_out_sum.T,
        ffn_in_sum.astype(f32).reshape(width, 2, hidden_units),
        ffn_out_sum.T,
        attn_in[:, :heads_cols],
        attn_in[:, heads_cols:].reshape(-1, 2, attn_keyval.shape[2]),
        attn_out_sum.T,
        model_sum[4 : 4 + EXPERTS].T,
        expert_in_grad,
        expert_out_grad.transpose(0, 2, 1),
    )


def solution(mesh):
    return jax.shard_map(
        shards,
        mesh=mesh,
        in_specs=(
            P(("dp", "tensor"), None),
            P(("dp", "tensor"), None),
            P(),
            P(None, None, "tensor"),
            P(None, "tensor"),
            P("tensor", None),
            P(None, "tensor"),
            P("tensor"),
            P("tensor", None),
            P("tensor"),
            P("tensor", None),
            P(None, None, "tensor"),
            P("tensor", None),
            P(None, "tensor"),
            P(None, None, "tensor"),
            P("tensor", None),
            P(),
            P(None, None, None, "tensor"),
            P(None, "tensor", None),
            P("dp", None),
        ),
        out_specs=(
            P(("dp", "tensor"), None),
            P(("dp", "tensor"), None),
            P(None, "dp"),
            P("dp", None, "tensor"),
            P(None, ("tensor", "dp")),
            P("tensor", "dp"),
            P("dp", "tensor"),
            P(("tensor", "dp")),
            P(("tensor", "dp"), None),
            P(("tensor", "dp")),
            P("tensor", "dp"),
            P("dp", None, "tensor"),
            P("tensor", "dp"),
            P("dp", "tensor"),
            P("dp", None, "tensor"),
            P("tensor", "dp"),
            P("dp", None),
            P(None, "dp", None, "tensor"),
            P(None, "tensor", "dp"),
        ),
        check_vma=False,
    )
```

```python
import functools
import math

import jax
import jax.numpy as jnp
from jax import lax
from jax.experimental import pallas as pl
from jax.experimental.pallas import tpu as pltpu
from jax.sharding import PartitionSpec as P

D = 1536
STATE = 16
CONV = 4
DT_RANK = 96
HEADS = 24
KV_HEADS = 8
HEAD_DIM = 64
EXPERTS = 16
LEN = 256
CAP = 48

epsilon = 1e-06
floor_square = 0.1
masked_score = -1e30
LOG2E = 1.4426950408889634
PAD = 8
CHUNK = 16
GROUP = 16
VMEM_LIMIT = 56 * 1024 * 1024

f32 = jnp.float32
bf16 = jnp.bfloat16


def matmul(left, right):
    return jnp.dot(left, right, preferred_element_type=f32)


def times_transposed(left, right):
    return lax.dot_general(left, right, (((1,), (1,)), ((), ())), preferred_element_type=f32)


def transposed_times(left, right):
    return lax.dot_general(left, right, (((0,), (0,)), ((), ())), preferred_element_type=f32)


def sigmoid(v):
    return 1.0 / (1.0 + jnp.exp(-v))


def dot_exact(left, right):
    return jnp.dot(left, right, precision=lax.Precision.HIGHEST, preferred_element_type=f32)


def column_norm_parts(projected):
    lane = lax.broadcasted_iota(jnp.int32, projected.shape, 1)
    square = projected * projected
    in_step = lane < DT_RANK
    in_b = jnp.logical_and(lane >= DT_RANK, lane < DT_RANK + STATE)
    in_c = lane >= DT_RANK + STATE
    mean_step = jnp.sum(jnp.where(in_step, square, 0.0), axis=1, keepdims=True) / DT_RANK
    mean_b = jnp.sum(jnp.where(in_b, square, 0.0), axis=1, keepdims=True) / STATE
    mean_c = jnp.sum(jnp.where(in_c, square, 0.0), axis=1, keepdims=True) / STATE
    r_step = lax.rsqrt(mean_step + epsilon)
    r_b = lax.rsqrt(jnp.maximum(mean_b, floor_square))
    r_c = lax.rsqrt(jnp.maximum(mean_c, floor_square))
    scale = jnp.where(in_step, r_step, jnp.where(in_b, r_b, r_c))
    return scale, in_step, in_b, in_c, mean_b, mean_c


def row_spread(cols_ref, first, out_ref):
    pick = (
        lax.broadcasted_iota(jnp.int32, (128, CHUNK * STATE), 0) - first
        == lax.broadcasted_iota(jnp.int32, (128, CHUNK * STATE), 1) % STATE
    ).astype(f32)
    out_ref[...] = (dot_exact(cols_ref[...], pick) * chunk_mask(LEN)).astype(bf16)


def chunk_mask(rows):
    return (
        lax.broadcasted_iota(jnp.int32, (rows, CHUNK * STATE), 0) % CHUNK
        == lax.broadcasted_iota(jnp.int32, (rows, CHUNK * STATE), 1) // STATE
    ).astype(f32)


def conv_total(pad_ref, weight_ref, length):
    total = weight_ref[0:1, :] * pad_ref[pl.ds(PAD - CONV + 1, length), :]
    for tap in range(1, CONV):
        total = total + weight_ref[tap : tap + 1, :] * pad_ref[pl.ds(PAD - CONV + 1 + tap, length), :]
    return total


def conv_forward_kernel(blocks, me_ref, xz_ref, weight_ref, xproj_ref, u_ref, proj_ref, pad_ref):
    me = me_ref[0]
    size = LEN // blocks
    pad_ref[0:PAD, :] = jnp.zeros((PAD, pad_ref.shape[1]), f32)
    for m in range(blocks):
        at = pl.multiple_of(jnp.bitwise_xor(me, m) * size, size)
        pad_ref[PAD + m * size : PAD + (m + 1) * size, :] = xz_ref[0, pl.ds(at, size), :]
    total = conv_total(pad_ref, weight_ref, LEN)
    u = total * sigmoid(total)
    for m in range(blocks):
        at = pl.multiple_of(jnp.bitwise_xor(me, m) * size, size)
        u_ref[pl.ds(at, size), :] = u[m * size : (m + 1) * size, :]
    proj_ref[...] = matmul(u_ref[...].astype(bf16), xproj_ref[...]).astype(bf16)


def scan_setup(proj_ref, cols_ref, b_ref, c_ref):
    projected = proj_ref[...]
    scale = column_norm_parts(projected)[0]
    cols_ref[...] = projected * scale
    row_spread(cols_ref, DT_RANK, b_ref)
    row_spread(cols_ref, DT_RANK + STATE, c_ref)


def step_sizes(cols_ref, dt_proj_ref, bias_ref):
    low = cols_ref[:, :DT_RANK].astype(bf16)
    pre = matmul(low, dt_proj_ref[...]) + bias_ref[...]
    return low, pre, jnp.maximum(pre, 0.0) + jnp.log1p(jnp.exp(-jnp.abs(pre)))


def chunk_place(index, me, size):
    block = index // (size // CHUNK)
    inner = index % (size // CHUNK)
    return pl.multiple_of(jnp.bitwise_xor(block, me) * size + inner * CHUNK, CHUNK)


def chunk_group(index):
    out = []
    for q in range(GROUP):
        base = (index * GROUP + q) * CHUNK
        out.append(
            (
                pl.ds(pl.multiple_of(base, CHUNK), CHUNK),
                pl.ds(pl.multiple_of(base * STATE, CHUNK * STATE), CHUNK * STATE),
            )
        )
    return out


def push_chunks(left_ref, right_ref, out_ref):
    def body(index, carry):
        for rows, many in chunk_group(index):
            out_ref[many, :] = transposed_times(left_ref[rows, :], right_ref[rows, :])
        return carry

    lax.fori_loop(0, LEN // CHUNK // GROUP, body, 0)


def scan_forward_kernel(
    blocks,
    me_ref,
    proj_ref,
    dt_proj_ref,
    bias_ref,
    alog_ref,
    skip_ref,
    u_ref,
    xz_ref,
    out_w_ref,
    gated_ref,
    ys_ref,
    states_ref,
    *rest,
):
    out_refs = rest[:blocks]
    cols_ref, b_ref, c_ref, delta_ref, drive_ref, push_ref, kept_ref, sems = rest[blocks:]
    me = me_ref[0]
    size = LEN // blocks
    lanes = u_ref.shape[1]
    scan_setup(proj_ref, cols_ref, b_ref, c_ref)

    _, _, delta = step_sizes(cols_ref, dt_proj_ref, bias_ref)
    delta_ref[...] = delta
    drive_ref[...] = (delta * u_ref[...]).astype(bf16)
    rate = -jnp.exp(alog_ref[...]) * LOG2E
    push_chunks(b_ref, drive_ref, push_ref)

    def chunk(index, state):
        base = chunk_place(index, me, size)
        steps = delta_ref[pl.ds(base, CHUNK), :]
        for j in range(CHUNK):
            at = pl.ds(pl.multiple_of((base + j) * STATE, STATE), STATE)
            state = jnp.exp2(steps[j : j + 1, :] * rate) * state + push_ref[at, :]
            kept_ref[at, :] = state.astype(bf16)
        return state

    state = jnp.zeros((STATE, lanes), f32)
    copies = []
    per = size // CHUNK
    for block in range(blocks):
        state = lax.fori_loop(block * per, (block + 1) * per, chunk, state)
        copies.append(states_copy(kept_ref, states_ref, sems, block, me, size))
        copies[-1].start()

    def output(index, carry):
        for rows, many in chunk_group(index):
            ys_ref[rows, :] = matmul(c_ref[rows, :], kept_ref[many, :])
        return carry

    lax.fori_loop(0, LEN // CHUNK // GROUP, output, 0)
    ys = ys_ref[...] + skip_ref[...] * u_ref[...]
    ys_ref[...] = ys
    zs = xz_ref[0]
    gated = (ys * (zs * sigmoid(zs))).astype(bf16)
    gated_ref[...] = gated
    store_blocks(out_refs, matmul(gated, out_w_ref[...]))
    for copy in copies:
        copy.wait()


def states_copy(from_ref, to_ref, sems, block, me, size):
    many = size * STATE
    rows = pl.ds(pl.multiple_of(jnp.bitwise_xor(me, block) * many, many), many)
    return pltpu.make_async_copy(from_ref.at[rows, :], to_ref.at[rows, :], sems.at[block])


def scan_backward_kernel(
    blocks,
    me_ref,
    proj_ref,
    dt_proj_ref,
    bias_ref,
    alog_ref,
    skip_ref,
    u_ref,
    xz_ref,
    out_w_ref,
    ys_ref,
    stored_ref,
    *rest,
):
    grad_refs = rest[:blocks]
    (
        du_ref,
        dzs_ref,
        small_ref,
        dalog_ref,
        ddt_ref,
        dcols_ref,
        grad_ref,
        cols_ref,
        b_ref,
        c_ref,
        pb_ref,
        pc_ref,
        delta_ref,
        drive_ref,
        dys_ref,
        ddrive_ref,
        drate_ref,
        dlow_ref,
        push_ref,
        grads_ref,
        rates_ref,
        states_ref,
        sems,
    ) = rest[blocks:]
    me = me_ref[0]
    size = LEN // blocks
    lanes = u_ref.shape[1]
    copies = [
        states_copy(stored_ref, states_ref, sems, block, me, size) for block in range(blocks)
    ]
    for copy in copies:
        copy.start()
    scan_setup(proj_ref, cols_ref, b_ref, c_ref)
    join_blocks(grad_refs, grad_ref)

    low, pre, delta = step_sizes(cols_ref, dt_proj_ref, bias_ref)
    u = u_ref[...]
    delta_ref[...] = delta
    drive_ref[...] = (delta * u).astype(bf16)
    dgated = times_transposed(grad_ref[...], out_w_ref[...])
    zs = xz_ref[0]
    gate = sigmoid(zs)
    dys = dgated * (zs * gate)
    dys_ref[...] = dys.astype(bf16)
    dzs_ref[...] = (dgated * ys_ref[...] * (gate * (1.0 + zs * (1.0 - gate)))).astype(bf16)
    a_matrix = -jnp.exp(alog_ref[...])
    rate = a_matrix * LOG2E
    chunks = LEN // CHUNK
    mask = chunk_mask(CHUNK)
    push_chunks(c_ref, dys_ref, push_ref)

    def chunk(step_index, carry):
        adjoint, da = carry
        index = chunks - 1 - step_index
        base = chunk_place(index, me, size)
        before = chunk_place(jnp.maximum(index - 1, 0), me, size)
        first = (index > 0).astype(f32)
        steps = delta_ref[pl.ds(base, CHUNK), :]
        for j in range(CHUNK - 1, -1, -1):
            at = pl.ds(pl.multiple_of((base + j) * STATE, STATE), STATE)
            if j > 0:
                last = (base + j - 1) * STATE
                earlier = states_ref[pl.ds(pl.multiple_of(last, STATE), STATE), :].astype(f32)
            else:
                last = (before + CHUNK - 1) * STATE
                earlier = states_ref[pl.ds(pl.multiple_of(last, STATE), STATE), :].astype(f32) * first
            grad = adjoint + push_ref[at, :]
            grads_ref[at, :] = grad.astype(bf16)
            adjoint = grad * jnp.exp2(steps[j : j + 1, :] * rate)
            through = adjoint * earlier
            rates_ref[at, :] = (through * a_matrix).astype(bf16)
            da = da + through * steps[j : j + 1, :]
        return adjoint, da

    for copy in copies:
        copy.wait()
    zero = jnp.zeros((STATE, lanes), f32)
    _, da = lax.fori_loop(0, chunks, chunk, (zero, zero))
    mask_low = mask.astype(bf16)

    def output(index, carry):
        for rows, many in chunk_group(index):
            grads = grads_ref[many, :]
            ddrive_ref[rows, :] = matmul(b_ref[rows, :], grads)
            drate_ref[rows, :] = matmul(mask_low, rates_ref[many, :])
            pb_ref[rows, :] = times_transposed(drive_ref[rows, :], grads) * mask
            pc_ref[rows, :] = times_transposed(dys_ref[rows, :], states_ref[many, :]) * mask
        return carry

    lax.fori_loop(0, chunks // GROUP, output, 0)
    dalog_ref[...] = da * a_matrix
    ddrive = ddrive_ref[...]
    du_ref[...] = ddrive * delta + skip_ref[...] * dys
    dpre = (ddrive * u + drate_ref[...]) * sigmoid(pre)
    dpre_low = dpre.astype(bf16)
    small_ref[...] = jnp.concatenate(
        [
            jnp.sum(dpre, axis=0, keepdims=True),
            jnp.sum(dys * u, axis=0, keepdims=True),
            jnp.zeros((6, lanes), f32),
        ],
        axis=0,
    )
    ddt_ref[...] = transposed_times(low, dpre_low)
    dlow_ref[...] = times_transposed(dpre_low, dt_proj_ref[...])
    collect = (
        lax.broadcasted_iota(jnp.int32, (CHUNK * STATE, STATE), 0) % STATE
        == lax.broadcasted_iota(jnp.int32, (CHUNK * STATE, STATE), 1)
    ).astype(f32)
    dcols_ref[...] = jnp.concatenate(
        [dlow_ref[...], dot_exact(pb_ref[...], collect), dot_exact(pc_ref[...], collect)], axis=1
    )


def conv_backward_kernel(
    blocks,
    me_ref,
    dcols_ref,
    proj_ref,
    u_ref,
    xz_ref,
    du_ref,
    weight_ref,
    xproj_ref,
    dxs_ref,
    dxproj_ref,
    dweight_ref,
    pad_ref,
    grad_ref,
):
    me = me_ref[0]
    size = LEN // blocks
    lanes = u_ref.shape[1]
    projected = proj_ref[...]
    scale, in_step, in_b, in_c, mean_b, mean_c = column_norm_parts(projected)
    normed = projected * scale
    dcols = dcols_ref[...]
    product = dcols * normed
    dot_step = jnp.sum(jnp.where(in_step, product, 0.0), axis=1, keepdims=True) / DT_RANK
    dot_b = jnp.sum(jnp.where(in_b, product, 0.0), axis=1, keepdims=True) / STATE
    dot_c = jnp.sum(jnp.where(in_c, product, 0.0), axis=1, keepdims=True) / STATE
    dot_b = jnp.where(mean_b > floor_square, dot_b, 0.0)
    dot_c = jnp.where(mean_c > floor_square, dot_c, 0.0)
    mean = jnp.where(in_step, dot_step, jnp.where(in_b, dot_b, dot_c))
    dproj = (scale * (dcols - normed * mean)).astype(bf16)
    dxproj_ref[...] = transposed_times(dproj, u_ref[...].astype(bf16))
    du = du_ref[...] + times_transposed(dproj, xproj_ref[...])
    pad_ref[0:PAD, :] = jnp.zeros((PAD, lanes), f32)
    grad_ref[LEN : LEN + PAD, :] = jnp.zeros((PAD, lanes), f32)
    for m in range(blocks):
        at = pl.multiple_of(jnp.bitwise_xor(me, m) * size, size)
        pad_ref[PAD + m * size : PAD + (m + 1) * size, :] = xz_ref[0, pl.ds(at, size), :]
    dxs_ref[...] = du.astype(bf16)
    du_ref_rows = []
    grad_ref[0:LEN, :] = du
    total = conv_total(pad_ref, weight_ref, LEN)
    gate = sigmoid(total)
    slope = gate * (1.0 + total * (1.0 - gate))
    for m in range(blocks):
        at = pl.multiple_of(jnp.bitwise_xor(me, m) * size, size)
        du_ref_rows.append(grad_ref[pl.ds(at, size), :])
    grad_ref[0:LEN, :] = jnp.concatenate(du_ref_rows, axis=0) * slope
    dcv = grad_ref[0:LEN, :]
    dweight_ref[...] = jnp.concatenate(
        [
            jnp.sum(dcv * pad_ref[pl.ds(PAD - CONV + 1 + tap, LEN), :], axis=0, keepdims=True)
            for tap in range(CONV)
        ],
        axis=0,
    )
    dxs = weight_ref[CONV - 1 : CONV, :] * dcv
    for tap in range(CONV - 1):
        dxs = dxs + weight_ref[tap : tap + 1, :] * grad_ref[pl.ds(CONV - 1 - tap, LEN), :]
    dxs = dxs.astype(bf16)
    for m in range(blocks):
        at = pl.multiple_of(jnp.bitwise_xor(me, m) * size, size)
        dxs_ref[pl.ds(at, size), :] = dxs[m * size : (m + 1) * size, :]


def store_blocks(refs, value):
    size = value.shape[0] // len(refs)
    for k, ref in enumerate(refs):
        ref[...] = value[k * size : (k + 1) * size].astype(ref.dtype)


def join_blocks(refs, out_ref):
    size = out_ref.shape[0] // len(refs)
    for k, ref in enumerate(refs):
        out_ref[k * size : (k + 1) * size, :] = ref[...]


SMEM = pl.BlockSpec(memory_space=pltpu.SMEM)


def whole(shape):
    return pl.BlockSpec(shape, lambda *_: (0,) * len(shape))


def params():
    return pltpu.CompilerParams(vmem_limit_bytes=VMEM_LIMIT)


def takes(microseconds):
    return pl.CostEstimate(
        flops=int(microseconds * 1.15e9), bytes_accessed=1 << 20, transcendentals=0
    )


def shape_of(shape, dtype=f32):
    return jax.ShapeDtypeStruct(shape, dtype)


def conv_forward(me, blocks, xz, weight, x_proj):
    channels = xz.shape[2]
    return pl.pallas_call(
        functools.partial(conv_forward_kernel, blocks),
        grid=(1,),
        in_specs=[
            SMEM,
            pl.BlockSpec((1, LEN, channels), lambda i: (0, 0, 0)),
            whole(weight.shape),
            whole(x_proj.shape),
        ],
        out_specs=(whole((LEN, channels)), whole((LEN, 128))),
        out_shape=(shape_of((LEN, channels)), shape_of((LEN, 128), bf16)),
        scratch_shapes=[pltpu.VMEM((LEN + PAD, channels), f32)],
        compiler_params=params(),
        cost_estimate=takes(3),
        name="conv_forward",
    )(me, xz, weight, x_proj)


def lane_block(channels):
    return channels


def scan_forward(me, blocks, proj, dt_proj, bias, alog, skip, u, xz, out_w):
    channels = u.shape[1]
    lanes = lane_block(channels)
    col = lambda i: (0, i)
    return pl.pallas_call(
        functools.partial(scan_forward_kernel, blocks),
        grid=(channels // lanes,),
        in_specs=[
            SMEM,
            whole((LEN, 128)),
            pl.BlockSpec((DT_RANK, lanes), col),
            pl.BlockSpec((1, lanes), col),
            pl.BlockSpec((STATE, lanes), col),
            pl.BlockSpec((1, lanes), col),
            pl.BlockSpec((LEN, lanes), col),
            pl.BlockSpec((1, LEN, lanes), lambda i: (1, 0, i)),
            pl.BlockSpec((lanes, D), lambda i: (i, 0)),
        ],
        out_specs=(
            pl.BlockSpec((LEN, lanes), col),
            pl.BlockSpec((LEN, lanes), col),
            pl.BlockSpec(memory_space=pl.ANY),
        )
        + (whole((LEN // blocks, D)),) * blocks,
        out_shape=(
            shape_of((LEN, channels), bf16),
            shape_of((LEN, channels)),
            shape_of((LEN * STATE, channels), bf16),
        )
        + (shape_of((LEN // blocks, D), bf16),) * blocks,
        scratch_shapes=[
            pltpu.VMEM((LEN, 128), f32),
            pltpu.VMEM((LEN, CHUNK * STATE), bf16),
            pltpu.VMEM((LEN, CHUNK * STATE), bf16),
            pltpu.VMEM((LEN, lanes), f32),
            pltpu.VMEM((LEN, lanes), bf16),
            pltpu.VMEM((LEN * STATE, lanes), f32),
            pltpu.VMEM((LEN * STATE, lanes), bf16),
            pltpu.SemaphoreType.DMA((blocks,)),
        ],
        compiler_params=params(),
        cost_estimate=takes(13),
        name="scan_forward",
    )(me, proj, dt_proj, bias, alog, skip, u, xz, out_w)


def scan_backward(me, blocks, proj, dt_proj, bias, alog, skip, u, xz, out_w, grad, ys, states):
    channels = u.shape[1]
    lanes = lane_block(channels)
    col = lambda i: (0, i)
    rows = pl.BlockSpec((LEN, lanes), col)
    return pl.pallas_call(
        functools.partial(scan_backward_kernel, blocks),
        grid=(channels // lanes,),
        in_specs=[
            SMEM,
            whole((LEN, 128)),
            pl.BlockSpec((DT_RANK, lanes), col),
            pl.BlockSpec((1, lanes), col),
            pl.BlockSpec((STATE, lanes), col),
            pl.BlockSpec((1, lanes), col),
            rows,
            pl.BlockSpec((1, LEN, lanes), lambda i: (1, 0, i)),
            pl.BlockSpec((lanes, D), lambda i: (i, 0)),
            rows,
            pl.BlockSpec(memory_space=pl.ANY),
        ]
        + [whole((LEN // blocks, D))] * blocks,
        out_specs=(
            rows,
            rows,
            pl.BlockSpec((8, lanes), col),
            pl.BlockSpec((STATE, lanes), col),
            pl.BlockSpec((DT_RANK, lanes), col),
            whole((LEN, 128)),
        ),
        out_shape=(
            shape_of((LEN, channels)),
            shape_of((LEN, channels), bf16),
            shape_of((8, channels)),
            shape_of((STATE, channels)),
            shape_of((DT_RANK, channels)),
            shape_of((LEN, 128)),
        ),
        scratch_shapes=[
            pltpu.VMEM((LEN, D), bf16),
            pltpu.VMEM((LEN, 128), f32),
            pltpu.VMEM((LEN, CHUNK * STATE), bf16),
            pltpu.VMEM((LEN, CHUNK * STATE), bf16),
            pltpu.VMEM((LEN, CHUNK * STATE), f32),
            pltpu.VMEM((LEN, CHUNK * STATE), f32),
            pltpu.VMEM((LEN, lanes), f32),
            pltpu.VMEM((LEN, lanes), bf16),
            pltpu.VMEM((LEN, lanes), bf16),
            pltpu.VMEM((LEN, lanes), f32),
            pltpu.VMEM((LEN, lanes), f32),
            pltpu.VMEM((LEN, DT_RANK), f32),
            pltpu.VMEM((LEN * STATE, lanes), f32),
            pltpu.VMEM((LEN * STATE, lanes), bf16),
            pltpu.VMEM((LEN * STATE, lanes), bf16),
            pltpu.VMEM((LEN * STATE, lanes), bf16),
            pltpu.SemaphoreType.DMA((blocks,)),
        ],
        compiler_params=params(),
        cost_estimate=takes(21),
        name="scan_backward",
    )(me, proj, dt_proj, bias, alog, skip, u, xz, out_w, ys, states, *grad)


def conv_backward(me, blocks, dcols, proj, u, xz, du, weight, x_proj):
    channels = u.shape[1]
    return pl.pallas_call(
        functools.partial(conv_backward_kernel, blocks),
        grid=(1,),
        in_specs=[
            SMEM,
            whole((LEN, 128)),
            whole((LEN, 128)),
            whole((LEN, channels)),
            pl.BlockSpec((1, LEN, channels), lambda i: (0, 0, 0)),
            whole((LEN, channels)),
            whole(weight.shape),
            whole(x_proj.shape),
        ],
        out_specs=(whole((LEN, channels)), whole((128, channels)), whole((CONV, channels))),
        out_shape=(
            shape_of((LEN, channels), bf16),
            shape_of((128, channels)),
            shape_of((CONV, channels)),
        ),
        scratch_shapes=[
            pltpu.VMEM((LEN + PAD, channels), f32),
            pltpu.VMEM((LEN + PAD, channels), f32),
        ],
        compiler_params=params(),
        cost_estimate=takes(5),
        name="conv_backward",
    )(me, dcols, proj, u, xz, du, weight, x_proj)


def attention_probabilities(q, k, allowed):
    scores = times_transposed(q, k) * (1.0 / math.sqrt(HEAD_DIM))
    scores = jnp.where(allowed, scores, masked_score)
    peak = jnp.max(scores, axis=1, keepdims=True)
    exponent = jnp.exp(scores - peak)
    return exponent / jnp.sum(exponent, axis=1, keepdims=True)


def causal(me, blocks):
    size = LEN // blocks

    def position(axis):
        index = lax.broadcasted_iota(jnp.int32, (LEN, LEN), axis)
        return jnp.bitwise_xor(index // size, me) * size + index % size

    return position(1) <= position(0)


def attention_forward_kernel(
    blocks, me_ref, wq_ref, wkv_ref, wo_ref, *rest
):
    joined_ref, q_ref, kv_ref, o_ref = rest[blocks : blocks + 4]
    out_refs = rest[blocks + 4 :]
    join_blocks(rest[:blocks], joined_ref)
    normed = joined_ref[...]
    q_ref[...] = matmul(normed, wq_ref[...]).astype(bf16)
    kv_ref[...] = matmul(normed, wkv_ref[...]).astype(bf16)
    kv_heads = wkv_ref.shape[1] // (2 * HEAD_DIM)
    group = HEADS // KV_HEADS
    allowed = causal(me_ref[0], blocks)
    outs = []
    for head in range(kv_heads * group):
        kv = head // group
        q = q_ref[:, head * HEAD_DIM : (head + 1) * HEAD_DIM]
        k = kv_ref[:, kv * HEAD_DIM : (kv + 1) * HEAD_DIM]
        v = kv_ref[:, (kv_heads + kv) * HEAD_DIM : (kv_heads + kv + 1) * HEAD_DIM]
        soft = attention_probabilities(q, k, allowed)
        outs.append(matmul(soft.astype(bf16), v).astype(bf16))
    o_ref[...] = jnp.concatenate(outs, axis=1)
    store_blocks(out_refs, matmul(o_ref[...], wo_ref[...]))


def attention_backward_kernel(
    blocks,
    me_ref,
    q_ref,
    kv_ref,
    wq_ref,
    wkv_ref,
    wo_ref,
    *rest,
):
    dqkv_ref, grad_ref = rest[blocks], rest[-1]
    join_blocks(rest[:blocks], grad_ref)
    dout = times_transposed(grad_ref[...], wo_ref[...]).astype(bf16)
    kv_heads = wkv_ref.shape[1] // (2 * HEAD_DIM)
    group = HEADS // KV_HEADS
    allowed = causal(me_ref[0], blocks)
    scale = 1.0 / math.sqrt(HEAD_DIM)
    dqs, dks, dvs = [], [], []
    for kv in range(kv_heads):
        k = kv_ref[:, kv * HEAD_DIM : (kv + 1) * HEAD_DIM]
        v = kv_ref[:, (kv_heads + kv) * HEAD_DIM : (kv_heads + kv + 1) * HEAD_DIM]
        dk = jnp.zeros((LEN, HEAD_DIM), f32)
        dv = jnp.zeros((LEN, HEAD_DIM), f32)
        for head in range(kv * group, (kv + 1) * group):
            q = q_ref[:, head * HEAD_DIM : (head + 1) * HEAD_DIM]
            do = dout[:, head * HEAD_DIM : (head + 1) * HEAD_DIM]
            soft = attention_probabilities(q, k, allowed)
            dsoft = times_transposed(do, v)
            dscore = soft * (dsoft - jnp.sum(soft * dsoft, axis=1, keepdims=True))
            dscore = dscore.astype(bf16)
            dqs.append((matmul(dscore, k) * scale).astype(bf16))
            dk = dk + transposed_times(dscore, q) * scale
            dv = dv + transposed_times(soft.astype(bf16), do)
        dks.append(dk.astype(bf16))
        dvs.append(dv.astype(bf16))
    dq = jnp.concatenate(dqs, axis=1)
    dkv = jnp.concatenate(dks + dvs, axis=1)
    dqkv_ref[:, : dq.shape[1]] = dq
    dqkv_ref[:, dq.shape[1] :] = dkv
    dn = times_transposed(dq, wq_ref[...]) + times_transposed(dkv, wkv_ref[...])
    store_blocks(rest[blocks + 1 : -1], dn)


def attention_forward(me, blocks, normed, wq, wkv, wo):
    size = LEN // blocks
    heads = shape_of((LEN, wq.shape[1]), bf16)
    kept = (shape_of((LEN, D), bf16), heads, shape_of((LEN, wkv.shape[1]), bf16), heads)
    return pl.pallas_call(
        functools.partial(attention_forward_kernel, blocks),
        grid=(1,),
        in_specs=[SMEM, whole(wq.shape), whole(wkv.shape), whole(wo.shape)]
        + [whole((size, D))] * blocks,
        out_specs=tuple(whole(item.shape) for item in kept) + (whole((size, D)),) * blocks,
        out_shape=kept + (shape_of((size, D), bf16),) * blocks,
        compiler_params=params(),
        cost_estimate=takes(6),
        name="attention_forward",
    )(me, wq, wkv, wo, *normed)


def attention_backward(me, blocks, grad, q, kv, wq, wkv, wo):
    size = LEN // blocks
    cols = wq.shape[1] + wkv.shape[1]
    return pl.pallas_call(
        functools.partial(attention_backward_kernel, blocks),
        grid=(1,),
        in_specs=[
            SMEM,
            whole(q.shape),
            whole(kv.shape),
            whole(wq.shape),
            whole(wkv.shape),
            whole(wo.shape),
        ]
        + [whole((size, D))] * blocks,
        out_specs=(whole((LEN, cols)),) + (whole((size, D)),) * blocks,
        out_shape=(shape_of((LEN, cols), bf16),) + (shape_of((size, D), bf16),) * blocks,
        scratch_shapes=[pltpu.VMEM((LEN, D), bf16)],
        compiler_params=params(),
        cost_estimate=takes(8),
        name="attention_backward",
    )(me, q, kv, wq, wkv, wo, *grad)


def norm_forward_kernel(hidden_ref, gain_ref, *rest):
    part_refs, (out_ref, normed_ref) = rest[:-2], rest[-2:]
    hidden = hidden_ref[...].astype(f32)
    for ref in part_refs:
        hidden = hidden + ref[...].astype(f32)
    scale = lax.rsqrt(jnp.mean(hidden * hidden, axis=1, keepdims=True) + epsilon)
    out_ref[...] = hidden
    normed_ref[...] = (hidden * scale * gain_ref[...]).astype(bf16)


def norm_forward(hidden, gain, parts):
    shape = hidden.shape
    return pl.pallas_call(
        norm_forward_kernel,
        grid=(1,),
        in_specs=[whole(shape), whole((1, D))] + [whole(shape)] * len(parts),
        out_specs=(whole(shape), whole(shape)),
        out_shape=(shape_of(shape), shape_of(shape, bf16)),
        compiler_params=params(),
        cost_estimate=takes(2),
        name="norm_forward",
    )(hidden, gain, *parts)


def pull_norm(grad, hidden, gain):
    scale = lax.rsqrt(jnp.mean(hidden * hidden, axis=1, keepdims=True) + epsilon)
    unit = hidden * scale
    through = grad * gain
    back = scale * (through - unit * jnp.mean(through * unit, axis=1, keepdims=True))
    return back, jnp.sum(grad * unit, axis=0, keepdims=True)


def norm_backward_kernel(grad_ref, hidden_ref, gain_ref, *rest):
    part_refs, (out_ref, low_ref, dgain_ref) = rest[:-3], rest[-3:]
    dn = part_refs[0][...].astype(f32)
    for ref in part_refs[1:]:
        dn = dn + ref[...].astype(f32)
    back, dgain = pull_norm(dn, hidden_ref[...], gain_ref[...])
    grad = grad_ref[...] + back
    out_ref[...] = grad
    low_ref[...] = grad.astype(bf16)
    dgain_ref[...] = dgain


def norm_backward(grad, hidden, gain, parts):
    shape = hidden.shape
    return pl.pallas_call(
        norm_backward_kernel,
        grid=(1,),
        in_specs=[whole(shape), whole(shape), whole((1, D))] + [whole(shape)] * len(parts),
        out_specs=(whole(shape), whole(shape), whole((1, D))),
        out_shape=(shape_of(shape), shape_of(shape, bf16), shape_of((1, D))),
        compiler_params=params(),
        cost_estimate=takes(2.5),
        name="norm_backward",
    )(grad, hidden, gain, *parts)


def router_backward_kernel(grad_ref, hidden_ref, gain_ref, normed_ref, picks_ref, router_ref, *rest):
    part_refs, (out_ref, low_ref, dgain_ref, drouter_ref) = rest[:-4], rest[-4:]
    dn = part_refs[0][...].astype(f32)
    for ref in part_refs[1:]:
        dn = dn + ref[...].astype(f32)
    normed, router = normed_ref[...], router_ref[...]
    rows = normed.shape[0]
    ids = lax.broadcasted_iota(jnp.int32, (rows, EXPERTS), 1)
    logits = times_transposed(normed, router)
    hot = [(ids == picks_ref[:, k : k + 1]).astype(f32) for k in (0, 1)]
    chosen = [jnp.sum(hot[k] * logits, axis=1, keepdims=True) for k in (0, 1)]
    peak = jnp.maximum(chosen[0], chosen[1])
    weight = [jnp.exp(value - peak) for value in chosen]
    total = weight[0] + weight[1]
    weight = [value / total for value in weight]
    dw = [dn[:, D + k : D + k + 1] for k in (0, 1)]
    mean = weight[0] * dw[0] + weight[1] * dw[1]
    dlog = sum(hot[k] * (weight[k] * (dw[k] - mean)) for k in (0, 1)).astype(bf16)
    dn = dn[:, :D] + matmul(dlog, router)
    back, dgain = pull_norm(dn, hidden_ref[...], gain_ref[...])
    grad = grad_ref[...].astype(f32) + back
    out_ref[...] = grad
    low_ref[...] = grad.astype(bf16)
    dgain_ref[...] = dgain
    drouter_ref[...] = transposed_times(dlog, normed)


def router_backward(grad, hidden, gain, normed, picks, router, parts):
    shape = hidden.shape
    wide_rows = whole((shape[0], D + 128))
    return pl.pallas_call(
        router_backward_kernel,
        grid=(1,),
        in_specs=[
            whole(shape),
            whole(shape),
            whole((1, D)),
            whole(shape),
            whole((shape[0], 2)),
            whole((EXPERTS, D)),
        ]
        + [wide_rows] * len(parts),
        out_specs=(whole(shape), whole(shape), whole((1, D)), whole((EXPERTS, D))),
        out_shape=(
            shape_of(shape),
            shape_of(shape, bf16),
            shape_of((1, D)),
            shape_of((EXPERTS, D)),
        ),
        compiler_params=params(),
        cost_estimate=takes(3),
        name="router_backward",
    )(grad, hidden, gain, normed, picks, router, *parts)


def experts_kernel(blocks, routes_ref, router_ref, w_in_ref, w_out_ref, *rest):
    normed_refs, grad_refs = rest[:blocks], rest[blocks : 2 * blocks]
    moved_ref, act_ref, weighted_ref = rest[2 * blocks : 2 * blocks + 3]
    dn_refs = rest[2 * blocks + 3 : 3 * blocks + 3]
    (
        normed_ref,
        grad_ref,
        even_ref,
        odd_ref,
        grads_ref,
        place_ref,
        first_ref,
        second_ref,
        scale_ref,
        back_ref,
        kept_ref,
        dw_ref,
        sort_ref,
    ) = rest[3 * blocks + 3 :]
    expert = pl.program_id(0)
    slots = EXPERTS * CAP
    units = w_out_ref.shape[1]

    @pl.when(expert == 0)
    def _():
        join_blocks(normed_refs, normed_ref)
        join_blocks(grad_refs, grad_ref)
        routes = routes_ref[...]
        ids = lax.broadcasted_iota(jnp.int32, (EXPERTS, LEN), 0)
        hot = [(ids == routes[k : k + 1, :]).astype(f32) for k in (0, 1)]
        earlier = (
            lax.broadcasted_iota(jnp.int32, (LEN, LEN), 0)
            < lax.broadcasted_iota(jnp.int32, (LEN, LEN), 1)
        ).astype(bf16)
        rank0 = matmul(hot[0].astype(bf16), earlier)
        rank1 = matmul(hot[1].astype(bf16), earlier) + jnp.sum(hot[0], axis=1, keepdims=True)
        counts = jnp.sum(hot[0] + hot[1], axis=1, keepdims=True)
        below = (
            lax.broadcasted_iota(jnp.int32, (EXPERTS, EXPERTS), 1)
            < lax.broadcasted_iota(jnp.int32, (EXPERTS, EXPERTS), 0)
        ).astype(f32)
        starts = dot_exact(below, jnp.broadcast_to(counts, (EXPERTS, 128)))[:, 0:1]
        slot = lax.broadcasted_iota(jnp.int32, (EXPERTS, slots), 1)
        owner = (
            slot // CAP == lax.broadcasted_iota(jnp.int32, (EXPERTS, slots), 0)
        ).astype(f32)
        place_in = (slot % CAP).astype(f32)
        row = jnp.sum(owner * (starts + place_in + 1.0), axis=0, keepdims=True) - 1.0
        used = jnp.sum(owner * (place_in < counts).astype(f32), axis=0, keepdims=True)
        row = jnp.where(used > 0.5, row, -1.0).astype(jnp.int32)
        rows = lax.broadcasted_iota(jnp.int32, (2 * LEN, slots), 0)
        sort_ref[...] = (rows == row).astype(f32).astype(bf16)
        first = ids.astype(f32) * CAP
        position = [
            jnp.sum(hot[k] * (first + rank), axis=0, keepdims=True).astype(jnp.int32)
            for k, rank in ((0, rank0), (1, rank1))
        ]
        logits = times_transposed(router_ref[...], normed_ref[...])
        chosen = [jnp.sum(hot[k] * logits, axis=0, keepdims=True) for k in (0, 1)]
        peak = jnp.maximum(chosen[0], chosen[1])
        weight = [jnp.exp(value - peak) for value in chosen]
        total = weight[0] + weight[1]
        weight = [value / total for value in weight]
        slot = lax.broadcasted_iota(jnp.int32, (slots, LEN), 0)
        in0 = (slot == position[0]).astype(f32)
        in1 = (slot == position[1]).astype(f32)
        weighted = in0 * weight[0] + in1 * weight[1]
        place = (in0 + in1).astype(bf16)
        first_ref[...] = in0.astype(bf16)
        second_ref[...] = in1.astype(bf16)
        place_ref[...] = place
        weighted_ref[...] = weighted.astype(bf16)
        scale_ref[...] = jnp.broadcast_to(jnp.sum(weighted, axis=1, keepdims=True), (slots, 128))
        grads_ref[...] = matmul(place, grad_ref[...]).astype(bf16)
        spread = lax.broadcasted_iota(jnp.int32, (128, 256), 1) - 2 * lax.broadcasted_iota(
            jnp.int32, (128, 256), 0
        )
        for block in range(D // 128):
            rows = matmul(place, normed_ref[:, block * 128 : (block + 1) * 128]).astype(bf16)
            cols = slice(block * 256, (block + 1) * 256)
            even_ref[:, cols] = matmul(rows, (spread == 0).astype(bf16)).astype(bf16)
            odd_ref[:, cols] = matmul(rows, (spread == 1).astype(bf16)).astype(bf16)

    mine = pl.ds(pl.multiple_of(expert * CAP, CAP), CAP)
    w_in = w_in_ref[0].reshape(2 * D, units)
    w_out = w_out_ref[0]
    both = matmul(jnp.concatenate([even_ref[mine, :], odd_ref[mine, :]], axis=0), w_in)
    gate, up = both[:CAP], both[CAP:]
    sig = sigmoid(gate)
    silu = gate * sig
    act = silu * up
    act_low = act.astype(bf16)
    act_ref[0] = act_low
    scale = scale_ref[mine, 0:1]
    plain = times_transposed(grads_ref[mine, :], w_out)
    dw_ref[mine, :] = jnp.broadcast_to(
        jnp.sum(plain * act_low.astype(f32), axis=1, keepdims=True), (CAP, 128)
    ).astype(bf16)
    dact = plain * scale
    dgate = (dact * sig * (1.0 + gate * (1.0 - sig)) * up).astype(bf16)
    dup = (dact * silu).astype(bf16)
    back = times_transposed(jnp.concatenate([dgate, dup], axis=0), w_in)
    lane = lax.broadcasted_iota(jnp.int32, (CAP, 2 * D), 1)
    back_ref[mine, :] = jnp.where(lane % 2 == 0, back[:CAP], back[CAP:]).astype(bf16)
    kept_ref[mine, :] = jnp.concatenate([dgate, dup, (act * scale).astype(bf16)], axis=1)

    @pl.when(expert == EXPERTS - 1)
    def _():
        pairs = (
            lax.broadcasted_iota(jnp.int32, (256, 128), 0) // 2
            == lax.broadcasted_iota(jnp.int32, (256, 128), 1)
        ).astype(bf16)
        size = LEN // blocks
        for block in range(D // 128):
            cols = slice(block * 256, (block + 1) * 256)
            wide_rows = transposed_times(place_ref[...], back_ref[:, cols]).astype(bf16)
            dn = matmul(wide_rows, pairs).astype(bf16)
            for k, ref in enumerate(dn_refs):
                ref[:, block * 128 : (block + 1) * 128] = dn[k * size : (k + 1) * size]
        lanes = lax.broadcasted_iota(jnp.int32, (LEN, 128), 1)
        gates = [transposed_times(ref[...], dw_ref[...]) for ref in (first_ref, second_ref)]
        gates = jnp.where(lanes == 0, gates[0], jnp.where(lanes == 1, gates[1], 0.0)).astype(bf16)
        for k, ref in enumerate(dn_refs):
            ref[:, D:] = gates[k * size : (k + 1) * size]
        moved_ref[...] = matmul(sort_ref[...], kept_ref[...]).astype(bf16)


def experts(blocks, routes, router, normed, grad, w_in, w_out):
    units = w_out.shape[1]
    slots = EXPERTS * CAP
    size = LEN // blocks
    return pl.pallas_call(
        functools.partial(experts_kernel, blocks),
        grid=(EXPERTS,),
        in_specs=[
            whole((2, LEN)),
            whole((EXPERTS, D)),
            pl.BlockSpec((1, D, 2, units), lambda e: (e, 0, 0, 0)),
            pl.BlockSpec((1, units, D), lambda e: (e, 0, 0)),
        ]
        + [whole((size, D))] * (2 * blocks),
        out_specs=(
            whole((2 * LEN, 3 * units)),
            pl.BlockSpec((1, CAP, units), lambda e: (e, 0, 0)),
            whole((slots, LEN)),
        )
        + (whole((size, D + 128)),) * blocks,
        out_shape=(
            shape_of((2 * LEN, 3 * units), bf16),
            shape_of((EXPERTS, CAP, units), bf16),
            shape_of((slots, LEN), bf16),
        )
        + (shape_of((size, D + 128), bf16),) * blocks,
        scratch_shapes=[
            pltpu.VMEM((LEN, D), bf16),
            pltpu.VMEM((LEN, D), bf16),
            pltpu.VMEM((slots, 2 * D), bf16),
            pltpu.VMEM((slots, 2 * D), bf16),
            pltpu.VMEM((slots, D), bf16),
            pltpu.VMEM((slots, LEN), bf16),
            pltpu.VMEM((slots, LEN), bf16),
            pltpu.VMEM((slots, LEN), bf16),
            pltpu.VMEM((slots, 128), f32),
            pltpu.VMEM((slots, 2 * D), bf16),
            pltpu.VMEM((slots, 3 * units), bf16),
            pltpu.VMEM((slots, 128), bf16),
            pltpu.VMEM((2 * LEN, slots), bf16),
        ],
        compiler_params=params(),
        cost_estimate=takes(37),
        name="experts",
    )(routes, router, w_in, w_out, *normed, *grad)


def experts_out_kernel(blocks, act_ref, weighted_ref, w_out_ref, *rest):
    made_refs, ye_ref = rest[-1 - blocks : -1], rest[-1]
    expert = pl.program_id(0)
    mine = pl.ds(pl.multiple_of(expert * CAP, CAP), CAP)
    ye_ref[mine, :] = matmul(act_ref[0], w_out_ref[0]).astype(bf16)

    @pl.when(expert == pl.num_programs(0) - 1)
    def _():
        made = transposed_times(weighted_ref[...], ye_ref[...])
        size = LEN // blocks
        if len(rest) > blocks + 1:
            made = made + jnp.concatenate([ref[...].astype(f32) for ref in rest[:blocks]], axis=0)
        for k, ref in enumerate(made_refs):
            ref[...] = made[k * size : (k + 1) * size].astype(bf16)


def experts_out(blocks, part, parts, act, weighted, w_out, earlier=()):
    units = w_out.shape[1]
    count = EXPERTS // parts
    slots = count * CAP
    rows = whole((LEN // blocks, D))
    return pl.pallas_call(
        functools.partial(experts_out_kernel, blocks),
        grid=(count,),
        in_specs=[
            pl.BlockSpec((1, CAP, units), lambda e: (e + part * count, 0, 0)),
            pl.BlockSpec((slots, LEN), lambda e: (part, 0)),
            pl.BlockSpec((1, units, D), lambda e: (e + part * count, 0, 0)),
        ]
        + [rows] * len(earlier),
        out_specs=(rows,) * blocks,
        out_shape=(shape_of((LEN // blocks, D), bf16),) * blocks,
        scratch_shapes=[pltpu.VMEM((slots, D), bf16)],
        compiler_params=params(),
        cost_estimate=takes(14 / parts),
        name="experts_out",
    )(act, weighted, w_out, *earlier)


def sort_rows(refs, groups, out_ref):
    share = LEN // len(refs)
    for group in range(groups):
        for k, ref in enumerate(refs):
            at = group * LEN + k * share
            out_ref[at : at + share, :] = ref[group * share : (group + 1) * share, :]


def sorted_columns_kernel(groups, *refs):
    column_refs, (left_ref, right_ref, starts_ref, counts_ref, rows_ref) = refs[:-5], refs[-5:]
    width = left_ref.shape[1]
    sort_rows(column_refs, groups, rows_ref)
    ids = lax.broadcasted_iota(jnp.int32, (LEN, EXPERTS), 1).astype(f32)
    earlier = (
        lax.broadcasted_iota(jnp.int32, (LEN, LEN), 1)
        < lax.broadcasted_iota(jnp.int32, (LEN, LEN), 0)
    ).astype(bf16)
    below = (
        lax.broadcasted_iota(jnp.int32, (EXPERTS, EXPERTS), 0)
        < lax.broadcasted_iota(jnp.int32, (EXPERTS, EXPERTS), 1)
    ).astype(f32)
    lane = lax.broadcasted_iota(jnp.int32, (LEN, 2 * LEN), 1).astype(f32)
    all_starts, all_counts = [], []
    for group in range(groups):
        rows = rows_ref[group * LEN : (group + 1) * LEN, :]
        picks = rows[:, 4 * width : 4 * width + 2].astype(f32)
        hot = [(picks[:, k : k + 1] == ids).astype(f32) for k in (0, 1)]
        first = jnp.sum(hot[0], axis=0, keepdims=True)
        counts = first + jnp.sum(hot[1], axis=0, keepdims=True)
        starts = dot_exact(jnp.broadcast_to(counts, (8, EXPERTS)), below)[0:1]
        ranks = [matmul(earlier, hot[0].astype(bf16)), matmul(earlier, hot[1].astype(bf16)) + first]
        place = [jnp.sum(hot[k] * (starts + ranks[k]), axis=1, keepdims=True) for k in (0, 1)]
        move = ((lane == place[0]).astype(f32) + (lane == place[1]).astype(f32)).astype(bf16)
        to = slice(group * 2 * LEN, (group + 1) * 2 * LEN)
        left_ref[to, :] = transposed_times(move, rows[:, :width]).astype(bf16)
        right_ref[to, :] = transposed_times(move, rows[:, width : 2 * width]).astype(bf16)
        all_starts.append(starts)
        all_counts.append(counts)
    starts_ref[...] = jnp.concatenate(all_starts, axis=0).astype(jnp.int32)
    counts_ref[...] = jnp.concatenate(all_counts, axis=0).astype(jnp.int32)


def sorted_columns(groups, columns):
    rows, width = groups * 2 * LEN, D // groups
    table = shape_of((groups, EXPERTS), jnp.int32)
    return pl.pallas_call(
        functools.partial(sorted_columns_kernel, groups),
        grid=(1,),
        in_specs=[whole(item.shape) for item in columns],
        out_specs=(whole((rows, width)),) * 2 + (whole(table.shape),) * 2,
        out_shape=(shape_of((rows, width), bf16),) * 2 + (table,) * 2,
        scratch_shapes=[pltpu.VMEM((groups * LEN, columns[0].shape[1]), bf16)],
        compiler_params=params(),
        cost_estimate=takes(6),
        name="sorted_columns",
    )(*columns)


def expert_grad_kernel(groups, starts_ref, counts_ref, moved_ref, left_ref, right_ref, *rest):
    din_ref, dout_ref = rest
    expert = pl.program_id(0)
    units = moved_ref.shape[1] // 3
    window = CAP + 16
    row = lax.broadcasted_iota(jnp.int32, (window, 1), 0)
    lefts, rights, moves = [], [], []
    for group in range(groups):
        start, count = starts_ref[group, expert], counts_ref[group, expert]
        base = jnp.minimum((start // 16) * 16, 2 * LEN - window)
        keep = jnp.logical_and(row >= start - base, row < start - base + count).astype(bf16)
        rows = pl.ds(pl.multiple_of(group * 2 * LEN + base, 16), window)
        lefts.append(left_ref[rows, :] * keep)
        rights.append(right_ref[rows, :] * keep)
        moves.append(moved_ref[rows, :])
    moved = jnp.concatenate(moves, axis=0)
    din = transposed_times(jnp.concatenate(lefts, axis=0), moved[:, : 2 * units])
    din_ref[0, :, 0, :] = din[:, :units]
    din_ref[0, :, 1, :] = din[:, units:]
    dout_ref[0] = transposed_times(jnp.concatenate(rights, axis=0), moved[:, 2 * units :])


def expert_grads(groups, moved, left, right, starts, counts):
    width = left.shape[1]
    units = moved.shape[1] // 3
    inputs = (moved, left, right)
    return pl.pallas_call(
        functools.partial(expert_grad_kernel, groups),
        grid=(EXPERTS,),
        in_specs=[SMEM, SMEM] + [whole(item.shape) for item in inputs],
        out_specs=(
            pl.BlockSpec((1, width, 2, units), lambda e: (e, 0, 0, 0)),
            pl.BlockSpec((1, width, units), lambda e: (e, 0, 0)),
        ),
        out_shape=(
            shape_of((EXPERTS, width, 2, units)),
            shape_of((EXPERTS, width, units)),
        ),
        compiler_params=params(),
        cost_estimate=takes(12),
        name="expert_grads",
    )(starts, counts, *inputs)


def pack_columns_kernel(groups, lanes, *refs):
    in_refs, out_ref = refs[:-1], refs[-1]
    width = D // groups
    values = [ref[...].astype(f32) for ref in in_refs]
    rows = values[0].shape[0]
    for group in range(groups):
        parts = [
            value[:, group * width : (group + 1) * width] if value.shape[1] == D else value
            for value in values
        ]
        spare = lanes - sum(part.shape[1] for part in parts)
        if spare:
            parts.append(jnp.zeros((rows, spare), f32))
        whole_row = jnp.concatenate(parts, axis=1) if len(parts) > 1 else parts[0]
        out_ref[group] = whole_row.astype(bf16)


def pack_columns(groups, *values):
    width, rows = D // groups, values[0].shape[0]
    lanes = sum(width if value.shape[1] == D else value.shape[1] for value in values)
    if len(values) > 1:
        lanes += -lanes % 128
    return pl.pallas_call(
        functools.partial(pack_columns_kernel, groups, lanes),
        grid=(1,),
        in_specs=[whole(value.shape) for value in values],
        out_specs=whole((groups, rows, lanes)),
        out_shape=shape_of((groups, rows, lanes), bf16),
        compiler_params=params(),
        cost_estimate=takes(3),
        name="pack_columns",
    )(*values)


def mix_grad_kernel(groups, normed_ref, first_ref, second_ref, *refs):
    extra_refs, out_ref = refs[:-1], refs[-1]
    width = D // groups
    grads = [
        transposed_times(normed_ref[...], ref[...]).astype(bf16) for ref in (first_ref, second_ref)
    ]
    channels = grads[0].shape[1]
    share = channels // groups
    extras = [ref[...] for ref in extra_refs]
    tall = [extra for extra in extras if extra.shape[0] > STATE]
    flat = [extra for extra in extras if extra.shape[0] <= STATE]
    for group in range(groups):
        at = 0
        for grad in grads:
            out_ref[group, at : at + width, :] = grad[group * width : (group + 1) * width]
            at += width
        rows = [
            extra[group * (extra.shape[0] // groups) : (group + 1) * (extra.shape[0] // groups)]
            for extra in tall
        ]
        line = jnp.concatenate(
            [
                extra[row : row + 1, group * share : (group + 1) * share]
                for extra in flat
                for row in range(extra.shape[0])
            ],
            axis=1,
        )
        spare = -line.shape[1] % channels
        line = jnp.concatenate([line, jnp.zeros((1, spare), f32)], axis=1)
        for first in range(0, line.shape[1], channels):
            rows.append(line[:, first : first + channels])
        spare = out_ref.shape[1] - at - sum(row.shape[0] for row in rows)
        if spare:
            rows.append(jnp.zeros((spare, channels), f32))
        out_ref[group, at:, :] = jnp.concatenate(rows, axis=0).astype(bf16)


def mix_grads(groups, normed, first, second, *extras):
    channels = first.shape[1]
    rows = sum(extra.shape[0] // groups for extra in extras if extra.shape[0] > STATE)
    lines = sum(extra.shape[0] for extra in extras if extra.shape[0] <= STATE)
    rows += -(-lines // groups)
    rows += -rows % 16 + 2 * (D // groups)
    return pl.pallas_call(
        functools.partial(mix_grad_kernel, groups),
        grid=(1,),
        in_specs=[whole(item.shape) for item in (normed, first, second) + extras],
        out_specs=whole((groups, rows, channels)),
        out_shape=shape_of((groups, rows, channels), bf16),
        compiler_params=params(),
        cost_estimate=takes(7),
        name="mix_grads",
    )(normed, first, second, *extras)


def unpack_mix_kernel(groups, sum_ref, mix_ref, xproj_ref, dt_ref, flat_ref):
    width = D // groups
    channels = sum_ref.shape[1]
    for half in (0, 1):
        mix_ref[:, half, :] = sum_ref[half * width : (half + 1) * width, :].astype(f32)
    small = sum_ref[2 * width :, :].astype(f32)
    at, count = xproj_ref.shape[0], dt_ref.shape[0]
    xproj_ref[...] = small[:at]
    dt_ref[...] = small[at : at + count]
    share = channels // groups
    for line in range(flat_ref.shape[0]):
        row, first = divmod(line * share, channels)
        flat_ref[line : line + 1, :] = small[at + count + row : at + count + row + 1, first : first + share]


def unpack_mix(groups, total):
    width, channels = D // groups, total.shape[1]
    shapes = (
        (width, 2, channels),
        (128 // groups, channels),
        (DT_RANK // groups, channels),
        (STATE + 2 + CONV, channels // groups),
    )
    return pl.pallas_call(
        functools.partial(unpack_mix_kernel, groups),
        grid=(1,),
        in_specs=[whole(total.shape)],
        out_specs=tuple(whole(shape) for shape in shapes),
        out_shape=tuple(shape_of(shape) for shape in shapes),
        compiler_params=params(),
        cost_estimate=takes(3),
        name="unpack_mix",
    )(total)


def out_grad_kernel(groups, first, heads_ref, acted_ref, *rest):
    column_refs, out_refs, rows_ref = rest[:-3], rest[-3:-1], rest[-1]
    width = out_refs[0].shape[0]
    sort_rows(column_refs, groups, rows_ref)
    for k, (left_ref, out_ref) in enumerate(zip((heads_ref, acted_ref), out_refs)):
        columns = rows_ref[:, (first + k) * width : (first + k + 1) * width]
        out_ref[...] = transposed_times(columns, left_ref[...])


def out_grads(groups, first, columns, heads, acted):
    width = D // groups
    lefts = (heads, acted)
    return pl.pallas_call(
        functools.partial(out_grad_kernel, groups, first),
        grid=(1,),
        in_specs=[whole(item.shape) for item in lefts + tuple(columns)],
        out_specs=tuple(whole((width, item.shape[1])) for item in lefts),
        out_shape=tuple(shape_of((width, item.shape[1])) for item in lefts),
        scratch_shapes=[pltpu.VMEM((groups * LEN, columns[0].shape[1]), bf16)],
        compiler_params=params(),
        cost_estimate=takes(6),
        name="out_grads",
    )(*lefts, *columns)


def last_grad_kernel(groups, gated_ref, *rest):
    column_refs, (out_ref, sums_ref, rows_ref) = rest[:-3], rest[-3:]
    share = LEN // len(column_refs)
    stride = column_refs[0].shape[0] // groups
    sums = jnp.zeros(sums_ref.shape, f32)
    for group in range(groups):
        for k, ref in enumerate(column_refs):
            at = group * LEN + k * share
            first = group * stride
            rows_ref[at : at + share, :] = ref[first : first + share, :]
            sums = sums + ref[first + share : first + stride, :].astype(f32)
    sums_ref[...] = sums
    out_ref[...] = transposed_times(rows_ref[...], gated_ref[...])


def last_grads(groups, columns, gated):
    width = D // groups
    extra = columns[0].shape[0] // groups - LEN // len(columns)
    shapes = ((width, gated.shape[1]), (extra, width))
    return pl.pallas_call(
        functools.partial(last_grad_kernel, groups),
        grid=(1,),
        in_specs=[whole(gated.shape)] + [whole(item.shape) for item in columns],
        out_specs=tuple(whole(shape) for shape in shapes),
        out_shape=tuple(shape_of(shape) for shape in shapes),
        scratch_shapes=[pltpu.VMEM((groups * LEN, width), bf16)],
        compiler_params=params(),
        cost_estimate=takes(5),
        name="last_grads",
    )(gated, *columns)


def shards(
    tokens,
    cotangent,
    norm_gains,
    mix_in,
    conv_weight,
    x_proj,
    dt_proj,
    dt_bias,
    a_log,
    skip_gain,
    mix_out,
    ffn_in,
    ffn_out,
    attn_query,
    attn_keyval,
    attn_out,
    router,
    expert_in,
    expert_out,
    routes,
):
    members = lax.axis_size("tensor")
    member = lax.axis_index("tensor")
    share = LEN // members
    groups = lax.axis_size("dp")
    gains = norm_gains.astype(f32)
    me = member.astype(jnp.int32).reshape(1)

    def swap(value, k):
        return lax.ppermute(value, "tensor", [(i, i ^ k) for i in range(members)])

    def join_list(rows):
        return [rows] + [swap(rows, k) for k in range(1, members)]

    def join(rows):
        return jnp.concatenate(join_list(rows), axis=0)

    def split_list(blocks):
        return [blocks[0]] + [swap(blocks[k], k) for k in range(1, members)]

    def blocks_of(partial):
        return [partial[k * share : (k + 1) * share].astype(bf16) for k in range(members)]

    def all_sum(partial):
        total = partial.astype(f32)
        for k in range(1, members):
            total = total + swap(partial, k).astype(f32)
        return total

    def all_sum_rows(partial):
        total = partial.astype(f32)
        for k in range(1, members):
            blocks = swap(partial, k).reshape(members, share, -1)
            ordered = jnp.concatenate([blocks[j ^ k] for j in range(members)], axis=0)
            total = total + ordered.astype(f32)
        return total

    def dp_scatter(value):
        return lax.psum_scatter(value, "dp", scatter_dimension=0, tiled=True)

    def dp_gather(value):
        return lax.all_gather(value, "dp", axis=0, tiled=True)

    def to_columns(*rows):
        came = lax.all_to_all(pack_columns(groups, *rows), "dp", 0, 0, tiled=True)
        return came.reshape(-1, came.shape[2])

    def hold(value, *others):
        return lax.optimization_barrier((value,) + others)[0]

    def gain(index):
        return gains[index : index + 1]

    hidden1, rows1 = norm_forward(tokens, gain(0), [])
    normed1 = join(rows1)
    channels = mix_in.shape[2]
    bias, skip = dt_bias.reshape(1, channels), skip_gain.reshape(1, channels)
    alog = a_log.T
    xz = jnp.einsum("td,dgc->gtc", normed1, mix_in, preferred_element_type=f32)
    u, proj_part = conv_forward(me, members, xz, conv_weight, x_proj)
    proj = all_sum_rows(proj_part)
    gated_low, ys, states, *mixed = scan_forward(
        me, members, proj, dt_proj, bias, alog, skip, u, xz, mix_out
    )
    all_gated = dp_gather(gated_low)
    hidden2, rows2 = norm_forward(hidden1, gain(1), split_list(mixed))
    normed2 = join(rows2)
    gate_up = jnp.einsum("td,dgc->gtc", normed2, ffn_in, preferred_element_type=f32)
    ffn_gate = sigmoid(gate_up[0])
    acted_low = (gate_up[0] * ffn_gate * gate_up[1]).astype(bf16)
    all_acted = dp_gather(acted_low)
    hidden3, rows3 = norm_forward(
        hidden2, gain(2), split_list(blocks_of(matmul(acted_low, ffn_out)))
    )
    keyval = attn_keyval.reshape(D, -1)
    rows3 = join_list(rows3)
    rows3[0] = hold(rows3[0], all_gated)
    normed3, query_low, keyval_low, attended_low, *attended = attention_forward(
        me, members, rows3, attn_query, keyval, attn_out
    )
    all_attended = dp_gather(attended_low)
    hidden4, rows4 = norm_forward(hidden3, gain(3), split_list(attended))
    normed4 = join_list(rows4)

    at = jnp.bitwise_xor(jnp.arange(members, dtype=jnp.int32), member)
    picks = routes.reshape(members, share, 2)[at].reshape(LEN, 2)
    own_picks = picks[:share]
    router_rows = router.T
    moved, expert_low, slot_weights, *dn_part = experts(
        members, picks.T, router_rows, normed4, join_list(cotangent), expert_in, expert_out
    )
    dn_part[0] = hold(dn_part[0], all_acted, all_attended)
    all_moved = dp_gather(moved)
    dn_part = split_list(dn_part)
    made = experts_out(members, 0, 2, expert_low, slot_weights, expert_out)
    dn_part[0] = hold(dn_part[0], made[0])
    grad, low4, gain4, grad_router = router_backward(
        cotangent, hidden4, gain(3), rows4, own_picks, router_rows, dn_part
    )
    grad_low4 = join_list(low4)

    width = D // groups
    units = expert_out.shape[1]

    dqkv, *dnormed = attention_backward(
        me, members, grad_low4, query_low, keyval_low, attn_query, keyval, attn_out
    )
    dn_blocks = split_list(dnormed)
    made = [hold(made[0], dn_blocks[0])] + list(made[1:])
    made = experts_out(members, 1, 2, expert_low, slot_weights, expert_out, made)
    attn_in_part = transposed_times(normed3, dqkv).astype(bf16)
    attn_in_sum = dp_scatter(attn_in_part)
    grad, low3, gain3 = norm_backward(
        hold(grad, attn_in_part, made[0]), hidden3, gain(2), dn_blocks
    )
    grad_low3 = join(low3)

    dact = times_transposed(grad_low3, ffn_out)
    dgate_up = jnp.concatenate(
        [
            dact * ffn_gate * (1.0 + gate_up[0] * (1.0 - ffn_gate)) * gate_up[1],
            dact * gate_up[0] * ffn_gate,
        ],
        axis=1,
    ).astype(bf16)
    hidden_units = ffn_in.shape[2]
    dnormed = jnp.einsum(
        "tgc,dgc->td",
        dgate_up.reshape(LEN, 2, hidden_units),
        ffn_in,
        preferred_element_type=f32,
    )
    dn_blocks = blocks_of(dnormed)
    ffn_in_part = transposed_times(normed2, hold(dgate_up, dn_blocks[0])).astype(bf16)
    ffn_in_sum = dp_scatter(ffn_in_part)
    columns = to_columns(
        hold(rows4, dn_blocks[0]), cotangent, low4, low3, own_picks.astype(f32)
    )
    grad, low2, gain2 = norm_backward(
        hold(grad, ffn_in_part, all_moved),
        hidden2,
        gain(1),
        split_list(dn_blocks),
    )
    grad_low2 = join_list(low2)

    du, dzs, small, dalog, ddt, dcols_part = scan_backward(
        me, members, proj, dt_proj, bias, alog, skip, u, xz, mix_out, grad_low2, ys, states
    )
    dcols = all_sum_rows(dcols_part.astype(bf16))
    dcols = hold(dcols, attn_in_sum, columns)
    columns = join_list(hold(columns, dcols))
    dxs, dxproj, dconv = conv_backward(
        me, members, dcols, proj, u, xz, du, conv_weight, x_proj
    )
    dmixed = jnp.stack([dxs, dzs])
    dnormed = jnp.einsum("gtc,dgc->td", dmixed, mix_in, preferred_element_type=f32)
    dn_blocks = blocks_of(dnormed)
    mix_part = mix_grads(
        groups, normed1, hold(dxs, dn_blocks[0]), dzs, dxproj, ddt, dalog, small[:2], dconv
    )
    mix_sum = dp_scatter(mix_part.reshape(-1, channels))
    dn_blocks = split_list(dn_blocks)
    dn_blocks[0] = hold(dn_blocks[0], mix_part)
    grad, _, gain1 = norm_backward(grad, hidden1, gain(0), dn_blocks)

    extra = jnp.concatenate([gain1, gain2, gain3, gain4, grad_router], axis=0).astype(bf16)
    extra = jnp.pad(extra, ((0, -extra.shape[0] % 16), (0, 0)))
    last = to_columns(jnp.concatenate([low2, extra], axis=0))
    sorted_rows = sorted_columns(groups, [hold(columns[0], grad, ffn_in_sum)] + columns[1:])
    expert_in_grad, expert_out_grad = expert_grads(groups, all_moved, *sorted_rows)
    made = split_list([hold(made[0], expert_out_grad)] + list(made[1:]))
    hidden5 = hidden4
    for block in made:
        hidden5 = hidden5 + block.astype(f32)
    last = join_list(hold(last, expert_out_grad))
    columns[0] = hold(columns[0], expert_out_grad)
    attn_out_sum, ffn_out_sum = out_grads(groups, 2, columns, all_attended, all_acted)
    last[0] = hold(last[0], ffn_out_sum, hidden5)
    mix_out_sum, model_sum = last_grads(groups, last, all_gated)

    mix_in_grad, xproj_grad, dt_grad, flat = unpack_mix(groups, mix_sum)
    heads_cols = attn_query.shape[1]
    attn_in = attn_in_sum.astype(f32)
    return (
        hidden5.astype(bf16),
        grad,
        model_sum[:4],
        mix_in_grad,
        flat[STATE + 2 :],
        xproj_grad.T,
        dt_grad,
        flat[STATE],
        flat[:STATE].T,
        flat[STATE + 1],
        mix_out_sum.T,
        ffn_in_sum.astype(f32).reshape(width, 2, hidden_units),
        ffn_out_sum.T,
        attn_in[:, :heads_cols],
        attn_in[:, heads_cols:].reshape(-1, 2, attn_keyval.shape[2]),
        attn_out_sum.T,
        model_sum[4 : 4 + EXPERTS].T,
        expert_in_grad,
        expert_out_grad.transpose(0, 2, 1),
    )


def solution(mesh):
    return jax.shard_map(
        shards,
        mesh=mesh,
        in_specs=(
            P(("dp", "tensor"), None),
            P(("dp", "tensor"), None),
            P(),
            P(None, None, "tensor"),
            P(None, "tensor"),
            P("tensor", None),
            P(None, "tensor"),
            P("tensor"),
            P("tensor", None),
            P("tensor"),
            P("tensor", None),
            P(None, None, "tensor"),
            P("tensor", None),
            P(None, "tensor"),
            P(None, None, "tensor"),
            P("tensor", None),
            P(),
            P(None, None, None, "tensor"),
            P(None, "tensor", None),
            P("dp", None),
        ),
        out_specs=(
            P(("dp", "tensor"), None),
            P(("dp", "tensor"), None),
            P(None, "dp"),
            P("dp", None, "tensor"),
            P(None, ("tensor", "dp")),
            P("tensor", "dp"),
            P("dp", "tensor"),
            P(("tensor", "dp")),
            P(("tensor", "dp"), None),
            P(("tensor", "dp")),
            P("tensor", "dp"),
            P("dp", None, "tensor"),
            P("tensor", "dp"),
            P("dp", "tensor"),
            P("dp", None, "tensor"),
            P("tensor", "dp"),
            P("dp", None),
            P(None, "dp", None, "tensor"),
            P(None, "tensor", "dp"),
        ),
        check_vma=False,
    )
```

```python
import functools
import math

import jax
import jax.numpy as jnp
from jax import lax
from jax.experimental import pallas as pl
from jax.experimental.pallas import tpu as pltpu
from jax.sharding import PartitionSpec as P

D = 1536
STATE = 16
CONV = 4
DT_RANK = 96
HEADS = 24
KV_HEADS = 8
HEAD_DIM = 64
EXPERTS = 16
LEN = 256
CAP = 48

epsilon = 1e-06
floor_square = 0.1
masked_score = -1e30
LOG2E = 1.4426950408889634
PAD = 8
CHUNK = 16
GROUP = 16
SIDE = 2
VMEM_LIMIT = 56 * 1024 * 1024

f32 = jnp.float32
bf16 = jnp.bfloat16


def matmul(left, right):
    return jnp.dot(left, right, preferred_element_type=f32)


def times_transposed(left, right):
    return lax.dot_general(left, right, (((1,), (1,)), ((), ())), preferred_element_type=f32)


def transposed_times(left, right):
    return lax.dot_general(left, right, (((0,), (0,)), ((), ())), preferred_element_type=f32)


def sigmoid(v):
    return 1.0 / (1.0 + jnp.exp(-v))


def dot_exact(left, right):
    return jnp.dot(left, right, precision=lax.Precision.HIGHEST, preferred_element_type=f32)


def column_norm_parts(projected):
    lane = lax.broadcasted_iota(jnp.int32, projected.shape, 1)
    square = projected * projected
    in_step = lane < DT_RANK
    in_b = jnp.logical_and(lane >= DT_RANK, lane < DT_RANK + STATE)
    in_c = lane >= DT_RANK + STATE
    mean_step = jnp.sum(jnp.where(in_step, square, 0.0), axis=1, keepdims=True) / DT_RANK
    mean_b = jnp.sum(jnp.where(in_b, square, 0.0), axis=1, keepdims=True) / STATE
    mean_c = jnp.sum(jnp.where(in_c, square, 0.0), axis=1, keepdims=True) / STATE
    r_step = lax.rsqrt(mean_step + epsilon)
    r_b = lax.rsqrt(jnp.maximum(mean_b, floor_square))
    r_c = lax.rsqrt(jnp.maximum(mean_c, floor_square))
    scale = jnp.where(in_step, r_step, jnp.where(in_b, r_b, r_c))
    return scale, in_step, in_b, in_c, mean_b, mean_c


def row_spread(cols_ref, first, out_ref):
    pick = (
        lax.broadcasted_iota(jnp.int32, (128, CHUNK * STATE), 0) - first
        == lax.broadcasted_iota(jnp.int32, (128, CHUNK * STATE), 1) % STATE
    ).astype(f32)
    out_ref[...] = (dot_exact(cols_ref[...], pick) * chunk_mask(LEN)).astype(bf16)


def chunk_mask(rows):
    return (
        lax.broadcasted_iota(jnp.int32, (rows, CHUNK * STATE), 0) % CHUNK
        == lax.broadcasted_iota(jnp.int32, (rows, CHUNK * STATE), 1) // STATE
    ).astype(f32)


def conv_total(pad_ref, weight_ref, length):
    total = weight_ref[0:1, :] * pad_ref[pl.ds(PAD - CONV + 1, length), :]
    for tap in range(1, CONV):
        total = total + weight_ref[tap : tap + 1, :] * pad_ref[pl.ds(PAD - CONV + 1 + tap, length), :]
    return total


def conv_forward_kernel(blocks, me_ref, xz_ref, weight_ref, xproj_ref, u_ref, proj_ref, pad_ref):
    me = me_ref[0]
    size = LEN // blocks
    pad_ref[0:PAD, :] = jnp.zeros((PAD, pad_ref.shape[1]), f32)
    for m in range(blocks):
        at = pl.multiple_of(jnp.bitwise_xor(me, m) * size, size)
        pad_ref[PAD + m * size : PAD + (m + 1) * size, :] = xz_ref[0, pl.ds(at, size), :]
    total = conv_total(pad_ref, weight_ref, LEN)
    u = total * sigmoid(total)
    for m in range(blocks):
        at = pl.multiple_of(jnp.bitwise_xor(me, m) * size, size)
        u_ref[pl.ds(at, size), :] = u[m * size : (m + 1) * size, :]
    proj_ref[...] = matmul(u_ref[...].astype(bf16), xproj_ref[...]).astype(bf16)


def scan_setup(proj_ref, cols_ref, b_ref, c_ref):
    projected = proj_ref[...]
    scale = column_norm_parts(projected)[0]
    cols_ref[...] = projected * scale
    row_spread(cols_ref, DT_RANK, b_ref)
    row_spread(cols_ref, DT_RANK + STATE, c_ref)


def step_sizes(cols_ref, dt_proj_ref, bias_ref):
    low = cols_ref[:, :DT_RANK].astype(bf16)
    pre = matmul(low, dt_proj_ref[...]) + bias_ref[...]
    return low, pre, jnp.maximum(pre, 0.0) + jnp.log1p(jnp.exp(-jnp.abs(pre)))


def chunk_place(index, me, size):
    block = index // (size // CHUNK)
    inner = index % (size // CHUNK)
    return pl.multiple_of(jnp.bitwise_xor(block, me) * size + inner * CHUNK, CHUNK)


def chunk_group(index):
    out = []
    for q in range(GROUP):
        base = (index * GROUP + q) * CHUNK
        out.append(
            (
                pl.ds(pl.multiple_of(base, CHUNK), CHUNK),
                pl.ds(pl.multiple_of(base * STATE, CHUNK * STATE), CHUNK * STATE),
            )
        )
    return out


def push_chunks(left_ref, right_ref, out_ref):
    def body(index, carry):
        for rows, many in chunk_group(index):
            out_ref[many, :] = transposed_times(left_ref[rows, :], right_ref[rows, :])
        return carry

    lax.fori_loop(0, LEN // CHUNK // GROUP, body, 0)


def scan_forward_kernel(
    blocks,
    me_ref,
    proj_ref,
    dt_proj_ref,
    bias_ref,
    alog_ref,
    skip_ref,
    u_ref,
    xz_ref,
    out_w_ref,
    gated_ref,
    ys_ref,
    states_ref,
    *rest,
):
    out_refs = rest[:blocks]
    cols_ref, b_ref, c_ref, delta_ref, drive_ref, push_ref, kept_ref, sems = rest[blocks:]
    me = me_ref[0]
    size = LEN // blocks
    lanes = u_ref.shape[1]
    scan_setup(proj_ref, cols_ref, b_ref, c_ref)

    _, _, delta = step_sizes(cols_ref, dt_proj_ref, bias_ref)
    delta_ref[...] = delta
    drive_ref[...] = (delta * u_ref[...]).astype(bf16)
    rate = -jnp.exp(alog_ref[...]) * LOG2E
    push_chunks(b_ref, drive_ref, push_ref)

    def chunk(index, state):
        base = chunk_place(index, me, size)
        steps = delta_ref[pl.ds(base, CHUNK), :]
        for j in range(CHUNK):
            at = pl.ds(pl.multiple_of((base + j) * STATE, STATE), STATE)
            state = jnp.exp2(steps[j : j + 1, :] * rate) * state + push_ref[at, :]
            kept_ref[at, :] = state.astype(bf16)
        return state

    state = jnp.zeros((STATE, lanes), f32)
    copies = []
    per = size // CHUNK
    for block in range(blocks):
        state = lax.fori_loop(block * per, (block + 1) * per, chunk, state)
        copies.append(states_copy(kept_ref, states_ref, sems, block, me, size))
        copies[-1].start()

    def output(index, carry):
        for rows, many in chunk_group(index):
            ys_ref[rows, :] = matmul(c_ref[rows, :], kept_ref[many, :])
        return carry

    lax.fori_loop(0, LEN // CHUNK // GROUP, output, 0)
    ys = ys_ref[...] + skip_ref[...] * u_ref[...]
    ys_ref[...] = ys
    zs = xz_ref[0]
    gated = (ys * (zs * sigmoid(zs))).astype(bf16)
    gated_ref[...] = gated
    store_blocks(out_refs, matmul(gated, out_w_ref[...]))
    for copy in copies:
        copy.wait()


def states_copy(from_ref, to_ref, sems, block, me, size):
    many = size * STATE
    rows = pl.ds(pl.multiple_of(jnp.bitwise_xor(me, block) * many, many), many)
    return pltpu.make_async_copy(from_ref.at[rows, :], to_ref.at[rows, :], sems.at[block])


def scan_backward_kernel(
    blocks,
    me_ref,
    proj_ref,
    dt_proj_ref,
    bias_ref,
    alog_ref,
    skip_ref,
    u_ref,
    xz_ref,
    out_w_ref,
    ys_ref,
    stored_ref,
    *rest,
):
    grad_refs = rest[:blocks]
    (
        du_ref,
        dzs_ref,
        small_ref,
        dalog_ref,
        ddt_ref,
        dcols_ref,
        grad_ref,
        cols_ref,
        b_ref,
        c_ref,
        pb_ref,
        pc_ref,
        delta_ref,
        drive_ref,
        dys_ref,
        ddrive_ref,
        drate_ref,
        dlow_ref,
        push_ref,
        grads_ref,
        rates_ref,
        states_ref,
        sems,
    ) = rest[blocks:]
    me = me_ref[0]
    size = LEN // blocks
    lanes = u_ref.shape[1]
    copies = [
        states_copy(stored_ref, states_ref, sems, block, me, size) for block in range(blocks)
    ]
    for copy in copies:
        copy.start()
    scan_setup(proj_ref, cols_ref, b_ref, c_ref)
    join_blocks(grad_refs, grad_ref)

    low, pre, delta = step_sizes(cols_ref, dt_proj_ref, bias_ref)
    u = u_ref[...]
    delta_ref[...] = delta
    drive_ref[...] = (delta * u).astype(bf16)
    dgated = times_transposed(grad_ref[...], out_w_ref[...])
    zs = xz_ref[0]
    gate = sigmoid(zs)
    dys = dgated * (zs * gate)
    dys_ref[...] = dys.astype(bf16)
    dzs_ref[...] = (dgated * ys_ref[...] * (gate * (1.0 + zs * (1.0 - gate)))).astype(bf16)
    a_matrix = -jnp.exp(alog_ref[...])
    rate = a_matrix * LOG2E
    chunks = LEN // CHUNK
    mask = chunk_mask(CHUNK)
    push_chunks(c_ref, dys_ref, push_ref)

    def chunk(step_index, carry):
        adjoint, da = carry
        index = chunks - 1 - step_index
        base = chunk_place(index, me, size)
        before = chunk_place(jnp.maximum(index - 1, 0), me, size)
        first = (index > 0).astype(f32)
        steps = delta_ref[pl.ds(base, CHUNK), :]
        for j in range(CHUNK - 1, -1, -1):
            at = pl.ds(pl.multiple_of((base + j) * STATE, STATE), STATE)
            if j > 0:
                last = (base + j - 1) * STATE
                earlier = states_ref[pl.ds(pl.multiple_of(last, STATE), STATE), :].astype(f32)
            else:
                last = (before + CHUNK - 1) * STATE
                earlier = states_ref[pl.ds(pl.multiple_of(last, STATE), STATE), :].astype(f32) * first
            grad = adjoint + push_ref[at, :]
            grads_ref[at, :] = grad.astype(bf16)
            adjoint = grad * jnp.exp2(steps[j : j + 1, :] * rate)
            through = adjoint * earlier
            rates_ref[at, :] = (through * a_matrix).astype(bf16)
            da = da + through * steps[j : j + 1, :]
        return adjoint, da

    for copy in copies:
        copy.wait()
    zero = jnp.zeros((STATE, lanes), f32)
    _, da = lax.fori_loop(0, chunks, chunk, (zero, zero))
    mask_low = mask.astype(bf16)

    def output(index, carry):
        for rows, many in chunk_group(index):
            grads = grads_ref[many, :]
            ddrive_ref[rows, :] = matmul(b_ref[rows, :], grads)
            drate_ref[rows, :] = matmul(mask_low, rates_ref[many, :])
            pb_ref[rows, :] = times_transposed(drive_ref[rows, :], grads) * mask
            pc_ref[rows, :] = times_transposed(dys_ref[rows, :], states_ref[many, :]) * mask
        return carry

    lax.fori_loop(0, chunks // GROUP, output, 0)
    dalog_ref[...] = da * a_matrix
    ddrive = ddrive_ref[...]
    du_ref[...] = ddrive * delta + skip_ref[...] * dys
    dpre = (ddrive * u + drate_ref[...]) * sigmoid(pre)
    dpre_low = dpre.astype(bf16)
    small_ref[...] = jnp.concatenate(
        [
            jnp.sum(dpre, axis=0, keepdims=True),
            jnp.sum(dys * u, axis=0, keepdims=True),
            jnp.zeros((6, lanes), f32),
        ],
        axis=0,
    )
    ddt_ref[...] = transposed_times(low, dpre_low)
    dlow_ref[...] = times_transposed(dpre_low, dt_proj_ref[...])
    collect = (
        lax.broadcasted_iota(jnp.int32, (CHUNK * STATE, STATE), 0) % STATE
        == lax.broadcasted_iota(jnp.int32, (CHUNK * STATE, STATE), 1)
    ).astype(f32)
    dcols_ref[...] = jnp.concatenate(
        [dlow_ref[...], dot_exact(pb_ref[...], collect), dot_exact(pc_ref[...], collect)], axis=1
    )


def conv_backward_kernel(
    blocks,
    me_ref,
    dcols_ref,
    proj_ref,
    u_ref,
    xz_ref,
    du_ref,
    weight_ref,
    xproj_ref,
    dxs_ref,
    dxproj_ref,
    dweight_ref,
    pad_ref,
    grad_ref,
):
    me = me_ref[0]
    size = LEN // blocks
    lanes = u_ref.shape[1]
    projected = proj_ref[...]
    scale, in_step, in_b, in_c, mean_b, mean_c = column_norm_parts(projected)
    normed = projected * scale
    dcols = dcols_ref[...]
    product = dcols * normed
    dot_step = jnp.sum(jnp.where(in_step, product, 0.0), axis=1, keepdims=True) / DT_RANK
    dot_b = jnp.sum(jnp.where(in_b, product, 0.0), axis=1, keepdims=True) / STATE
    dot_c = jnp.sum(jnp.where(in_c, product, 0.0), axis=1, keepdims=True) / STATE
    dot_b = jnp.where(mean_b > floor_square, dot_b, 0.0)
    dot_c = jnp.where(mean_c > floor_square, dot_c, 0.0)
    mean = jnp.where(in_step, dot_step, jnp.where(in_b, dot_b, dot_c))
    dproj = (scale * (dcols - normed * mean)).astype(bf16)
    dxproj_ref[...] = transposed_times(dproj, u_ref[...].astype(bf16))
    du = du_ref[...] + times_transposed(dproj, xproj_ref[...])
    pad_ref[0:PAD, :] = jnp.zeros((PAD, lanes), f32)
    grad_ref[LEN : LEN + PAD, :] = jnp.zeros((PAD, lanes), f32)
    for m in range(blocks):
        at = pl.multiple_of(jnp.bitwise_xor(me, m) * size, size)
        pad_ref[PAD + m * size : PAD + (m + 1) * size, :] = xz_ref[0, pl.ds(at, size), :]
    dxs_ref[...] = du.astype(bf16)
    du_ref_rows = []
    grad_ref[0:LEN, :] = du
    total = conv_total(pad_ref, weight_ref, LEN)
    gate = sigmoid(total)
    slope = gate * (1.0 + total * (1.0 - gate))
    for m in range(blocks):
        at = pl.multiple_of(jnp.bitwise_xor(me, m) * size, size)
        du_ref_rows.append(grad_ref[pl.ds(at, size), :])
    grad_ref[0:LEN, :] = jnp.concatenate(du_ref_rows, axis=0) * slope
    dcv = grad_ref[0:LEN, :]
    dweight_ref[...] = jnp.concatenate(
        [
            jnp.sum(dcv * pad_ref[pl.ds(PAD - CONV + 1 + tap, LEN), :], axis=0, keepdims=True)
            for tap in range(CONV)
        ],
        axis=0,
    )
    dxs = weight_ref[CONV - 1 : CONV, :] * dcv
    for tap in range(CONV - 1):
        dxs = dxs + weight_ref[tap : tap + 1, :] * grad_ref[pl.ds(CONV - 1 - tap, LEN), :]
    dxs = dxs.astype(bf16)
    for m in range(blocks):
        at = pl.multiple_of(jnp.bitwise_xor(me, m) * size, size)
        dxs_ref[pl.ds(at, size), :] = dxs[m * size : (m + 1) * size, :]


def store_blocks(refs, value):
    size = value.shape[0] // len(refs)
    for k, ref in enumerate(refs):
        ref[...] = value[k * size : (k + 1) * size].astype(ref.dtype)


def join_blocks(refs, out_ref):
    size = out_ref.shape[0] // len(refs)
    for k, ref in enumerate(refs):
        out_ref[k * size : (k + 1) * size, :] = ref[...]


SMEM = pl.BlockSpec(memory_space=pltpu.SMEM)


def whole(shape):
    return pl.BlockSpec(shape, lambda *_: (0,) * len(shape))


def params():
    return pltpu.CompilerParams(vmem_limit_bytes=VMEM_LIMIT)


def takes(microseconds):
    return pl.CostEstimate(
        flops=int(microseconds * 1.15e9), bytes_accessed=1 << 20, transcendentals=0
    )


def shape_of(shape, dtype=f32):
    return jax.ShapeDtypeStruct(shape, dtype)


def conv_forward(me, blocks, xz, weight, x_proj):
    channels = xz.shape[2]
    return pl.pallas_call(
        functools.partial(conv_forward_kernel, blocks),
        grid=(1,),
        in_specs=[
            SMEM,
            pl.BlockSpec((1, LEN, channels), lambda i: (0, 0, 0)),
            whole(weight.shape),
            whole(x_proj.shape),
        ],
        out_specs=(whole((LEN, channels)), whole((LEN, 128))),
        out_shape=(shape_of((LEN, channels)), shape_of((LEN, 128), bf16)),
        scratch_shapes=[pltpu.VMEM((LEN + PAD, channels), f32)],
        compiler_params=params(),
        cost_estimate=takes(3),
        name="conv_forward",
    )(me, xz, weight, x_proj)


def lane_block(channels):
    return channels


def scan_forward(me, blocks, proj, dt_proj, bias, alog, skip, u, xz, out_w):
    channels = u.shape[1]
    lanes = lane_block(channels)
    col = lambda i: (0, i)
    return pl.pallas_call(
        functools.partial(scan_forward_kernel, blocks),
        grid=(channels // lanes,),
        in_specs=[
            SMEM,
            whole((LEN, 128)),
            pl.BlockSpec((DT_RANK, lanes), col),
            pl.BlockSpec((1, lanes), col),
            pl.BlockSpec((STATE, lanes), col),
            pl.BlockSpec((1, lanes), col),
            pl.BlockSpec((LEN, lanes), col),
            pl.BlockSpec((1, LEN, lanes), lambda i: (1, 0, i)),
            pl.BlockSpec((lanes, D), lambda i: (i, 0)),
        ],
        out_specs=(
            pl.BlockSpec((LEN, lanes), col),
            pl.BlockSpec((LEN, lanes), col),
            pl.BlockSpec(memory_space=pl.ANY),
        )
        + (whole((LEN // blocks, D)),) * blocks,
        out_shape=(
            shape_of((LEN, channels), bf16),
            shape_of((LEN, channels)),
            shape_of((LEN * STATE, channels), bf16),
        )
        + (shape_of((LEN // blocks, D), bf16),) * blocks,
        scratch_shapes=[
            pltpu.VMEM((LEN, 128), f32),
            pltpu.VMEM((LEN, CHUNK * STATE), bf16),
            pltpu.VMEM((LEN, CHUNK * STATE), bf16),
            pltpu.VMEM((LEN, lanes), f32),
            pltpu.VMEM((LEN, lanes), bf16),
            pltpu.VMEM((LEN * STATE, lanes), f32),
            pltpu.VMEM((LEN * STATE, lanes), bf16),
            pltpu.SemaphoreType.DMA((blocks,)),
        ],
        compiler_params=params(),
        cost_estimate=takes(13),
        name="scan_forward",
    )(me, proj, dt_proj, bias, alog, skip, u, xz, out_w)


def scan_backward(me, blocks, proj, dt_proj, bias, alog, skip, u, xz, out_w, grad, ys, states):
    channels = u.shape[1]
    lanes = lane_block(channels)
    col = lambda i: (0, i)
    rows = pl.BlockSpec((LEN, lanes), col)
    return pl.pallas_call(
        functools.partial(scan_backward_kernel, blocks),
        grid=(channels // lanes,),
        in_specs=[
            SMEM,
            whole((LEN, 128)),
            pl.BlockSpec((DT_RANK, lanes), col),
            pl.BlockSpec((1, lanes), col),
            pl.BlockSpec((STATE, lanes), col),
            pl.BlockSpec((1, lanes), col),
            rows,
            pl.BlockSpec((1, LEN, lanes), lambda i: (1, 0, i)),
            pl.BlockSpec((lanes, D), lambda i: (i, 0)),
            rows,
            pl.BlockSpec(memory_space=pl.ANY),
        ]
        + [whole((LEN // blocks, D))] * blocks,
        out_specs=(
            rows,
            rows,
            pl.BlockSpec((8, lanes), col),
            pl.BlockSpec((STATE, lanes), col),
            pl.BlockSpec((DT_RANK, lanes), col),
            whole((LEN, 128)),
        ),
        out_shape=(
            shape_of((LEN, channels)),
            shape_of((LEN, channels), bf16),
            shape_of((8, channels)),
            shape_of((STATE, channels)),
            shape_of((DT_RANK, channels)),
            shape_of((LEN, 128)),
        ),
        scratch_shapes=[
            pltpu.VMEM((LEN, D), bf16),
            pltpu.VMEM((LEN, 128), f32),
            pltpu.VMEM((LEN, CHUNK * STATE), bf16),
            pltpu.VMEM((LEN, CHUNK * STATE), bf16),
            pltpu.VMEM((LEN, CHUNK * STATE), f32),
            pltpu.VMEM((LEN, CHUNK * STATE), f32),
            pltpu.VMEM((LEN, lanes), f32),
            pltpu.VMEM((LEN, lanes), bf16),
            pltpu.VMEM((LEN, lanes), bf16),
            pltpu.VMEM((LEN, lanes), f32),
            pltpu.VMEM((LEN, lanes), f32),
            pltpu.VMEM((LEN, DT_RANK), f32),
            pltpu.VMEM((LEN * STATE, lanes), f32),
            pltpu.VMEM((LEN * STATE, lanes), bf16),
            pltpu.VMEM((LEN * STATE, lanes), bf16),
            pltpu.VMEM((LEN * STATE, lanes), bf16),
            pltpu.SemaphoreType.DMA((blocks,)),
        ],
        compiler_params=params(),
        cost_estimate=takes(21),
        name="scan_backward",
    )(me, proj, dt_proj, bias, alog, skip, u, xz, out_w, ys, states, *grad)


def conv_backward(me, blocks, dcols, proj, u, xz, du, weight, x_proj):
    channels = u.shape[1]
    return pl.pallas_call(
        functools.partial(conv_backward_kernel, blocks),
        grid=(1,),
        in_specs=[
            SMEM,
            whole((LEN, 128)),
            whole((LEN, 128)),
            whole((LEN, channels)),
            pl.BlockSpec((1, LEN, channels), lambda i: (0, 0, 0)),
            whole((LEN, channels)),
            whole(weight.shape),
            whole(x_proj.shape),
        ],
        out_specs=(whole((LEN, channels)), whole((128, channels)), whole((CONV, channels))),
        out_shape=(
            shape_of((LEN, channels), bf16),
            shape_of((128, channels)),
            shape_of((CONV, channels)),
        ),
        scratch_shapes=[
            pltpu.VMEM((LEN + PAD, channels), f32),
            pltpu.VMEM((LEN + PAD, channels), f32),
        ],
        compiler_params=params(),
        cost_estimate=takes(5),
        name="conv_backward",
    )(me, dcols, proj, u, xz, du, weight, x_proj)


def attention_probabilities(q, k, allowed):
    scores = times_transposed(q, k) * (1.0 / math.sqrt(HEAD_DIM))
    scores = jnp.where(allowed, scores, masked_score)
    peak = jnp.max(scores, axis=1, keepdims=True)
    exponent = jnp.exp(scores - peak)
    return exponent / jnp.sum(exponent, axis=1, keepdims=True)


def causal(me, blocks):
    size = LEN // blocks

    def position(axis):
        index = lax.broadcasted_iota(jnp.int32, (LEN, LEN), axis)
        return jnp.bitwise_xor(index // size, me) * size + index % size

    return position(1) <= position(0)


def attention_forward_kernel(
    blocks, me_ref, wq_ref, wkv_ref, wo_ref, *rest
):
    joined_ref, q_ref, kv_ref, o_ref = rest[blocks : blocks + 4]
    out_refs = rest[blocks + 4 :]
    join_blocks(rest[:blocks], joined_ref)
    normed = joined_ref[...]
    q_ref[...] = matmul(normed, wq_ref[...]).astype(bf16)
    kv_ref[...] = matmul(normed, wkv_ref[...]).astype(bf16)
    kv_heads = wkv_ref.shape[1] // (2 * HEAD_DIM)
    group = HEADS // KV_HEADS
    allowed = causal(me_ref[0], blocks)
    outs = []
    for head in range(kv_heads * group):
        kv = head // group
        q = q_ref[:, head * HEAD_DIM : (head + 1) * HEAD_DIM]
        k = kv_ref[:, kv * HEAD_DIM : (kv + 1) * HEAD_DIM]
        v = kv_ref[:, (kv_heads + kv) * HEAD_DIM : (kv_heads + kv + 1) * HEAD_DIM]
        soft = attention_probabilities(q, k, allowed)
        outs.append(matmul(soft.astype(bf16), v).astype(bf16))
    o_ref[...] = jnp.concatenate(outs, axis=1)
    store_blocks(out_refs, matmul(o_ref[...], wo_ref[...]))


def attention_backward_kernel(
    blocks,
    me_ref,
    q_ref,
    kv_ref,
    wq_ref,
    wkv_ref,
    wo_ref,
    *rest,
):
    dqkv_ref, grad_ref = rest[blocks], rest[-1]
    join_blocks(rest[:blocks], grad_ref)
    dout = times_transposed(grad_ref[...], wo_ref[...]).astype(bf16)
    kv_heads = wkv_ref.shape[1] // (2 * HEAD_DIM)
    group = HEADS // KV_HEADS
    allowed = causal(me_ref[0], blocks)
    scale = 1.0 / math.sqrt(HEAD_DIM)
    dqs, dks, dvs = [], [], []
    for kv in range(kv_heads):
        k = kv_ref[:, kv * HEAD_DIM : (kv + 1) * HEAD_DIM]
        v = kv_ref[:, (kv_heads + kv) * HEAD_DIM : (kv_heads + kv + 1) * HEAD_DIM]
        dk = jnp.zeros((LEN, HEAD_DIM), f32)
        dv = jnp.zeros((LEN, HEAD_DIM), f32)
        for head in range(kv * group, (kv + 1) * group):
            q = q_ref[:, head * HEAD_DIM : (head + 1) * HEAD_DIM]
            do = dout[:, head * HEAD_DIM : (head + 1) * HEAD_DIM]
            soft = attention_probabilities(q, k, allowed)
            dsoft = times_transposed(do, v)
            dscore = soft * (dsoft - jnp.sum(soft * dsoft, axis=1, keepdims=True))
            dscore = dscore.astype(bf16)
            dqs.append((matmul(dscore, k) * scale).astype(bf16))
            dk = dk + transposed_times(dscore, q) * scale
            dv = dv + transposed_times(soft.astype(bf16), do)
        dks.append(dk.astype(bf16))
        dvs.append(dv.astype(bf16))
    dq = jnp.concatenate(dqs, axis=1)
    dkv = jnp.concatenate(dks + dvs, axis=1)
    dqkv_ref[:, : dq.shape[1]] = dq
    dqkv_ref[:, dq.shape[1] :] = dkv
    dn = times_transposed(dq, wq_ref[...]) + times_transposed(dkv, wkv_ref[...])
    store_blocks(rest[blocks + 1 : -1], dn)


def attention_forward(me, blocks, normed, wq, wkv, wo):
    size = LEN // blocks
    heads = shape_of((LEN, wq.shape[1]), bf16)
    kept = (shape_of((LEN, D), bf16), heads, shape_of((LEN, wkv.shape[1]), bf16), heads)
    return pl.pallas_call(
        functools.partial(attention_forward_kernel, blocks),
        grid=(1,),
        in_specs=[SMEM, whole(wq.shape), whole(wkv.shape), whole(wo.shape)]
        + [whole((size, D))] * blocks,
        out_specs=tuple(whole(item.shape) for item in kept) + (whole((size, D)),) * blocks,
        out_shape=kept + (shape_of((size, D), bf16),) * blocks,
        compiler_params=params(),
        cost_estimate=takes(6),
        name="attention_forward",
    )(me, wq, wkv, wo, *normed)


def attention_backward(me, blocks, grad, q, kv, wq, wkv, wo):
    size = LEN // blocks
    cols = wq.shape[1] + wkv.shape[1]
    return pl.pallas_call(
        functools.partial(attention_backward_kernel, blocks),
        grid=(1,),
        in_specs=[
            SMEM,
            whole(q.shape),
            whole(kv.shape),
            whole(wq.shape),
            whole(wkv.shape),
            whole(wo.shape),
        ]
        + [whole((size, D))] * blocks,
        out_specs=(whole((LEN, cols)),) + (whole((size, D)),) * blocks,
        out_shape=(shape_of((LEN, cols), bf16),) + (shape_of((size, D), bf16),) * blocks,
        scratch_shapes=[pltpu.VMEM((LEN, D), bf16)],
        compiler_params=params(),
        cost_estimate=takes(8),
        name="attention_backward",
    )(me, q, kv, wq, wkv, wo, *grad)


def norm_forward_kernel(hidden_ref, gain_ref, *rest):
    part_refs, (out_ref, normed_ref) = rest[:-2], rest[-2:]
    hidden = hidden_ref[...].astype(f32)
    for ref in part_refs:
        hidden = hidden + ref[...].astype(f32)
    scale = lax.rsqrt(jnp.mean(hidden * hidden, axis=1, keepdims=True) + epsilon)
    out_ref[...] = hidden
    normed_ref[...] = (hidden * scale * gain_ref[...]).astype(bf16)


def norm_forward(hidden, gain, parts):
    shape = hidden.shape
    return pl.pallas_call(
        norm_forward_kernel,
        grid=(1,),
        in_specs=[whole(shape), whole((1, D))] + [whole(shape)] * len(parts),
        out_specs=(whole(shape), whole(shape)),
        out_shape=(shape_of(shape), shape_of(shape, bf16)),
        compiler_params=params(),
        cost_estimate=takes(2),
        name="norm_forward",
    )(hidden, gain, *parts)


def pull_norm(grad, hidden, gain):
    scale = lax.rsqrt(jnp.mean(hidden * hidden, axis=1, keepdims=True) + epsilon)
    unit = hidden * scale
    through = grad * gain
    back = scale * (through - unit * jnp.mean(through * unit, axis=1, keepdims=True))
    return back, jnp.sum(grad * unit, axis=0, keepdims=True)


def norm_backward_kernel(grad_ref, hidden_ref, gain_ref, *rest):
    part_refs, (out_ref, low_ref, dgain_ref) = rest[:-3], rest[-3:]
    dn = part_refs[0][...].astype(f32)
    for ref in part_refs[1:]:
        dn = dn + ref[...].astype(f32)
    back, dgain = pull_norm(dn, hidden_ref[...], gain_ref[...])
    grad = grad_ref[...] + back
    out_ref[...] = grad
    low_ref[...] = grad.astype(bf16)
    dgain_ref[...] = dgain


def norm_backward(grad, hidden, gain, parts):
    shape = hidden.shape
    return pl.pallas_call(
        norm_backward_kernel,
        grid=(1,),
        in_specs=[whole(shape), whole(shape), whole((1, D))] + [whole(shape)] * len(parts),
        out_specs=(whole(shape), whole(shape), whole((1, D))),
        out_shape=(shape_of(shape), shape_of(shape, bf16), shape_of((1, D))),
        compiler_params=params(),
        cost_estimate=takes(2.5),
        name="norm_backward",
    )(grad, hidden, gain, *parts)


def router_backward_kernel(grad_ref, hidden_ref, gain_ref, normed_ref, picks_ref, router_ref, *rest):
    part_refs, (out_ref, low_ref, dgain_ref, drouter_ref) = rest[:-4], rest[-4:]
    dn = part_refs[0][...].astype(f32)
    for ref in part_refs[1:]:
        dn = dn + ref[...].astype(f32)
    normed, router = normed_ref[...], router_ref[...]
    rows = normed.shape[0]
    ids = lax.broadcasted_iota(jnp.int32, (rows, EXPERTS), 1)
    logits = times_transposed(normed, router)
    hot = [(ids == picks_ref[:, k : k + 1]).astype(f32) for k in (0, 1)]
    chosen = [jnp.sum(hot[k] * logits, axis=1, keepdims=True) for k in (0, 1)]
    peak = jnp.maximum(chosen[0], chosen[1])
    weight = [jnp.exp(value - peak) for value in chosen]
    total = weight[0] + weight[1]
    weight = [value / total for value in weight]
    dw = [dn[:, D + k : D + k + 1] for k in (0, 1)]
    mean = weight[0] * dw[0] + weight[1] * dw[1]
    dlog = sum(hot[k] * (weight[k] * (dw[k] - mean)) for k in (0, 1)).astype(bf16)
    dn = dn[:, :D] + matmul(dlog, router)
    back, dgain = pull_norm(dn, hidden_ref[...], gain_ref[...])
    grad = grad_ref[...].astype(f32) + back
    out_ref[...] = grad
    low_ref[...] = grad.astype(bf16)
    dgain_ref[...] = dgain
    drouter_ref[...] = transposed_times(dlog, normed)


def router_backward(grad, hidden, gain, normed, picks, router, parts):
    shape = hidden.shape
    wide_rows = whole((shape[0], D + 128))
    return pl.pallas_call(
        router_backward_kernel,
        grid=(1,),
        in_specs=[
            whole(shape),
            whole(shape),
            whole((1, D)),
            whole(shape),
            whole((shape[0], 2)),
            whole((EXPERTS, D)),
        ]
        + [wide_rows] * len(parts),
        out_specs=(whole(shape), whole(shape), whole((1, D)), whole((EXPERTS, D))),
        out_shape=(
            shape_of(shape),
            shape_of(shape, bf16),
            shape_of((1, D)),
            shape_of((EXPERTS, D)),
        ),
        compiler_params=params(),
        cost_estimate=takes(3),
        name="router_backward",
    )(grad, hidden, gain, normed, picks, router, *parts)


def experts_kernel(blocks, routes_ref, router_ref, w_in_ref, w_out_ref, *rest):
    normed_refs, grad_refs = rest[:blocks], rest[blocks : 2 * blocks]
    moved_ref, act_ref, weighted_ref = rest[2 * blocks : 2 * blocks + 3]
    dn_refs = rest[2 * blocks + 3 : 3 * blocks + 3]
    (
        normed_ref,
        grad_ref,
        even_ref,
        odd_ref,
        grads_ref,
        place_ref,
        first_ref,
        second_ref,
        scale_ref,
        back_ref,
        kept_ref,
        dw_ref,
        sort_ref,
    ) = rest[3 * blocks + 3 :]
    expert = pl.program_id(0)
    slots = EXPERTS * CAP
    units = w_out_ref.shape[1]

    @pl.when(expert == 0)
    def _():
        join_blocks(normed_refs, normed_ref)
        join_blocks(grad_refs, grad_ref)
        routes = routes_ref[...]
        ids = lax.broadcasted_iota(jnp.int32, (EXPERTS, LEN), 0)
        hot = [(ids == routes[k : k + 1, :]).astype(f32) for k in (0, 1)]
        earlier = (
            lax.broadcasted_iota(jnp.int32, (LEN, LEN), 0)
            < lax.broadcasted_iota(jnp.int32, (LEN, LEN), 1)
        ).astype(bf16)
        rank0 = matmul(hot[0].astype(bf16), earlier)
        rank1 = matmul(hot[1].astype(bf16), earlier) + jnp.sum(hot[0], axis=1, keepdims=True)
        counts = jnp.sum(hot[0] + hot[1], axis=1, keepdims=True)
        below = (
            lax.broadcasted_iota(jnp.int32, (EXPERTS, EXPERTS), 1)
            < lax.broadcasted_iota(jnp.int32, (EXPERTS, EXPERTS), 0)
        ).astype(f32)
        starts = dot_exact(below, jnp.broadcast_to(counts, (EXPERTS, 128)))[:, 0:1]
        slot = lax.broadcasted_iota(jnp.int32, (EXPERTS, slots), 1)
        owner = (
            slot // CAP == lax.broadcasted_iota(jnp.int32, (EXPERTS, slots), 0)
        ).astype(f32)
        place_in = (slot % CAP).astype(f32)
        row = jnp.sum(owner * (starts + place_in + 1.0), axis=0, keepdims=True) - 1.0
        used = jnp.sum(owner * (place_in < counts).astype(f32), axis=0, keepdims=True)
        row = jnp.where(used > 0.5, row, -1.0).astype(jnp.int32)
        rows = lax.broadcasted_iota(jnp.int32, (2 * LEN, slots), 0)
        sort_ref[...] = (rows == row).astype(f32).astype(bf16)
        first = ids.astype(f32) * CAP
        position = [
            jnp.sum(hot[k] * (first + rank), axis=0, keepdims=True).astype(jnp.int32)
            for k, rank in ((0, rank0), (1, rank1))
        ]
        logits = times_transposed(router_ref[...], normed_ref[...])
        chosen = [jnp.sum(hot[k] * logits, axis=0, keepdims=True) for k in (0, 1)]
        peak = jnp.maximum(chosen[0], chosen[1])
        weight = [jnp.exp(value - peak) for value in chosen]
        total = weight[0] + weight[1]
        weight = [value / total for value in weight]
        slot = lax.broadcasted_iota(jnp.int32, (slots, LEN), 0)
        in0 = (slot == position[0]).astype(f32)
        in1 = (slot == position[1]).astype(f32)
        weighted = in0 * weight[0] + in1 * weight[1]
        place = (in0 + in1).astype(bf16)
        first_ref[...] = in0.astype(bf16)
        second_ref[...] = in1.astype(bf16)
        place_ref[...] = place
        weighted_ref[...] = weighted.astype(bf16)
        scale_ref[...] = jnp.broadcast_to(jnp.sum(weighted, axis=1, keepdims=True), (slots, 128))
        grads_ref[...] = matmul(place, grad_ref[...]).astype(bf16)
        spread = lax.broadcasted_iota(jnp.int32, (128, 256), 1) - 2 * lax.broadcasted_iota(
            jnp.int32, (128, 256), 0
        )
        for block in range(D // 128):
            rows = matmul(place, normed_ref[:, block * 128 : (block + 1) * 128]).astype(bf16)
            cols = slice(block * 256, (block + 1) * 256)
            even_ref[:, cols] = matmul(rows, (spread == 0).astype(bf16)).astype(bf16)
            odd_ref[:, cols] = matmul(rows, (spread == 1).astype(bf16)).astype(bf16)

    lane = lax.broadcasted_iota(jnp.int32, (CAP, 2 * D), 1)
    for index in range(SIDE):
        mine = pl.ds(pl.multiple_of((expert * SIDE + index) * CAP, CAP), CAP)
        w_in = w_in_ref[index].reshape(2 * D, units)
        w_out = w_out_ref[index]
        both = matmul(jnp.concatenate([even_ref[mine, :], odd_ref[mine, :]], axis=0), w_in)
        plain = times_transposed(grads_ref[mine, :], w_out)
        gate, up = both[:CAP], both[CAP:]
        sig = sigmoid(gate)
        silu = gate * sig
        act = silu * up
        act_low = act.astype(bf16)
        act_ref[index] = act_low
        scale = scale_ref[mine, 0:1]
        dw_ref[mine, :] = jnp.broadcast_to(
            jnp.sum(plain * act_low.astype(f32), axis=1, keepdims=True), (CAP, 128)
        ).astype(bf16)
        dact = plain * scale
        dgate = (dact * sig * (1.0 + gate * (1.0 - sig)) * up).astype(bf16)
        dup = (dact * silu).astype(bf16)
        back = times_transposed(jnp.concatenate([dgate, dup], axis=0), w_in)
        back_ref[mine, :] = jnp.where(lane % 2 == 0, back[:CAP], back[CAP:]).astype(bf16)
        kept_ref[mine, :] = jnp.concatenate([dgate, dup, (act * scale).astype(bf16)], axis=1)

    @pl.when(expert == EXPERTS // SIDE - 1)
    def _():
        pairs = (
            lax.broadcasted_iota(jnp.int32, (256, 128), 0) // 2
            == lax.broadcasted_iota(jnp.int32, (256, 128), 1)
        ).astype(bf16)
        size = LEN // blocks
        for block in range(D // 128):
            cols = slice(block * 256, (block + 1) * 256)
            wide_rows = transposed_times(place_ref[...], back_ref[:, cols]).astype(bf16)
            dn = matmul(wide_rows, pairs).astype(bf16)
            for k, ref in enumerate(dn_refs):
                ref[:, block * 128 : (block + 1) * 128] = dn[k * size : (k + 1) * size]
        lanes = lax.broadcasted_iota(jnp.int32, (LEN, 128), 1)
        gates = [transposed_times(ref[...], dw_ref[...]) for ref in (first_ref, second_ref)]
        gates = jnp.where(lanes == 0, gates[0], jnp.where(lanes == 1, gates[1], 0.0)).astype(bf16)
        for k, ref in enumerate(dn_refs):
            ref[:, D:] = gates[k * size : (k + 1) * size]
        moved_ref[...] = matmul(sort_ref[...], kept_ref[...]).astype(bf16)


def experts(blocks, routes, router, normed, grad, w_in, w_out):
    units = w_out.shape[1]
    slots = EXPERTS * CAP
    size = LEN // blocks
    return pl.pallas_call(
        functools.partial(experts_kernel, blocks),
        grid=(EXPERTS // SIDE,),
        in_specs=[
            whole((2, LEN)),
            whole((EXPERTS, D)),
            pl.BlockSpec((SIDE, D, 2, units), lambda e: (e, 0, 0, 0)),
            pl.BlockSpec((SIDE, units, D), lambda e: (e, 0, 0)),
        ]
        + [whole((size, D))] * (2 * blocks),
        out_specs=(
            whole((2 * LEN, 3 * units)),
            pl.BlockSpec((SIDE, CAP, units), lambda e: (e, 0, 0)),
            whole((slots, LEN)),
        )
        + (whole((size, D + 128)),) * blocks,
        out_shape=(
            shape_of((2 * LEN, 3 * units), bf16),
            shape_of((EXPERTS, CAP, units), bf16),
            shape_of((slots, LEN), bf16),
        )
        + (shape_of((size, D + 128), bf16),) * blocks,
        scratch_shapes=[
            pltpu.VMEM((LEN, D), bf16),
            pltpu.VMEM((LEN, D), bf16),
            pltpu.VMEM((slots, 2 * D), bf16),
            pltpu.VMEM((slots, 2 * D), bf16),
            pltpu.VMEM((slots, D), bf16),
            pltpu.VMEM((slots, LEN), bf16),
            pltpu.VMEM((slots, LEN), bf16),
            pltpu.VMEM((slots, LEN), bf16),
            pltpu.VMEM((slots, 128), f32),
            pltpu.VMEM((slots, 2 * D), bf16),
            pltpu.VMEM((slots, 3 * units), bf16),
            pltpu.VMEM((slots, 128), bf16),
            pltpu.VMEM((2 * LEN, slots), bf16),
        ],
        compiler_params=params(),
        cost_estimate=takes(37),
        name="experts",
    )(routes, router, w_in, w_out, *normed, *grad)


def experts_out_kernel(blocks, act_ref, weighted_ref, w_out_ref, *rest):
    made_refs, ye_ref = rest[-1 - blocks : -1], rest[-1]
    expert = pl.program_id(0)
    for index in range(SIDE):
        mine = pl.ds(pl.multiple_of((expert * SIDE + index) * CAP, CAP), CAP)
        ye_ref[mine, :] = matmul(act_ref[index], w_out_ref[index]).astype(bf16)

    @pl.when(expert == pl.num_programs(0) - 1)
    def _():
        made = transposed_times(weighted_ref[...], ye_ref[...])
        size = LEN // blocks
        if len(rest) > blocks + 1:
            made = made + jnp.concatenate([ref[...].astype(f32) for ref in rest[:blocks]], axis=0)
        for k, ref in enumerate(made_refs):
            ref[...] = made[k * size : (k + 1) * size].astype(bf16)


def experts_out(blocks, part, parts, act, weighted, w_out, earlier=()):
    units = w_out.shape[1]
    count = EXPERTS // parts
    slots = count * CAP
    rows = whole((LEN // blocks, D))
    return pl.pallas_call(
        functools.partial(experts_out_kernel, blocks),
        grid=(count // SIDE,),
        in_specs=[
            pl.BlockSpec((SIDE, CAP, units), lambda e: (e + part * (count // SIDE), 0, 0)),
            pl.BlockSpec((slots, LEN), lambda e: (part, 0)),
            pl.BlockSpec((SIDE, units, D), lambda e: (e + part * (count // SIDE), 0, 0)),
        ]
        + [rows] * len(earlier),
        out_specs=(rows,) * blocks,
        out_shape=(shape_of((LEN // blocks, D), bf16),) * blocks,
        scratch_shapes=[pltpu.VMEM((slots, D), bf16)],
        compiler_params=params(),
        cost_estimate=takes(14 / parts),
        name="experts_out",
    )(act, weighted, w_out, *earlier)


def sort_rows(refs, groups, out_ref):
    share = LEN // len(refs)
    for group in range(groups):
        for k, ref in enumerate(refs):
            at = group * LEN + k * share
            out_ref[at : at + share, :] = ref[group * share : (group + 1) * share, :]


def sorted_columns_kernel(groups, *refs):
    column_refs, (left_ref, right_ref, starts_ref, counts_ref, rows_ref) = refs[:-5], refs[-5:]
    width = left_ref.shape[1]
    sort_rows(column_refs, groups, rows_ref)
    ids = lax.broadcasted_iota(jnp.int32, (LEN, EXPERTS), 1).astype(f32)
    earlier = (
        lax.broadcasted_iota(jnp.int32, (LEN, LEN), 1)
        < lax.broadcasted_iota(jnp.int32, (LEN, LEN), 0)
    ).astype(bf16)
    below = (
        lax.broadcasted_iota(jnp.int32, (EXPERTS, EXPERTS), 0)
        < lax.broadcasted_iota(jnp.int32, (EXPERTS, EXPERTS), 1)
    ).astype(f32)
    lane = lax.broadcasted_iota(jnp.int32, (LEN, 2 * LEN), 1).astype(f32)
    all_starts, all_counts = [], []
    for group in range(groups):
        rows = rows_ref[group * LEN : (group + 1) * LEN, :]
        picks = rows[:, 4 * width : 4 * width + 2].astype(f32)
        hot = [(picks[:, k : k + 1] == ids).astype(f32) for k in (0, 1)]
        first = jnp.sum(hot[0], axis=0, keepdims=True)
        counts = first + jnp.sum(hot[1], axis=0, keepdims=True)
        starts = dot_exact(jnp.broadcast_to(counts, (8, EXPERTS)), below)[0:1]
        ranks = [matmul(earlier, hot[0].astype(bf16)), matmul(earlier, hot[1].astype(bf16)) + first]
        place = [jnp.sum(hot[k] * (starts + ranks[k]), axis=1, keepdims=True) for k in (0, 1)]
        move = ((lane == place[0]).astype(f32) + (lane == place[1]).astype(f32)).astype(bf16)
        to = slice(group * 2 * LEN, (group + 1) * 2 * LEN)
        left_ref[to, :] = transposed_times(move, rows[:, :width]).astype(bf16)
        right_ref[to, :] = transposed_times(move, rows[:, width : 2 * width]).astype(bf16)
        all_starts.append(starts)
        all_counts.append(counts)
    starts_ref[...] = jnp.concatenate(all_starts, axis=0).astype(jnp.int32)
    counts_ref[...] = jnp.concatenate(all_counts, axis=0).astype(jnp.int32)


def sorted_columns(groups, columns):
    rows, width = groups * 2 * LEN, D // groups
    table = shape_of((groups, EXPERTS), jnp.int32)
    return pl.pallas_call(
        functools.partial(sorted_columns_kernel, groups),
        grid=(1,),
        in_specs=[whole(item.shape) for item in columns],
        out_specs=(whole((rows, width)),) * 2 + (whole(table.shape),) * 2,
        out_shape=(shape_of((rows, width), bf16),) * 2 + (table,) * 2,
        scratch_shapes=[pltpu.VMEM((groups * LEN, columns[0].shape[1]), bf16)],
        compiler_params=params(),
        cost_estimate=takes(6),
        name="sorted_columns",
    )(*columns)


def expert_grad_kernel(groups, starts_ref, counts_ref, moved_ref, left_ref, right_ref, *rest):
    din_ref, dout_ref = rest
    units = moved_ref.shape[1] // 3
    window = CAP + 16
    row = lax.broadcasted_iota(jnp.int32, (window, 1), 0)
    for index in range(SIDE):
        expert = pl.program_id(0) * SIDE + index
        lefts, rights, moves = [], [], []
        for group in range(groups):
            start, count = starts_ref[group, expert], counts_ref[group, expert]
            base = jnp.minimum((start // 16) * 16, 2 * LEN - window)
            keep = jnp.logical_and(row >= start - base, row < start - base + count).astype(bf16)
            rows = pl.ds(pl.multiple_of(group * 2 * LEN + base, 16), window)
            lefts.append(left_ref[rows, :] * keep)
            rights.append(right_ref[rows, :] * keep)
            moves.append(moved_ref[rows, :])
        moved = jnp.concatenate(moves, axis=0)
        din = transposed_times(jnp.concatenate(lefts, axis=0), moved[:, : 2 * units])
        din_ref[index, :, 0, :] = din[:, :units]
        din_ref[index, :, 1, :] = din[:, units:]
        dout_ref[index] = transposed_times(jnp.concatenate(rights, axis=0), moved[:, 2 * units :])


def expert_grads(groups, moved, left, right, starts, counts):
    width = left.shape[1]
    units = moved.shape[1] // 3
    inputs = (moved, left, right)
    return pl.pallas_call(
        functools.partial(expert_grad_kernel, groups),
        grid=(EXPERTS // SIDE,),
        in_specs=[SMEM, SMEM] + [whole(item.shape) for item in inputs],
        out_specs=(
            pl.BlockSpec((SIDE, width, 2, units), lambda e: (e, 0, 0, 0)),
            pl.BlockSpec((SIDE, width, units), lambda e: (e, 0, 0)),
        ),
        out_shape=(
            shape_of((EXPERTS, width, 2, units)),
            shape_of((EXPERTS, width, units)),
        ),
        compiler_params=params(),
        cost_estimate=takes(12),
        name="expert_grads",
    )(starts, counts, *inputs)


def pack_columns_kernel(groups, lanes, *refs):
    in_refs, out_ref = refs[:-1], refs[-1]
    width = D // groups
    values = [ref[...].astype(f32) for ref in in_refs]
    rows = values[0].shape[0]
    for group in range(groups):
        parts = [
            value[:, group * width : (group + 1) * width] if value.shape[1] == D else value
            for value in values
        ]
        spare = lanes - sum(part.shape[1] for part in parts)
        if spare:
            parts.append(jnp.zeros((rows, spare), f32))
        whole_row = jnp.concatenate(parts, axis=1) if len(parts) > 1 else parts[0]
        out_ref[group] = whole_row.astype(bf16)


def pack_columns(groups, *values):
    width, rows = D // groups, values[0].shape[0]
    lanes = sum(width if value.shape[1] == D else value.shape[1] for value in values)
    if len(values) > 1:
        lanes += -lanes % 128
    return pl.pallas_call(
        functools.partial(pack_columns_kernel, groups, lanes),
        grid=(1,),
        in_specs=[whole(value.shape) for value in values],
        out_specs=whole((groups, rows, lanes)),
        out_shape=shape_of((groups, rows, lanes), bf16),
        compiler_params=params(),
        cost_estimate=takes(3),
        name="pack_columns",
    )(*values)


def mix_grad_kernel(groups, normed_ref, first_ref, second_ref, *refs):
    extra_refs, out_ref = refs[:-1], refs[-1]
    width = D // groups
    grads = [
        transposed_times(normed_ref[...], ref[...]).astype(bf16) for ref in (first_ref, second_ref)
    ]
    channels = grads[0].shape[1]
    share = channels // groups
    extras = [ref[...] for ref in extra_refs]
    tall = [extra for extra in extras if extra.shape[0] > STATE]
    flat = [extra for extra in extras if extra.shape[0] <= STATE]
    for group in range(groups):
        at = 0
        for grad in grads:
            out_ref[group, at : at + width, :] = grad[group * width : (group + 1) * width]
            at += width
        rows = [
            extra[group * (extra.shape[0] // groups) : (group + 1) * (extra.shape[0] // groups)]
            for extra in tall
        ]
        line = jnp.concatenate(
            [
                extra[row : row + 1, group * share : (group + 1) * share]
                for extra in flat
                for row in range(extra.shape[0])
            ],
            axis=1,
        )
        spare = -line.shape[1] % channels
        line = jnp.concatenate([line, jnp.zeros((1, spare), f32)], axis=1)
        for first in range(0, line.shape[1], channels):
            rows.append(line[:, first : first + channels])
        spare = out_ref.shape[1] - at - sum(row.shape[0] for row in rows)
        if spare:
            rows.append(jnp.zeros((spare, channels), f32))
        out_ref[group, at:, :] = jnp.concatenate(rows, axis=0).astype(bf16)


def mix_grads(groups, normed, first, second, *extras):
    channels = first.shape[1]
    rows = sum(extra.shape[0] // groups for extra in extras if extra.shape[0] > STATE)
    lines = sum(extra.shape[0] for extra in extras if extra.shape[0] <= STATE)
    rows += -(-lines // groups)
    rows += -rows % 16 + 2 * (D // groups)
    return pl.pallas_call(
        functools.partial(mix_grad_kernel, groups),
        grid=(1,),
        in_specs=[whole(item.shape) for item in (normed, first, second) + extras],
        out_specs=whole((groups, rows, channels)),
        out_shape=shape_of((groups, rows, channels), bf16),
        compiler_params=params(),
        cost_estimate=takes(7),
        name="mix_grads",
    )(normed, first, second, *extras)


def unpack_mix_kernel(groups, sum_ref, mix_ref, xproj_ref, dt_ref, flat_ref):
    width = D // groups
    channels = sum_ref.shape[1]
    for half in (0, 1):
        mix_ref[:, half, :] = sum_ref[half * width : (half + 1) * width, :].astype(f32)
    small = sum_ref[2 * width :, :].astype(f32)
    at, count = xproj_ref.shape[0], dt_ref.shape[0]
    xproj_ref[...] = small[:at]
    dt_ref[...] = small[at : at + count]
    share = channels // groups
    for line in range(flat_ref.shape[0]):
        row, first = divmod(line * share, channels)
        flat_ref[line : line + 1, :] = small[at + count + row : at + count + row + 1, first : first + share]


def unpack_mix(groups, total):
    width, channels = D // groups, total.shape[1]
    shapes = (
        (width, 2, channels),
        (128 // groups, channels),
        (DT_RANK // groups, channels),
        (STATE + 2 + CONV, channels // groups),
    )
    return pl.pallas_call(
        functools.partial(unpack_mix_kernel, groups),
        grid=(1,),
        in_specs=[whole(total.shape)],
        out_specs=tuple(whole(shape) for shape in shapes),
        out_shape=tuple(shape_of(shape) for shape in shapes),
        compiler_params=params(),
        cost_estimate=takes(3),
        name="unpack_mix",
    )(total)


def out_grad_kernel(groups, first, heads_ref, acted_ref, *rest):
    column_refs, out_refs, rows_ref = rest[:-3], rest[-3:-1], rest[-1]
    width = out_refs[0].shape[0]
    sort_rows(column_refs, groups, rows_ref)
    for k, (left_ref, out_ref) in enumerate(zip((heads_ref, acted_ref), out_refs)):
        columns = rows_ref[:, (first + k) * width : (first + k + 1) * width]
        out_ref[...] = transposed_times(columns, left_ref[...])


def out_grads(groups, first, columns, heads, acted):
    width = D // groups
    lefts = (heads, acted)
    return pl.pallas_call(
        functools.partial(out_grad_kernel, groups, first),
        grid=(1,),
        in_specs=[whole(item.shape) for item in lefts + tuple(columns)],
        out_specs=tuple(whole((width, item.shape[1])) for item in lefts),
        out_shape=tuple(shape_of((width, item.shape[1])) for item in lefts),
        scratch_shapes=[pltpu.VMEM((groups * LEN, columns[0].shape[1]), bf16)],
        compiler_params=params(),
        cost_estimate=takes(6),
        name="out_grads",
    )(*lefts, *columns)


def last_grad_kernel(groups, gated_ref, *rest):
    column_refs, (out_ref, sums_ref, rows_ref) = rest[:-3], rest[-3:]
    share = LEN // len(column_refs)
    stride = column_refs[0].shape[0] // groups
    sums = jnp.zeros(sums_ref.shape, f32)
    for group in range(groups):
        for k, ref in enumerate(column_refs):
            at = group * LEN + k * share
            first = group * stride
            rows_ref[at : at + share, :] = ref[first : first + share, :]
            sums = sums + ref[first + share : first + stride, :].astype(f32)
    sums_ref[...] = sums
    out_ref[...] = transposed_times(rows_ref[...], gated_ref[...])


def last_grads(groups, columns, gated):
    width = D // groups
    extra = columns[0].shape[0] // groups - LEN // len(columns)
    shapes = ((width, gated.shape[1]), (extra, width))
    return pl.pallas_call(
        functools.partial(last_grad_kernel, groups),
        grid=(1,),
        in_specs=[whole(gated.shape)] + [whole(item.shape) for item in columns],
        out_specs=tuple(whole(shape) for shape in shapes),
        out_shape=tuple(shape_of(shape) for shape in shapes),
        scratch_shapes=[pltpu.VMEM((groups * LEN, width), bf16)],
        compiler_params=params(),
        cost_estimate=takes(5),
        name="last_grads",
    )(gated, *columns)


def shards(
    tokens,
    cotangent,
    norm_gains,
    mix_in,
    conv_weight,
    x_proj,
    dt_proj,
    dt_bias,
    a_log,
    skip_gain,
    mix_out,
    ffn_in,
    ffn_out,
    attn_query,
    attn_keyval,
    attn_out,
    router,
    expert_in,
    expert_out,
    routes,
):
    members = lax.axis_size("tensor")
    member = lax.axis_index("tensor")
    share = LEN // members
    groups = lax.axis_size("dp")
    gains = norm_gains.astype(f32)
    me = member.astype(jnp.int32).reshape(1)

    def swap(value, k):
        return lax.ppermute(value, "tensor", [(i, i ^ k) for i in range(members)])

    def join_list(rows):
        return [rows] + [swap(rows, k) for k in range(1, members)]

    def join(rows):
        return jnp.concatenate(join_list(rows), axis=0)

    def split_list(blocks):
        return [blocks[0]] + [swap(blocks[k], k) for k in range(1, members)]

    def blocks_of(partial):
        return [partial[k * share : (k + 1) * share].astype(bf16) for k in range(members)]

    def all_sum(partial):
        total = partial.astype(f32)
        for k in range(1, members):
            total = total + swap(partial, k).astype(f32)
        return total

    def all_sum_rows(partial):
        total = partial.astype(f32)
        for k in range(1, members):
            blocks = swap(partial, k).reshape(members, share, -1)
            ordered = jnp.concatenate([blocks[j ^ k] for j in range(members)], axis=0)
            total = total + ordered.astype(f32)
        return total

    def dp_scatter(value):
        return lax.psum_scatter(value, "dp", scatter_dimension=0, tiled=True)

    def dp_gather(value):
        return lax.all_gather(value, "dp", axis=0, tiled=True)

    def to_columns(*rows):
        came = lax.all_to_all(pack_columns(groups, *rows), "dp", 0, 0, tiled=True)
        return came.reshape(-1, came.shape[2])

    def hold(value, *others):
        return lax.optimization_barrier((value,) + others)[0]

    def gain(index):
        return gains[index : index + 1]

    hidden1, rows1 = norm_forward(tokens, gain(0), [])
    normed1 = join(rows1)
    channels = mix_in.shape[2]
    bias, skip = dt_bias.reshape(1, channels), skip_gain.reshape(1, channels)
    alog = a_log.T
    xz = jnp.einsum("td,dgc->gtc", normed1, mix_in, preferred_element_type=f32)
    u, proj_part = conv_forward(me, members, xz, conv_weight, x_proj)
    proj = all_sum_rows(proj_part)
    gated_low, ys, states, *mixed = scan_forward(
        me, members, proj, dt_proj, bias, alog, skip, u, xz, mix_out
    )
    all_gated = dp_gather(gated_low)
    hidden2, rows2 = norm_forward(hidden1, gain(1), split_list(mixed))
    normed2 = join(rows2)
    gate_up = jnp.einsum("td,dgc->gtc", normed2, ffn_in, preferred_element_type=f32)
    ffn_gate = sigmoid(gate_up[0])
    acted_low = (gate_up[0] * ffn_gate * gate_up[1]).astype(bf16)
    all_acted = dp_gather(acted_low)
    hidden3, rows3 = norm_forward(
        hidden2, gain(2), split_list(blocks_of(matmul(acted_low, ffn_out)))
    )
    keyval = attn_keyval.reshape(D, -1)
    rows3 = join_list(rows3)
    rows3[0] = hold(rows3[0], all_gated)
    normed3, query_low, keyval_low, attended_low, *attended = attention_forward(
        me, members, rows3, attn_query, keyval, attn_out
    )
    all_attended = dp_gather(attended_low)
    hidden4, rows4 = norm_forward(hidden3, gain(3), split_list(attended))
    normed4 = join_list(rows4)

    at = jnp.bitwise_xor(jnp.arange(members, dtype=jnp.int32), member)
    picks = routes.reshape(members, share, 2)[at].reshape(LEN, 2)
    own_picks = picks[:share]
    router_rows = router.T
    moved, expert_low, slot_weights, *dn_part = experts(
        members, picks.T, router_rows, normed4, join_list(cotangent), expert_in, expert_out
    )
    dn_part[0] = hold(dn_part[0], all_acted, all_attended)
    all_moved = dp_gather(moved)
    dn_part = split_list(dn_part)
    made = experts_out(members, 0, 2, expert_low, slot_weights, expert_out)
    dn_part[0] = hold(dn_part[0], made[0])
    grad, low4, gain4, grad_router = router_backward(
        cotangent, hidden4, gain(3), rows4, own_picks, router_rows, dn_part
    )
    grad_low4 = join_list(low4)

    width = D // groups
    units = expert_out.shape[1]

    dqkv, *dnormed = attention_backward(
        me, members, grad_low4, query_low, keyval_low, attn_query, keyval, attn_out
    )
    dn_blocks = split_list(dnormed)
    made = [hold(made[0], dn_blocks[0])] + list(made[1:])
    made = experts_out(members, 1, 2, expert_low, slot_weights, expert_out, made)
    attn_in_part = transposed_times(normed3, dqkv).astype(bf16)
    attn_in_sum = dp_scatter(attn_in_part)
    grad, low3, gain3 = norm_backward(
        hold(grad, attn_in_part, made[0]), hidden3, gain(2), dn_blocks
    )
    grad_low3 = join(low3)

    dact = times_transposed(grad_low3, ffn_out)
    dgate_up = jnp.concatenate(
        [
            dact * ffn_gate * (1.0 + gate_up[0] * (1.0 - ffn_gate)) * gate_up[1],
            dact * gate_up[0] * ffn_gate,
        ],
        axis=1,
    ).astype(bf16)
    hidden_units = ffn_in.shape[2]
    dnormed = jnp.einsum(
        "tgc,dgc->td",
        dgate_up.reshape(LEN, 2, hidden_units),
        ffn_in,
        preferred_element_type=f32,
    )
    dn_blocks = blocks_of(dnormed)
    ffn_in_part = transposed_times(normed2, hold(dgate_up, dn_blocks[0])).astype(bf16)
    ffn_in_sum = dp_scatter(ffn_in_part)
    columns = to_columns(
        hold(rows4, dn_blocks[0]), cotangent, low4, low3, own_picks.astype(f32)
    )
    grad, low2, gain2 = norm_backward(
        hold(grad, ffn_in_part, all_moved),
        hidden2,
        gain(1),
        split_list(dn_blocks),
    )
    grad_low2 = join_list(low2)

    du, dzs, small, dalog, ddt, dcols_part = scan_backward(
        me, members, proj, dt_proj, bias, alog, skip, u, xz, mix_out, grad_low2, ys, states
    )
    dcols = all_sum_rows(dcols_part.astype(bf16))
    dcols = hold(dcols, attn_in_sum, columns)
    columns = join_list(hold(columns, dcols))
    dxs, dxproj, dconv = conv_backward(
        me, members, dcols, proj, u, xz, du, conv_weight, x_proj
    )
    dmixed = jnp.stack([dxs, dzs])
    dnormed = jnp.einsum("gtc,dgc->td", dmixed, mix_in, preferred_element_type=f32)
    dn_blocks = blocks_of(dnormed)
    mix_part = mix_grads(
        groups, normed1, hold(dxs, dn_blocks[0]), dzs, dxproj, ddt, dalog, small[:2], dconv
    )
    mix_sum = dp_scatter(mix_part.reshape(-1, channels))
    dn_blocks = split_list(dn_blocks)
    dn_blocks[0] = hold(dn_blocks[0], mix_part)
    grad, _, gain1 = norm_backward(grad, hidden1, gain(0), dn_blocks)

    extra = jnp.concatenate([gain1, gain2, gain3, gain4, grad_router], axis=0).astype(bf16)
    extra = jnp.pad(extra, ((0, -extra.shape[0] % 16), (0, 0)))
    last = to_columns(jnp.concatenate([low2, extra], axis=0))
    sorted_rows = sorted_columns(groups, [hold(columns[0], grad, ffn_in_sum)] + columns[1:])
    expert_in_grad, expert_out_grad = expert_grads(groups, all_moved, *sorted_rows)
    made = split_list([hold(made[0], expert_out_grad)] + list(made[1:]))
    hidden5 = hidden4
    for block in made:
        hidden5 = hidden5 + block.astype(f32)
    last = join_list(hold(last, expert_out_grad))
    columns[0] = hold(columns[0], expert_out_grad)
    attn_out_sum, ffn_out_sum = out_grads(groups, 2, columns, all_attended, all_acted)
    last[0] = hold(last[0], ffn_out_sum, hidden5)
    mix_out_sum, model_sum = last_grads(groups, last, all_gated)

    mix_in_grad, xproj_grad, dt_grad, flat = unpack_mix(groups, mix_sum)
    heads_cols = attn_query.shape[1]
    attn_in = attn_in_sum.astype(f32)
    return (
        hidden5.astype(bf16),
        grad,
        model_sum[:4],
        mix_in_grad,
        flat[STATE + 2 :],
        xproj_grad.T,
        dt_grad,
        flat[STATE],
        flat[:STATE].T,
        flat[STATE + 1],
        mix_out_sum.T,
        ffn_in_sum.astype(f32).reshape(width, 2, hidden_units),
        ffn_out_sum.T,
        attn_in[:, :heads_cols],
        attn_in[:, heads_cols:].reshape(-1, 2, attn_keyval.shape[2]),
        attn_out_sum.T,
        model_sum[4 : 4 + EXPERTS].T,
        expert_in_grad,
        expert_out_grad.transpose(0, 2, 1),
    )


def solution(mesh):
    return jax.shard_map(
        shards,
        mesh=mesh,
        in_specs=(
            P(("dp", "tensor"), None),
            P(("dp", "tensor"), None),
            P(),
            P(None, None, "tensor"),
            P(None, "tensor"),
            P("tensor", None),
            P(None, "tensor"),
            P("tensor"),
            P("tensor", None),
            P("tensor"),
            P("tensor", None),
            P(None, None, "tensor"),
            P("tensor", None),
            P(None, "tensor"),
            P(None, None, "tensor"),
            P("tensor", None),
            P(),
            P(None, None, None, "tensor"),
            P(None, "tensor", None),
            P("dp", None),
        ),
        out_specs=(
            P(("dp", "tensor"), None),
            P(("dp", "tensor"), None),
            P(None, "dp"),
            P("dp", None, "tensor"),
            P(None, ("tensor", "dp")),
            P("tensor", "dp"),
            P("dp", "tensor"),
            P(("tensor", "dp")),
            P(("tensor", "dp"), None),
            P(("tensor", "dp")),
            P("tensor", "dp"),
            P("dp", None, "tensor"),
            P("tensor", "dp"),
            P("dp", "tensor"),
            P("dp", None, "tensor"),
            P("tensor", "dp"),
            P("dp", None),
            P(None, "dp", None, "tensor"),
            P(None, "tensor", "dp"),
        ),
        check_vma=False,
    )
```
